32 devices in a mesh: dom: 8 (over z, x), blk: 4 (over y, core).
Axes of the slice: x: 2, y: 2, z: 4, core: 2. Of those that a mesh axis runs over, the one named last changes fastest.
Arguments:
- displacement: float32 [4096, 96], P(('dom', 'blk')), may hold values from -6 to 6
- damage: float32 [4096, 96], P(('dom', 'blk')), may hold values from 0 to 0.95
- applied_load: float32 [4096, 96], P(('dom', 'blk')), may hold values from -300 to 300
- tangent: bfloat16 [4096, 5, 96, 96], P(('dom', 'blk')), may hold values from -0.625 to 0.625
- laplacian: bfloat16 [4096, 5, 96, 96], P(('dom', 'blk')), may hold values from -0.25 to 0.25
- block_columns: int32 [4096, 5], P(('dom', 'blk')), may hold values from 0 to 1023, as said below
- send_lists: int32 [8, 2, 256], P('dom'), may hold values from -1 to 511, as said below
- hist_mech: float32 [4096, 27, 96], P(('dom', 'blk')), may hold values from 0 to 200
- mech_dest: int32 [4096], P(('dom', 'blk')), may hold values from 0 to 4095, as said below
- strain_matrix: float32 [27, 96, 96], replicated, may hold values from -0.625 to 0.625
- quad_weight: float32 [27], replicated, may hold values from 0.018518519 to 0.055555556
Outputs:
- mech_out: float32 [4096, 96], P(('dom', 'blk'))
- dmg_out: float32 [4096, 96], P(('dom', 'blk'))
- norms: float32 [2], replicated
The draws below stay inside these ranges and needn't reach their ends.
Inputs may be any that keep to these rules, and one draw needn't show every extreme that they name: mech_dest is a permutation of the block rows. The 128 rows of one device go to at most 5 rows of any one device (itself included), and that many are reached in every draw. `send_lists`: -1 marks an unused slot; used slots come first and name distinct rows of the group, numbered within the group. Group 0 lists nothing for the group below and the last group nothing for the group above. Some list uses all 256 slots. `block_columns`: entries of the ghost parts of the extended numbering name only used slots of the neighbours' lists, never those of a missing neighbour, and every used slot is named by some block row of the receiving group.
All inputs are finite; a program needn't handle non-finite values.
Results may differ from the reference program's by a relative error of at most 0.00047.
Values may be sent and summed in bfloat16 or wider, within the bound.
No kernel may reach another device: no remote copies, remote signals or barrier semaphores. Data moves between devices by JAX's collectives and lax.ppermute only.
A program may use at most 128 MiB of HBM per device.

```python
import math
import jax
import jax.numpy as jnp
from jax import lax

BLOCK = 96
KBLK = 5
QUAD = 27
RDEV = 128
RGRP = 512
GMAX = 256
NBR = 4096
N_DOM = 8
DEVICES = 32


def perm_slots(sub_key):
    return jax.random.permutation(sub_key, RDEV)


def perm_group(sub_key):
    return jax.random.permutation(sub_key, RGRP)


def route_map(key):
    base_count = RDEV // DEVICES
    sub_keys = jax.random.split(jax.random.fold_in(key, 11), 4)
    offsets = jnp.arange(DEVICES)
    coins = jax.random.randint(sub_keys[0], (DEVICES,), 0, 2)
    chosen = jax.random.randint(sub_keys[1], (), 0, DEVICES)
    coins = jnp.where(offsets == chosen, 1, coins)
    coins = jnp.where(offsets == (chosen + 1) % DEVICES, 0, coins)
    counts = base_count + coins - jnp.roll(coins, -1)
    bounds = jnp.cumsum(counts)
    offset_of = jnp.searchsorted(bounds, jnp.arange(RDEV), side='right').astype(jnp.int32)
    shuffle = jax.random.permutation(sub_keys[2], RDEV)
    shift = jnp.zeros((RDEV,), jnp.int32).at[shuffle].set(offset_of)
    slot_perm = jax.vmap(perm_slots)(jax.random.split(sub_keys[3], DEVICES))
    sources = jnp.arange(DEVICES)[:, None]
    slot_ids = jnp.arange(RDEV)[None, :]
    target = (sources + shift[None, :]) % DEVICES
    dest = target * RDEV + slot_perm[target, slot_ids]
    return dest.reshape(-1).astype(jnp.int32)


def draw_mech_dest(key, part):
    return route_map(key)


def draw_hist_mech(key, part):
    dest = route_map(key)
    trend_pos = dest.astype(jnp.float32) / max(NBR - 1, 1)
    sub_keys = jax.random.split(jax.random.fold_in(key, 23), 2)
    row_scale = jnp.exp(jax.random.uniform(sub_keys[0], (NBR, 1, 1)) * math.log(10.0))
    values = jnp.exp(jax.random.uniform(sub_keys[1], (NBR, QUAD, BLOCK), minval=-3.0, maxval=0.7))
    trend = 1.0 + 2.0 * trend_pos
    return (values * row_scale * trend[:, None, None]).astype(jnp.float32)


def draw_applied_load(key, part):
    sub_keys = jax.random.split(jax.random.fold_in(key, 29), 3)
    trend_pos = jnp.arange(NBR).astype(jnp.float32) / max(NBR - 1, 1)
    row_scale = jnp.exp(jax.random.uniform(sub_keys[0], (NBR, 1)) * math.log(10.0))
    column_scale = jnp.exp(jax.random.uniform(sub_keys[1], (1, BLOCK)) * math.log(10.0))
    values = jax.random.truncated_normal(sub_keys[2], -6.0, 6.0, (NBR, BLOCK))
    trend = 1.0 + 2.0 * trend_pos
    return (0.1 * values * row_scale * column_scale * trend[:, None]).astype(jnp.float32)


def ghost_plan(key):
    sub_keys = jax.random.split(jax.random.fold_in(key, 37), 6)
    counts = jax.random.randint(sub_keys[0], (N_DOM, 2), GMAX // 4, GMAX + 1)
    chosen = jax.random.randint(sub_keys[1], (), 0, N_DOM - 1)
    group_ids = jnp.arange(N_DOM)
    counts = counts.at[:, 1].set(jnp.where(group_ids == chosen, GMAX, counts[:, 1]))
    counts = counts.at[0, 0].set(0).at[N_DOM - 1, 1].set(0)
    orders = jax.vmap(perm_group)(jax.random.split(sub_keys[2], N_DOM * 2)).reshape(N_DOM, 2, RGRP)[:, :, :GMAX]
    listed = jnp.where(jnp.arange(GMAX)[None, None, :] < counts[:, :, None], orders, -1)
    zero_one = jnp.zeros((1,), counts.dtype)
    below = jnp.concatenate([zero_one, counts[:-1, 1]])
    above = jnp.concatenate([counts[1:, 0], zero_one])
    mixers = jax.vmap(perm_group)(jax.random.split(sub_keys[3], N_DOM))
    spread = jax.random.randint(sub_keys[4], (N_DOM, RGRP, KBLK), 0, RGRP)
    own_index = jnp.broadcast_to(jnp.arange(RGRP)[None, :], (N_DOM, RGRP))
    low_col = jnp.where(below[:, None] > 0, RGRP + mixers % jnp.maximum(below[:, None], 1), spread[:, :, 1])
    high_col = jnp.where(above[:, None] > 0, RGRP + GMAX + mixers % jnp.maximum(above[:, None], 1), spread[:, :, 2])
    entries = jnp.concatenate([own_index[:, :, None], low_col[:, :, None], high_col[:, :, None], spread[:, :, 3:]], axis=2)
    scores = jax.random.randint(sub_keys[5], (N_DOM, RGRP, KBLK), 0, 1 << 20) * KBLK + jnp.arange(KBLK)[None, None, :]
    order_k = jnp.argsort(scores, axis=2)
    columns = jnp.take_along_axis(entries, order_k, axis=2)
    return (listed.astype(jnp.int32), columns.reshape(NBR, KBLK).astype(jnp.int32))


def draw_send_lists(key, part):
    return ghost_plan(key)[0]


def draw_block_columns(key, part):
    return ghost_plan(key)[1]


def level_of(rng, shape, shards, smallest, high):
    def one(dim, shards_of):
        heights = jax.random.uniform(jax.random.fold_in(jax.random.fold_in(rng, 6), dim), (shards_of,), jnp.float32, smallest / len(shards), high / len(shards))
        return jnp.repeat(jnp.exp(heights), shape[dim] // shards_of).reshape((-1,) + (1,) * (len(shape) - dim - 1))

    loudness = one(*shards[0])
    for cut in shards[1:]:
        loudness = loudness * one(*cut)
    return loudness


def gaussian(key, dims, scale, most, cuts=(), held_as=jnp.bfloat16):
    array = jax.random.normal(key, dims, jnp.float32) * scale
    if len(cuts) > 0:
        array = level_of(key, dims, cuts, -0.22, 0.18) * array
    return jnp.clip(array, min=-most, max=most).astype(held_as)


def setup_inputs(seed: int = 0) -> dict:
    splits = jax.random.split(jax.random.key(seed), 12)
    return {
        "displacement": gaussian(splits[0], (NBR, BLOCK), 1.0, 6.0, ((0, 32),), jnp.float32),
        "damage": jnp.clip(0.95 * jax.random.uniform(splits[1], (NBR, BLOCK), jnp.float32) ** level_of(splits[1], (NBR, BLOCK), ((0, 32),), -0.2, 0.2), 0.0, 0.95),
        "applied_load": draw_applied_load(jax.random.fold_in(splits[11], 71), 0),
        "tangent": gaussian(splits[3], (NBR, KBLK, BLOCK, BLOCK), BLOCK ** -0.5, 0.625, ((0, 32),)),
        "laplacian": gaussian(splits[4], (NBR, KBLK, BLOCK, BLOCK), (KBLK * BLOCK) ** -0.5, 0.25, ((0, 32),)),
        "block_columns": draw_block_columns(jax.random.fold_in(splits[11], 71), 0),
        "send_lists": draw_send_lists(jax.random.fold_in(splits[11], 71), 0),
        "hist_mech": draw_hist_mech(jax.random.fold_in(splits[11], 71), 0),
        "mech_dest": draw_mech_dest(jax.random.fold_in(splits[11], 71), 0),
        "strain_matrix": gaussian(splits[9], (QUAD, BLOCK, BLOCK), BLOCK ** -0.5, 0.625, (), jnp.float32),
        "quad_weight": jnp.clip(jax.random.uniform(splits[10], (QUAD,), jnp.float32, 0.018518519, 0.055555556), 0.018518519, 0.055555556),
    }


def apply_blocks(packed):
    tan_rows, lap_rows, disp_near, dmg_near = packed
    mech_sum = jnp.einsum('ikrc,ikc->ir', tan_rows.astype(jnp.float32), disp_near.astype(jnp.float32))
    diffuse = jnp.einsum('ikrc,ikc->ir', lap_rows.astype(jnp.float32), dmg_near.astype(jnp.float32))
    return (mech_sum, diffuse)

def reference(displacement, damage, applied_load, tangent, laplacian, block_columns, send_lists, hist_mech, mech_dest, strain_matrix, quad_weight):
    root_deg = jnp.sqrt((1.0 - damage) ** 2 + 0.001)
    fields = jnp.stack([(root_deg * displacement).astype(jnp.bfloat16), damage.astype(jnp.bfloat16)])
    grouped = fields.reshape(2, N_DOM, RGRP, BLOCK)
    listed = send_lists >= 0
    safe_index = jnp.maximum(send_lists, 0).astype(jnp.int32)
    group_index = jnp.arange(N_DOM, dtype=jnp.int32)[:, None, None]
    picked = grouped[:, group_index, safe_index]
    picked = jnp.where(listed[None, :, :, :, None], picked, jnp.zeros((), jnp.bfloat16))
    empty_rows = jnp.zeros((2, 1, GMAX, BLOCK), jnp.bfloat16)
    lower_ghost = jnp.concatenate([empty_rows, picked[:, :-1, 1]], axis=1)
    upper_ghost = jnp.concatenate([picked[:, 1:, 0], empty_rows], axis=1)
    extended = jnp.concatenate([grouped, lower_ghost, upper_ghost], axis=2)
    column_grid = block_columns.reshape(N_DOM, RGRP, KBLK).astype(jnp.int32)
    near_rows = extended[:, group_index, column_grid].reshape(2, NBR, KBLK, BLOCK)
    mech_sum, diffuse = lax.map(apply_blocks, (tangent.reshape(DEVICES, RDEV, KBLK, BLOCK, BLOCK), laplacian.reshape(DEVICES, RDEV, KBLK, BLOCK, BLOCK), near_rows[0].reshape(DEVICES, RDEV, KBLK, BLOCK), near_rows[1].reshape(DEVICES, RDEV, KBLK, BLOCK)))
    mech_sum = mech_sum.reshape(NBR, BLOCK)
    diffuse = diffuse.reshape(NBR, BLOCK)
    mech_res = root_deg * mech_sum - applied_load
    history = jnp.zeros((NBR, QUAD, BLOCK), jnp.float32).at[mech_dest].set(hist_mech)
    strain = jnp.einsum('qcr,ir->iqc', strain_matrix, displacement, precision=lax.Precision.HIGHEST)
    energy = 0.5 * strain * strain
    source = jnp.einsum('q,iqc->ic', quad_weight, jnp.maximum(history, energy), precision=lax.Precision.HIGHEST)
    dmg_res = diffuse + (1.0 + 2.0 * source) * damage - 2.0 * source
    mech_norm = jnp.sqrt(jnp.mean(mech_res * mech_res) + 1e-06)
    dmg_norm = jnp.sqrt(jnp.mean(dmg_res * dmg_res) + 1e-06)
    return (mech_res / mech_norm, dmg_res / dmg_norm, jnp.stack([mech_norm, dmg_norm]))
```

```python
import functools

import jax
import jax.numpy as jnp
from jax import lax
from jax.experimental import pallas as pl
from jax.experimental.pallas import tpu as pltpu
from jax.sharding import PartitionSpec as P

F32 = jnp.float32
BF16 = jnp.bfloat16
CAP = 8
VMEM_LIMIT = 48 * 1024 * 1024


def dot(a, b):
    return lax.dot_general(a, b, (((1,), (0,)), ((), ())), preferred_element_type=F32)


def dot_nt(a, b):
    return lax.dot_general(a, b, (((1,), (1,)), ((), ())), preferred_element_type=F32)


def split2(x):
    hi = x.astype(BF16)
    lo = (x - hi.astype(F32)).astype(BF16)
    return hi, lo


def split3(x):
    hi = x.astype(BF16)
    rest = x - hi.astype(F32)
    mid = rest.astype(BF16)
    lo = (rest - mid.astype(F32)).astype(BF16)
    return hi, mid, lo


def one_hot(cond):
    return jnp.where(cond, 1.0, 0.0).astype(BF16)


def iota(shape, dim):
    return lax.broadcasted_iota(jnp.int32, shape, dim)


def root_of(damage):
    return jnp.sqrt((1.0 - damage) ** 2 + 0.001)


def fields_kernel(disp, damage, out):
    width = disp.shape[0]
    dmg = damage[...]
    out[:width, :] = (root_of(dmg) * disp[...]).astype(BF16)
    out[width:, :] = dmg.astype(BF16)


def pick_kernel(group, lists, out):
    parts, _, lanes = group.shape
    for side in range(2):
        row = lists[side : side + 1, :]
        total = None
        for j in range(parts):
            hot = one_hot(iota((lanes, row.shape[1]), 0) + j * lanes == row)
            term = dot(group[j], hot)
            total = term if total is None else total + term
        out[side] = total.astype(BF16)


def source_kernel(every, dest, hist, smat, weight, out, dm_ref):
    devices, width, lanes = every.shape
    quads = hist.shape[0]
    d = dest[...]

    def gather(j, acc):
        hot = one_hot(iota((lanes, lanes), 0) + j * lanes == d)
        x = every[j]
        hi, mid, lo = split3(x)
        return acc + (dot(hi, hot) + dot(mid, hot) + dot(lo, hot))

    dm = lax.fori_loop(0, devices, gather, jnp.zeros((width, lanes), F32), unroll=4)
    dm_ref[...] = dm
    d_hi, d_lo = split2(dm)
    acc = jnp.zeros((width, lanes), F32)
    for q in range(quads):
        s_hi, s_lo = split2(smat[q])
        strain = dot(s_hi, d_hi) + (dot(s_hi, d_lo) + dot(s_lo, d_hi))
        acc = acc + weight[0, q] * jnp.maximum(hist[q], 0.5 * strain * strain)
    owner = d // lanes
    slot = d - owner * lanes
    square = jnp.broadcast_to(owner, (lanes, lanes))
    diag = iota((lanes, lanes), 0) == iota((lanes, lanes), 1)
    column = jnp.sum(jnp.where(diag, square.astype(F32), 0.0), axis=1, keepdims=True)
    before = iota((lanes, lanes), 0) < iota((lanes, lanes), 1)
    same = (column == square.astype(F32)) & before
    rank = jnp.sum(jnp.where(same, 1.0, 0.0), axis=0, keepdims=True).astype(jnp.int32)
    bucket = owner * CAP + rank
    hot = one_hot(iota((devices * CAP, lanes), 0) == bucket)
    pad = jnp.where(
        iota((lanes - width, lanes), 0) == 0, (slot + 1).astype(F32), 0.0
    )
    table = jnp.concatenate([acc, pad], axis=0)
    hi, mid, lo = split3(table)
    out[...] = dot_nt(hot, hi) + dot_nt(hot, mid) + dot_nt(hot, lo)


def matvec_kernel(group, ghosts, columns, tan, lap, mech, diff, near):
    kblk, rows, width, lanes = tan.shape
    parts = group.shape[0]
    ghost = ghosts.shape[2]

    @pl.when(pl.program_id(0) == 0)
    def _():
        for k in range(kblk):
            col = columns[k : k + 1, :]
            total = jnp.zeros((2 * width, lanes), F32)
            for j in range(parts):
                hot = one_hot(iota((lanes, lanes), 0) + j * lanes == col)
                total = total + dot(group[j], hot)
            for side in range(2):
                start = parts * lanes + side * ghost
                hot = one_hot(iota((ghost, lanes), 0) + start == col)
                total = total + dot(ghosts[side], hot)
            near[k] = total

    for field, (mat, out) in enumerate(((tan, mech), (lap, diff))):
        acc = [jnp.zeros((8, lanes), F32) for _ in range(rows)]
        for k in range(kblk):
            for c in range(0, width, 16):
                base = field * width + c
                lo = near[k, base : base + 8, :]
                hi = near[k, base + 8 : base + 16, :]
                for r in range(rows):
                    block = mat[k, r, c : c + 16, :].astype(F32)
                    acc[r] = acc[r] + block[:8] * lo + block[8:] * hi
        out[...] = jnp.concatenate(
            [jnp.sum(a, axis=0, keepdims=True) for a in acc], axis=0
        )


def residual_kernel(got, diffuse, mech_sum, load, damage, mech, dmg, sums):
    width, lanes = damage.shape
    parcels = got[...]
    slot = parcels[:, width : width + 1].astype(jnp.int32) - 1
    hot = one_hot(iota((parcels.shape[0], lanes), 1) == slot)
    turned = parcels.T[:width]
    hi, mid, lo = split3(turned)
    source = dot(hi, hot) + dot(mid, hot) + dot(lo, hot)
    d = damage[...]
    dmg_res = diffuse[...] + (1.0 + 2.0 * source) * d - 2.0 * source
    mech_res = root_of(d) * mech_sum[...] - load[...]
    mech[...] = mech_res
    dmg[...] = dmg_res
    sums[0:1, :] = jnp.sum(mech_res * mech_res, axis=0, keepdims=True)
    sums[1:2, :] = jnp.sum(dmg_res * dmg_res, axis=0, keepdims=True)


def scale_kernel(entries, sums, mech, dmg, mech_out, dmg_out, norms):
    total = jnp.sum(sums[...], axis=0)
    mean = jnp.sum(total, axis=1, keepdims=True) / entries
    norm = jnp.sqrt(mean + 1e-06)
    mech_out[...] = mech[...] / norm[0:1, :]
    dmg_out[...] = dmg[...] / norm[1:2, :]
    norms[...] = jnp.broadcast_to(norm, norms.shape)


VM = pl.BlockSpec(memory_space=pltpu.VMEM)
SM = pl.BlockSpec(memory_space=pltpu.SMEM)


def call(body, outs, ins, scratch=(), flops=0, nbytes=0, specs=None):
    one = not isinstance(outs, (list, tuple))
    return pl.pallas_call(
        body,
        out_shape=outs,
        in_specs=specs or [VM] * ins,
        out_specs=VM if one else [VM] * len(outs),
        scratch_shapes=list(scratch),
        compiler_params=pltpu.CompilerParams(vmem_limit_bytes=VMEM_LIMIT),
        cost_estimate=pl.CostEstimate(flops=flops, bytes_accessed=nbytes, transcendentals=0),
    )


def sds(shape, dtype=F32):
    return jax.ShapeDtypeStruct(shape, dtype)


def on_device(
    displacement,
    damage,
    applied_load,
    tangent,
    laplacian,
    block_columns,
    send_lists,
    hist_mech,
    mech_dest,
    strain_matrix,
    quad_weight,
):
    lanes, width = displacement.shape
    kblk = tangent.shape[1]
    quads = hist_mech.shape[1]
    ghost = send_lists.shape[2]
    both = ("dom", "blk")
    devices = lax.axis_size(both)
    groups = lax.axis_size("dom")
    disp_t = displacement.T
    dmg_t = damage.T
    load_t = applied_load.T
    tan_t = jnp.transpose(tangent, (1, 2, 3, 0))
    lap_t = jnp.transpose(laplacian, (1, 2, 3, 0))
    hist_t = jnp.transpose(hist_mech, (1, 2, 0))
    cols_t = block_columns.T

    with jax.named_scope("fields"):
        fields = call(fields_kernel, sds((2 * width, lanes), BF16), 2)(disp_t, dmg_t)
    every = lax.all_gather(disp_t, both, axis=0, tiled=False)
    group = lax.all_gather(fields, "blk", axis=0, tiled=False)
    with jax.named_scope("picks"):
        picked = call(pick_kernel, sds((2, 2 * width, ghost), BF16), 2)(group, send_lists[0])
    up = [(i, i + 1) for i in range(groups - 1)]
    down = [(i + 1, i) for i in range(groups - 1)]
    lower = lax.ppermute(picked[1], "dom", up)
    upper = lax.ppermute(picked[0], "dom", down)
    with jax.named_scope("source"):
        parcels = call(
            source_kernel,
            sds((devices * CAP, lanes)),
            5,
            [pltpu.VMEM((width, lanes), F32)],
            flops=6 * quads * width * width * lanes,
            nbytes=4 * quads * width * lanes * 2,
            specs=[VM, VM, VM, VM, SM],
        )(every, mech_dest[None, :], hist_t, strain_matrix, quad_weight[None, :])
    got = lax.all_to_all(
        parcels.reshape(devices, CAP, lanes), both, split_axis=0, concat_axis=0, tiled=True
    )
    ghosts = jnp.stack([lower, upper])
    rows = 8
    mat_spec = pl.BlockSpec((kblk, rows, width, lanes), lambda i: (0, i, 0, 0))
    out_spec = pl.BlockSpec((rows, lanes), lambda i: (i, 0))
    with jax.named_scope("matvec"):
        mech_sum, diffuse = pl.pallas_call(
            matvec_kernel,
            grid=(width // rows,),
            out_shape=[sds((width, lanes))] * 2,
            in_specs=[VM, VM, VM, mat_spec, mat_spec],
            out_specs=[out_spec, out_spec],
            scratch_shapes=[pltpu.VMEM((kblk, 2 * width, lanes), F32)],
            compiler_params=pltpu.CompilerParams(vmem_limit_bytes=VMEM_LIMIT),
            cost_estimate=pl.CostEstimate(
                flops=4 * kblk * width * width * lanes,
                bytes_accessed=4 * kblk * width * width * lanes,
                transcendentals=0,
            ),
        )(group, ghosts, cols_t, tan_t, lap_t)
    with jax.named_scope("residuals"):
        mech, dmg, sums = call(
            residual_kernel, [sds((width, lanes)), sds((width, lanes)), sds((2, lanes))], 5
        )(got.reshape(devices * CAP, lanes), diffuse, mech_sum, load_t, dmg_t)
    every_sum = lax.all_gather(sums, both, axis=0, tiled=False)
    with jax.named_scope("scale"):
        mech_out, dmg_out, norms = call(
            functools.partial(scale_kernel, float(lanes * width * devices)),
            [sds((width, lanes)), sds((width, lanes)), sds((2, lanes))],
            3,
        )(every_sum, mech, dmg)
    return mech_out.T, dmg_out.T, norms[:, 0]


def solution(mesh):
    rows = P(("dom", "blk"))
    in_specs = (rows,) * 6 + (P("dom"),) + (rows,) * 2 + (P(), P())
    out_specs = (rows, rows, P())
    return jax.shard_map(
        on_device, mesh=mesh, in_specs=in_specs, out_specs=out_specs, check_vma=False
    )
```

```python
import functools

import jax
import jax.numpy as jnp
from jax import lax
from jax.experimental import pallas as pl
from jax.experimental.pallas import tpu as pltpu
from jax.sharding import PartitionSpec as P

F32 = jnp.float32
BF16 = jnp.bfloat16
CAP = 8
VMEM_LIMIT = 48 * 1024 * 1024


def dot(a, b):
    return lax.dot_general(a, b, (((1,), (0,)), ((), ())), preferred_element_type=F32)


def dot_nt(a, b):
    return lax.dot_general(a, b, (((1,), (1,)), ((), ())), preferred_element_type=F32)


def split2(x):
    hi = x.astype(BF16)
    lo = (x - hi.astype(F32)).astype(BF16)
    return hi, lo


def split3(x):
    hi = x.astype(BF16)
    rest = x - hi.astype(F32)
    mid = rest.astype(BF16)
    lo = (rest - mid.astype(F32)).astype(BF16)
    return hi, mid, lo


def one_hot(cond):
    return jnp.where(cond, 1.0, 0.0).astype(BF16)


def iota(shape, dim):
    return lax.broadcasted_iota(jnp.int32, shape, dim)


def root_of(damage):
    return jnp.sqrt((1.0 - damage) ** 2 + 0.001)


def prep_kernel(disp, damage, dest, fields, parts, request, bucket):
    width, lanes = disp.shape
    devices = request.shape[0]
    x = disp[...]
    dmg = damage[...]
    fields[:width, :] = (root_of(dmg) * x).astype(BF16)
    fields[width:, :] = dmg.astype(BF16)
    hi, mid, lo = split3(x)
    parts[0] = hi
    parts[1] = mid
    parts[2] = lo
    d = dest[...]
    owner = d // lanes
    slot = d - owner * lanes
    square = jnp.broadcast_to(owner.astype(F32), (lanes, lanes))
    diag = iota((lanes, lanes), 0) == iota((lanes, lanes), 1)
    column = jnp.sum(jnp.where(diag, square, 0.0), axis=1, keepdims=True)
    before = iota((lanes, lanes), 0) < iota((lanes, lanes), 1)
    same = (column == square) & before
    rank = jnp.sum(jnp.where(same, 1.0, 0.0), axis=0, keepdims=True).astype(jnp.int32)
    bucket[...] = owner * CAP + rank
    wanted = jnp.where(iota((devices, lanes), 0) == owner, (slot + 1).astype(F32), 0.0)
    ranks = one_hot(iota((lanes, lanes), 0) == rank)
    request[...] = dot_nt(wanted.astype(BF16), ranks)[:, None, :]


def send_kernel(request, parts, parcels, hot_out):
    devices, _, lanes = request.shape
    width = parts.shape[1]
    spread = jnp.broadcast_to(request[...], (devices, CAP, lanes))
    spread = spread.reshape(devices * CAP, lanes)
    own = iota(spread.shape, 0) % CAP == iota(spread.shape, 1)
    slot = jnp.sum(jnp.where(own, spread, 0.0), axis=1, keepdims=True)
    hot = one_hot(iota(spread.shape, 1).astype(F32) == slot - 1.0)
    hot_out[...] = hot
    total = dot_nt(hot, parts[0]) + (dot_nt(hot, parts[1]) + dot_nt(hot, parts[2]))
    pad = jnp.zeros((total.shape[0], lanes - width), F32)
    parcels[...] = jnp.concatenate([total, pad], axis=1)


def pick_kernel(group, lists, below, above):
    parts, _, lanes = group.shape
    for side in range(2):
        row = lists[side : side + 1, :]
        total = None
        for j in range(parts):
            hot = one_hot(iota((lanes, row.shape[1]), 0) + j * lanes == row)
            term = dot(group[j], hot)
            total = term if total is None else total + term
        (below, above)[side][...] = total.astype(BF16)


def source_kernel(got, bucket, hist_hbm, smat_hbm, weight, out, hist, smat, sems):
    quads, width, lanes = hist.shape
    loads = [
        pltpu.make_async_copy(hist_hbm, hist, sems.at[0]),
        pltpu.make_async_copy(smat_hbm, smat, sems.at[1]),
    ]
    for load in loads:
        load.start()
    hot = one_hot(iota((got.shape[0], lanes), 0) == bucket[...])
    turned = got[...].T[:width]
    hi, mid, lo = split3(turned)
    dm = dot(hi, hot) + (dot(mid, hot) + dot(lo, hot))
    d_hi, d_lo = split2(dm)
    for load in loads:
        load.wait()
    acc = jnp.zeros((width, lanes), F32)
    for q in range(quads):
        s_hi, s_lo = split2(smat[q])
        strain = dot(s_hi, d_hi) + (dot(s_hi, d_lo) + dot(s_lo, d_hi))
        acc = acc + weight[0, q] * jnp.maximum(hist[q], 0.5 * strain * strain)
    table = jnp.concatenate([acc, jnp.zeros((lanes - width, lanes), F32)], axis=0)
    hi, mid, lo = split3(table)
    out[...] = dot_nt(hot, hi) + (dot_nt(hot, mid) + dot_nt(hot, lo))


def matvec_kernel(group, lower, upper, columns, tan, lap, mech, diff, near):
    kblk, rows, width, lanes = tan.shape
    parts = group.shape[0]
    ghost = lower.shape[1]
    depth = kblk * width

    @pl.when(pl.program_id(0) == 0)
    def _():
        found = []
        for k in range(kblk):
            col = columns[k : k + 1, :]
            total = jnp.zeros((2 * width, lanes), F32)
            for j in range(parts):
                hot = one_hot(iota((lanes, lanes), 0) + j * lanes == col)
                total = total + dot(group[j], hot)
            for side in range(2):
                start = parts * lanes + side * ghost
                hot = one_hot(iota((ghost, lanes), 0) + start == col)
                total = total + dot((lower, upper)[side][...], hot)
            found.append(total)
        for field in range(2):
            cut = [f[field * width : (field + 1) * width] for f in found]
            near[field] = jnp.concatenate(cut, axis=0).T.astype(BF16)

    lane = iota((8, 2 * lanes), 1) % lanes
    mine = iota((8, 2 * lanes), 0) == lane % 8
    for field, (mat, out) in enumerate(((tan, mech), (lap, diff))):
        left = near[field]
        lines = []
        for r in range(0, rows, 2):
            pair = [mat[:, r + j].reshape(depth, lanes) for j in range(2)]
            full = dot(left, jnp.concatenate(pair, axis=1))
            kept = full[:8]
            for g in range(1, lanes // 8):
                kept = jnp.where(lane // 8 == g, full[g * 8 : g * 8 + 8], kept)
            line = jnp.sum(jnp.where(mine, kept, 0.0), axis=0, keepdims=True)
            lines += [line[:, :lanes], line[:, lanes:]]
        out[...] = jnp.concatenate(lines, axis=0)


def residual_kernel(got, hot, diffuse, mech_sum, load, damage, mech, dmg, sums):
    width, lanes = damage.shape
    turned = got[...].T[:width]
    hi, mid, lo = split3(turned)
    spread = hot[...]
    source = dot(hi, spread) + (dot(mid, spread) + dot(lo, spread))
    d = damage[...]
    dmg_res = diffuse[...] + (1.0 + 2.0 * source) * d - 2.0 * source
    mech_res = root_of(d) * mech_sum[...] - load[...]
    mech[...] = mech_res
    dmg[...] = dmg_res
    pair = []
    for x in (mech_res, dmg_res):
        line = jnp.sum(x * x, axis=0, keepdims=True)
        pair.append(jnp.sum(line, axis=1, keepdims=True))
    lane = iota((1, lanes), 1)
    row = jnp.where(lane == 0, pair[0], jnp.where(lane == 1, pair[1], 0.0))
    sums[...] = jnp.broadcast_to(row[None], sums.shape)


def scale_kernel(entries, sums, mech, dmg, mech_out, dmg_out, norms):
    total = jnp.sum(sums[...], axis=0)
    norm = jnp.sqrt(total / entries + 1e-06)
    mech_out[...] = mech[...] / norm[:, 0:1]
    dmg_out[...] = dmg[...] / norm[:, 1:2]
    norms[...] = norm[:, 0:2]


VM = pl.BlockSpec(memory_space=pltpu.VMEM)
HB = pl.BlockSpec()
AN = pl.BlockSpec(memory_space=pl.ANY)
SM = pl.BlockSpec(memory_space=pltpu.SMEM)


def call(body, outs, ins, scratch=(), flops=0, nbytes=0, specs=None):
    one = not isinstance(outs, (list, tuple))
    return pl.pallas_call(
        body,
        out_shape=outs,
        in_specs=specs or [VM] * ins,
        out_specs=VM if one else [VM] * len(outs),
        scratch_shapes=list(scratch),
        compiler_params=pltpu.CompilerParams(vmem_limit_bytes=VMEM_LIMIT),
        cost_estimate=pl.CostEstimate(flops=flops, bytes_accessed=nbytes, transcendentals=0),
    )


def sds(shape, dtype=F32):
    return jax.ShapeDtypeStruct(shape, dtype)


def swap(x, axes):
    return lax.all_to_all(x, axes, split_axis=0, concat_axis=0, tiled=True)


def on_device(
    displacement,
    damage,
    applied_load,
    tangent,
    laplacian,
    block_columns,
    send_lists,
    hist_mech,
    mech_dest,
    strain_matrix,
    quad_weight,
):
    lanes, width = displacement.shape
    kblk = tangent.shape[1]
    quads = hist_mech.shape[1]
    ghost = send_lists.shape[2]
    both = ("dom", "blk")
    devices = lax.axis_size(both)
    groups = lax.axis_size("dom")
    blocks = lax.axis_size("blk")
    disp_t = displacement.T
    dmg_t = damage.T
    load_t = applied_load.T
    tan_t = jnp.transpose(tangent, (1, 2, 3, 0))
    lap_t = jnp.transpose(laplacian, (1, 2, 3, 0))
    hist_t = jnp.transpose(hist_mech, (1, 2, 0))
    cols_t = block_columns.T

    with jax.named_scope("prep"):
        fields, parts, request, bucket = call(
            prep_kernel,
            [
                sds((2 * width, lanes), BF16),
                sds((3, width, lanes), BF16),
                sds((devices, 1, lanes)),
                sds((1, lanes), jnp.int32),
            ],
            3,
            specs=[HB] * 3,
        )(disp_t, dmg_t, mech_dest[None, :])
    wanted = swap(request, both)
    group = swap(jnp.broadcast_to(fields[None], (blocks,) + fields.shape), "blk")
    with jax.named_scope("send"):
        parcels, hot = call(
            send_kernel, [sds((devices * CAP, lanes)), sds((devices * CAP, lanes), BF16)], 2
        )(wanted, parts)
    asked = swap(parcels.reshape(devices, CAP, lanes), both)
    with jax.named_scope("picks"):
        picked = call(pick_kernel, [sds((2 * width, ghost), BF16)] * 2, 2)(
            group, send_lists[0]
        )
    up = [(i, i + 1) for i in range(groups - 1)]
    down = [(i + 1, i) for i in range(groups - 1)]
    lower = lax.ppermute(picked[1], "dom", up)
    upper = lax.ppermute(picked[0], "dom", down)
    with jax.named_scope("source"):
        answer = call(
            source_kernel,
            sds((devices * CAP, lanes)),
            5,
            [
                pltpu.VMEM((quads, width, lanes), F32),
                pltpu.VMEM(strain_matrix.shape, F32),
                pltpu.SemaphoreType.DMA((2,)),
            ],
            flops=6 * quads * width * width * lanes,
            nbytes=4 * quads * width * lanes * 2,
            specs=[VM, VM, AN, AN, SM],
        )(
            asked.reshape(devices * CAP, lanes),
            bucket,
            hist_t,
            strain_matrix,
            quad_weight[None, :],
        )
    got = swap(answer.reshape(devices, CAP, lanes), both)
    rows = 8
    mat_spec = pl.BlockSpec((kblk, rows, width, lanes), lambda i: (0, i, 0, 0))
    out_spec = pl.BlockSpec((rows, lanes), lambda i: (i, 0))
    with jax.named_scope("matvec"):
        mech_sum, diffuse = pl.pallas_call(
            matvec_kernel,
            grid=(width // rows,),
            out_shape=[sds((width, lanes))] * 2,
            in_specs=[VM, VM, VM, VM, mat_spec, mat_spec],
            out_specs=[out_spec, out_spec],
            scratch_shapes=[pltpu.VMEM((2, lanes, kblk * width), BF16)],
            compiler_params=pltpu.CompilerParams(vmem_limit_bytes=VMEM_LIMIT),
            cost_estimate=pl.CostEstimate(
                flops=4 * kblk * width * width * lanes,
                bytes_accessed=4 * kblk * width * width * lanes,
                transcendentals=0,
            ),
        )(group, lower, upper, cols_t, tan_t, lap_t)
    with jax.named_scope("residuals"):
        mech, dmg, sums = call(
            residual_kernel,
            [sds((width, lanes)), sds((width, lanes)), sds((devices, 1, lanes))],
            6,
        )(got.reshape(devices * CAP, lanes), hot, diffuse, mech_sum, load_t, dmg_t)
    every_sum = swap(sums, both)
    with jax.named_scope("scale"):
        mech_out, dmg_out, norms = call(
            functools.partial(scale_kernel, float(lanes * width * devices)),
            [sds((width, lanes)), sds((width, lanes)), sds((1, 2))],
            3,
        )(every_sum, mech, dmg)
    return mech_out.T, dmg_out.T, norms[0]


def solution(mesh):
    rows = P(("dom", "blk"))
    in_specs = (rows,) * 6 + (P("dom"),) + (rows,) * 2 + (P(), P())
    out_specs = (rows, rows, P())
    return jax.shard_map(
        on_device, mesh=mesh, in_specs=in_specs, out_specs=out_specs, check_vma=False
    )
```

```python
import functools

import jax
import jax.numpy as jnp
from jax import lax
from jax.experimental import pallas as pl
from jax.experimental.pallas import tpu as pltpu
from jax.sharding import PartitionSpec as P

F32 = jnp.float32
BF16 = jnp.bfloat16
CAP = 8
FILL = 10**10
VMEM_LIMIT = 12 * 1024 * 1024


def dot(a, b):
    return lax.dot_general(a, b, (((1,), (0,)), ((), ())), preferred_element_type=F32)


def dot_nt(a, b):
    return lax.dot_general(a, b, (((1,), (1,)), ((), ())), preferred_element_type=F32)


def split2(x):
    hi = x.astype(BF16)
    lo = (x - hi.astype(F32)).astype(BF16)
    return hi, lo


def split3(x):
    hi = x.astype(BF16)
    rest = x - hi.astype(F32)
    mid = rest.astype(BF16)
    lo = (rest - mid.astype(F32)).astype(BF16)
    return hi, mid, lo


def one_hot(cond):
    return jnp.where(cond, 1.0, 0.0).astype(BF16)


def iota(shape, dim):
    return lax.broadcasted_iota(jnp.int32, shape, dim)


def root_of(damage):
    return jnp.sqrt((1.0 - damage) ** 2 + 0.001)


def prep_kernel(stacked, fields, parts, request, bucket):
    width, lanes = parts.shape[1:]
    devices = request.shape[0]
    x = stacked[:width, :]
    dmg = stacked[width : 2 * width, :]
    weighted = (root_of(dmg) * x).astype(BF16)
    half = dmg.astype(BF16)
    for j in range(fields.shape[0]):
        fields[j, :width, :] = weighted
        fields[j, width:, :] = half
    hi, mid, lo = split3(x)
    parts[0] = hi
    parts[1] = mid
    parts[2] = lo
    d = stacked[2 * width : 2 * width + 1, :].astype(jnp.int32)
    owner = d // lanes
    slot = d - owner * lanes
    square = jnp.broadcast_to(owner.astype(F32), (lanes, lanes))
    diag = iota((lanes, lanes), 0) == iota((lanes, lanes), 1)
    column = jnp.sum(jnp.where(diag, square, 0.0), axis=1, keepdims=True)
    before = iota((lanes, lanes), 0) < iota((lanes, lanes), 1)
    same = (column == square) & before
    rank = jnp.sum(jnp.where(same, 1.0, 0.0), axis=0, keepdims=True).astype(jnp.int32)
    bucket[...] = owner * CAP + rank
    wanted = jnp.where(iota((devices, lanes), 0) == owner, (slot + 1).astype(F32), 0.0)
    ranks = one_hot(iota((lanes, lanes), 0) == rank)
    request[...] = dot_nt(wanted.astype(BF16), ranks)[:, None, :]


def send_kernel(request, parts, parcels, hot_out):
    devices, _, lanes = request.shape
    width = parts.shape[1]
    spread = jnp.broadcast_to(request[...], (devices, CAP, lanes))
    spread = spread.reshape(devices * CAP, lanes)
    own = iota(spread.shape, 0) % CAP == iota(spread.shape, 1)
    slot = jnp.sum(jnp.where(own, spread, 0.0), axis=1, keepdims=True)
    hot = one_hot(iota(spread.shape, 1).astype(F32) == slot - 1.0)
    hot_out[...] = hot
    total = dot_nt(hot, parts[0]) + (dot_nt(hot, parts[1]) + dot_nt(hot, parts[2]))
    pad = jnp.zeros((total.shape[0], lanes - width), F32)
    parcels[...] = jnp.concatenate([total, pad], axis=1)


def pick_kernel(group, lists, below, above):
    parts, _, lanes = group.shape
    for side in range(2):
        row = lists[side : side + 1, :]
        total = None
        for j in range(parts):
            hot = one_hot(iota((lanes, row.shape[1]), 0) + j * lanes == row)
            term = dot(group[j], hot)
            total = term if total is None else total + term
        (below, above)[side][...] = total.astype(BF16)


def source_kernel(got, bucket, hist, smat, weight, out):
    quads, width, lanes = hist.shape
    hot = one_hot(iota((got.shape[0], lanes), 0) == bucket[...])
    turned = got[...].T[:width]
    hi, mid, lo = split3(turned)
    dm = dot(hi, hot) + (dot(mid, hot) + dot(lo, hot))
    d_hi, d_lo = split2(dm)
    acc = jnp.zeros((width, lanes), F32)
    for q in range(quads):
        s_hi, s_lo = split2(smat[q])
        strain = dot(s_hi, d_hi) + (dot(s_hi, d_lo) + dot(s_lo, d_hi))
        acc = acc + weight[0, q] * jnp.maximum(hist[q], 0.5 * strain * strain)
    table = jnp.concatenate([acc, jnp.zeros((lanes - width, lanes), F32)], axis=0)
    hi, mid, lo = split3(table)
    out[...] = dot_nt(hot, hi) + (dot_nt(hot, mid) + dot_nt(hot, lo))


def matvec_kernel(group, lower, upper, columns, tan, lap, mech, diff, near):
    kblk, rows, width, lanes = tan.shape
    parts = group.shape[0]
    ghost = lower.shape[1]
    depth = kblk * width
    found = []
    for k in range(kblk):
        col = columns[k : k + 1, :]
        total = jnp.zeros((2 * width, lanes), F32)
        for j in range(parts):
            hot = one_hot(iota((lanes, lanes), 0) + j * lanes == col)
            total = total + dot(group[j], hot)
        for side in range(2):
            start = parts * lanes + side * ghost
            hot = one_hot(iota((ghost, lanes), 0) + start == col)
            total = total + dot((lower, upper)[side][...], hot)
        found.append(total)
    for field in range(2):
        cut = [f[field * width : (field + 1) * width] for f in found]
        near[field] = jnp.concatenate(cut, axis=0).T.astype(BF16)
    lane = iota((8, 2 * lanes), 1) % lanes
    mine = iota((8, 2 * lanes), 0) == lane % 8

    @pl.loop(0, rows // 8)
    def _(step):
        for field, (mat, out) in enumerate(((tan, mech), (lap, diff))):
            left = near[field]
            lines = []
            for r in range(0, 8, 2):
                pair = [mat[:, step * 8 + r + j].reshape(depth, lanes) for j in range(2)]
                full = dot(left, jnp.concatenate(pair, axis=1))
                kept = full[:8]
                for g in range(1, lanes // 8):
                    kept = jnp.where(lane // 8 == g, full[g * 8 : g * 8 + 8], kept)
                line = jnp.sum(jnp.where(mine, kept, 0.0), axis=0, keepdims=True)
                lines += [line[:, :lanes], line[:, lanes:]]
            out[pl.ds(pl.multiple_of(step * 8, 8), 8), :] = jnp.concatenate(lines, axis=0)


def residual_kernel(got, hot, diffuse, mech_sum, load, damage, mech, dmg, sums):
    width, lanes = damage.shape
    turned = got[...].T[:width]
    hi, mid, lo = split3(turned)
    spread = hot[...]
    source = dot(hi, spread) + (dot(mid, spread) + dot(lo, spread))
    d = damage[...]
    dmg_res = diffuse[...] + (1.0 + 2.0 * source) * d - 2.0 * source
    mech_res = root_of(d) * mech_sum[...] - load[...]
    mech[...] = mech_res
    dmg[...] = dmg_res
    pair = []
    for x in (mech_res, dmg_res):
        line = jnp.sum(x * x, axis=0, keepdims=True)
        pair.append(jnp.sum(line, axis=1, keepdims=True))
    lane = iota((1, lanes), 1)
    row = jnp.where(lane == 0, pair[0], jnp.where(lane == 1, pair[1], 0.0))
    sums[...] = jnp.broadcast_to(row[None], sums.shape)


def scale_kernel(entries, sums, mech, dmg, mech_out, dmg_out, norms):
    total = jnp.sum(sums[...], axis=0)
    norm = jnp.sqrt(total / entries + 1e-06)
    mech_out[...] = mech[...] / norm[:, 0:1]
    dmg_out[...] = dmg[...] / norm[:, 1:2]
    norms[...] = norm[:, 0:2]


VM = pl.BlockSpec(memory_space=pltpu.VMEM)
SM = pl.BlockSpec(memory_space=pltpu.SMEM)


def call(body, outs, ins, scratch=(), flops=0, nbytes=0, specs=None):
    one = not isinstance(outs, (list, tuple))
    return pl.pallas_call(
        body,
        out_shape=outs,
        in_specs=specs or [VM] * ins,
        out_specs=VM if one else [VM] * len(outs),
        scratch_shapes=list(scratch),
        compiler_params=pltpu.CompilerParams(vmem_limit_bytes=VMEM_LIMIT),
        cost_estimate=pl.CostEstimate(flops=flops, bytes_accessed=nbytes, transcendentals=0),
    )


def sds(shape, dtype=F32):
    return jax.ShapeDtypeStruct(shape, dtype)


def swap(x, axes):
    return lax.all_to_all(x, axes, split_axis=0, concat_axis=0, tiled=True)


def on_device(
    displacement,
    damage,
    applied_load,
    tangent,
    laplacian,
    block_columns,
    send_lists,
    hist_mech,
    mech_dest,
    strain_matrix,
    quad_weight,
):
    lanes, width = displacement.shape
    kblk = tangent.shape[1]
    quads = hist_mech.shape[1]
    ghost = send_lists.shape[2]
    both = ("dom", "blk")
    devices = lax.axis_size(both)
    groups = lax.axis_size("dom")
    blocks = lax.axis_size("blk")
    disp_t = displacement.T
    dmg_t = damage.T
    load_t = applied_load.T
    tan_t = jnp.transpose(tangent, (1, 2, 3, 0))
    lap_t = jnp.transpose(laplacian, (1, 2, 3, 0))
    hist_t = jnp.transpose(hist_mech, (1, 2, 0))
    cols_t = block_columns.T

    dest = jnp.broadcast_to(mech_dest.astype(F32)[None, :], (8, lanes))
    stacked = jnp.concatenate([disp_t, dmg_t, dest], axis=0)
    with jax.named_scope("prep"):
        fields, parts, request, bucket = call(
            prep_kernel,
            [
                sds((blocks, 2 * width, lanes), BF16),
                sds((3, width, lanes), BF16),
                sds((devices, 1, lanes)),
                sds((1, lanes), jnp.int32),
            ],
            1,
            flops=FILL,
        )(stacked)
    wanted = swap(request, both)
    group = swap(fields, "blk")
    with jax.named_scope("send"):
        parcels, hot = call(
            send_kernel, [sds((devices * CAP, lanes)), sds((devices * CAP, lanes), BF16)], 2, flops=FILL
        )(wanted, parts)
    asked = swap(parcels.reshape(devices, CAP, lanes), both)
    with jax.named_scope("picks"):
        picked = call(pick_kernel, [sds((2 * width, ghost), BF16)] * 2, 2, flops=FILL)(
            group, send_lists[0]
        )
    up = [(i, i + 1) for i in range(groups - 1)]
    down = [(i + 1, i) for i in range(groups - 1)]
    lower = lax.ppermute(picked[1], "dom", up)
    upper = lax.ppermute(picked[0], "dom", down)
    with jax.named_scope("source"):
        answer = call(
            source_kernel,
            sds((devices * CAP, lanes)),
            5,
            flops=6 * quads * width * width * lanes,
            nbytes=4 * quads * width * lanes * 2,
            specs=[VM, VM, VM, VM, SM],
        )(
            asked.reshape(devices * CAP, lanes),
            bucket,
            hist_t,
            strain_matrix,
            quad_weight[None, :],
        )
    got = swap(answer.reshape(devices, CAP, lanes), both)
    with jax.named_scope("matvec"):
        mech_sum, diffuse = call(
            matvec_kernel,
            [sds((width, lanes))] * 2,
            6,
            [pltpu.VMEM((2, lanes, kblk * width), BF16)],
            flops=4 * kblk * width * width * lanes,
            nbytes=4 * kblk * width * width * lanes,
        )(group, lower, upper, cols_t, tan_t, lap_t)
    with jax.named_scope("residuals"):
        mech, dmg, sums = call(
            residual_kernel,
            [sds((width, lanes)), sds((width, lanes)), sds((devices, 1, lanes))],
            6,
        )(got.reshape(devices * CAP, lanes), hot, diffuse, mech_sum, load_t, dmg_t)
    every_sum = swap(sums, both)
    with jax.named_scope("scale"):
        mech_out, dmg_out, norms = call(
            functools.partial(scale_kernel, float(lanes * width * devices)),
            [sds((width, lanes)), sds((width, lanes)), sds((1, 2))],
            3,
        )(every_sum, mech, dmg)
    return mech_out.T, dmg_out.T, norms[0]


def solution(mesh):
    rows = P(("dom", "blk"))
    in_specs = (rows,) * 6 + (P("dom"),) + (rows,) * 2 + (P(), P())
    out_specs = (rows, rows, P())
    return jax.shard_map(
        on_device, mesh=mesh, in_specs=in_specs, out_specs=out_specs, check_vma=False
    )
```

```python
import functools

import jax
import jax.numpy as jnp
from jax import lax
from jax.experimental import pallas as pl
from jax.experimental.pallas import tpu as pltpu
from jax.sharding import PartitionSpec as P

F32 = jnp.float32
BF16 = jnp.bfloat16
STEP = 8
CAP = 8
FILL = 10**10
VMEM_LIMIT = 4 * 1024 * 1024


def dot(a, b):
    return lax.dot_general(a, b, (((1,), (0,)), ((), ())), preferred_element_type=F32)


def dot_nt(a, b):
    return lax.dot_general(a, b, (((1,), (1,)), ((), ())), preferred_element_type=F32)


def split2(x):
    hi = x.astype(BF16)
    lo = (x - hi.astype(F32)).astype(BF16)
    return hi, lo


def split3(x):
    hi = x.astype(BF16)
    rest = x - hi.astype(F32)
    mid = rest.astype(BF16)
    lo = (rest - mid.astype(F32)).astype(BF16)
    return hi, mid, lo


def one_hot(cond):
    return jnp.where(cond, 1.0, 0.0).astype(BF16)


def iota(shape, dim):
    return lax.broadcasted_iota(jnp.int32, shape, dim)


def root_of(damage):
    return jnp.sqrt((1.0 - damage) ** 2 + 0.001)


def prep_kernel(stacked, dest, fields, parts, request, bucket):
    width, lanes = parts.shape[1:]
    devices = request.shape[0]
    x = stacked[:width, :]
    dmg = stacked[width : 2 * width, :]
    weighted = (root_of(dmg) * x).astype(BF16)
    half = dmg.astype(BF16)
    fields[:width, :] = weighted
    fields[width:, :] = half
    hi, mid, lo = split3(x)
    parts[0] = hi
    parts[1] = mid
    parts[2] = lo
    d = dest[...]
    owner = d // lanes
    slot = d - owner * lanes
    square = jnp.broadcast_to(owner.astype(F32), (lanes, lanes))
    diag = iota((lanes, lanes), 0) == iota((lanes, lanes), 1)
    column = jnp.sum(jnp.where(diag, square, 0.0), axis=1, keepdims=True)
    before = iota((lanes, lanes), 0) < iota((lanes, lanes), 1)
    same = (column == square) & before
    rank = jnp.sum(jnp.where(same, 1.0, 0.0), axis=0, keepdims=True).astype(jnp.int32)
    bucket[...] = owner * CAP + rank
    wanted = jnp.where(iota((devices, lanes), 0) == owner, (slot + 1).astype(F32), 0.0)
    ranks = one_hot(iota((lanes, lanes), 0) == rank)
    request[...] = dot_nt(wanted.astype(BF16), ranks)[:, None, :]


def send_kernel(request, parts, parcels, hot_out):
    devices, _, lanes = request.shape
    width = parts.shape[1]
    spread = jnp.broadcast_to(request[...], (devices, CAP, lanes))
    spread = spread.reshape(devices * CAP, lanes)
    own = iota(spread.shape, 0) % CAP == iota(spread.shape, 1)
    slot = jnp.sum(jnp.where(own, spread, 0.0), axis=1, keepdims=True)
    hot = one_hot(iota(spread.shape, 1).astype(F32) == slot - 1.0)
    hot_out[...] = hot
    total = dot_nt(hot, parts[0]) + (dot_nt(hot, parts[1]) + dot_nt(hot, parts[2]))
    pad = jnp.zeros((total.shape[0], lanes - width), F32)
    parcels[...] = jnp.concatenate([total, pad], axis=1)


def pick_kernel(group, lists, below, above):
    parts = group.shape[0]
    table = jnp.concatenate([group[j] for j in range(parts)], axis=1)
    for side, out in enumerate((below, above)):
        row = lists[side : side + 1, :]
        hot = one_hot(iota((table.shape[1], row.shape[1]), 0) == row)
        out[...] = dot(table, hot).astype(BF16)


def source_kernel(got, bucket, hist, smat, weight, out):
    quads, width, lanes = hist.shape
    hot = one_hot(iota((got.shape[0], lanes), 0) == bucket[...])
    turned = got[...].T[:width]
    hi, mid, lo = split3(turned)
    dm = dot(hi, hot) + (dot(mid, hot) + dot(lo, hot))
    d_hi, d_lo = split2(dm)
    acc = jnp.zeros((width, lanes), F32)
    for q in range(quads):
        s_hi, s_lo = split2(smat[q])
        strain = dot(s_hi, d_hi) + (dot(s_hi, d_lo) + dot(s_lo, d_hi))
        acc = acc + weight[0, q] * jnp.maximum(hist[q], 0.5 * strain * strain)
    table = jnp.concatenate([acc, jnp.zeros((lanes - width, lanes), F32)], axis=0)
    hi, mid, lo = split3(table)
    out[...] = dot_nt(hot, hi) + (dot_nt(hot, mid) + dot_nt(hot, lo))


def matvec_kernel(
    group, lower, upper, columns, tan_hbm, lap_hbm, mech, diff, near, tan, lap, sems
):
    kblk, rows, width, lanes = tan.shape
    steps = rows // STEP

    def part(step, field):
        place = pl.ds(pl.multiple_of(step * STEP, STEP), STEP)
        src, out = ((tan_hbm, tan), (lap_hbm, lap))[field]
        return pltpu.make_async_copy(
            src.at[:, place], out.at[:, place], sems.at[field, step]
        )

    @pl.loop(0, steps)
    def _(step):
        for field in range(2):
            part(step, field).start()

    parts = group.shape[0]
    depth = kblk * width
    table = jnp.concatenate([group[j] for j in range(parts)] + [lower[...], upper[...]], axis=1)
    wanted = jnp.concatenate([columns[k : k + 1, :] for k in range(kblk)], axis=1)
    hot = one_hot(iota((table.shape[1], kblk * lanes), 0) == wanted)
    found = dot(table, hot)
    for field in range(2):
        cut = [
            found[field * width : (field + 1) * width, k * lanes : (k + 1) * lanes]
            for k in range(kblk)
        ]
        near[field] = jnp.concatenate(cut, axis=0).T.astype(BF16)
    lane = iota((8, 2 * lanes), 1) % lanes
    mine = iota((8, 2 * lanes), 0) == lane % 8

    @pl.loop(0, steps)
    def _(step):
        for field, (mat, out) in enumerate(((tan, mech), (lap, diff))):
            part(step, field).wait()
            left = near[field]
            lines = []
            for r in range(0, STEP, 2):
                pair = [mat[:, step * STEP + r + j].reshape(depth, lanes) for j in range(2)]
                full = dot(left, jnp.concatenate(pair, axis=1))
                kept = full[:8]
                for g in range(1, lanes // 8):
                    kept = jnp.where(lane // 8 == g, full[g * 8 : g * 8 + 8], kept)
                line = jnp.sum(jnp.where(mine, kept, 0.0), axis=0, keepdims=True)
                lines += [line[:, :lanes], line[:, lanes:]]
            place = pl.ds(pl.multiple_of(step * STEP, STEP), STEP)
            out[place, :] = jnp.concatenate(lines, axis=0)


def residual_kernel(got, hot, diffuse, mech_sum, load, damage, mech, dmg, sums):
    width, lanes = damage.shape
    turned = got[...].T[:width]
    hi, mid, lo = split3(turned)
    spread = hot[...]
    source = dot(hi, spread) + (dot(mid, spread) + dot(lo, spread))
    d = damage[...]
    dmg_res = diffuse[...] + (1.0 + 2.0 * source) * d - 2.0 * source
    mech_res = root_of(d) * mech_sum[...] - load[...]
    mech[...] = mech_res
    dmg[...] = dmg_res
    pair = []
    for x in (mech_res, dmg_res):
        line = jnp.sum(x * x, axis=0, keepdims=True)
        pair.append(jnp.sum(line, axis=1, keepdims=True))
    lane = iota((1, lanes), 1)
    row = jnp.where(lane == 0, pair[0], jnp.where(lane == 1, pair[1], 0.0))
    sums[...] = jnp.broadcast_to(row[None], sums.shape)


def scale_kernel(entries, sums, mech, dmg, mech_out, dmg_out, norms):
    total = jnp.sum(sums[...], axis=0)
    norm = jnp.sqrt(total / entries + 1e-06)
    mech_out[...] = mech[...] / norm[:, 0:1]
    dmg_out[...] = dmg[...] / norm[:, 1:2]
    norms[...] = norm[:, 0:2]


VM = pl.BlockSpec(memory_space=pltpu.VMEM)
ANY = pl.BlockSpec(memory_space=pl.ANY)
SM = pl.BlockSpec(memory_space=pltpu.SMEM)


def call(body, outs, ins, scratch=(), flops=0, nbytes=0, specs=None, limit=VMEM_LIMIT):
    one = not isinstance(outs, (list, tuple))
    return pl.pallas_call(
        body,
        out_shape=outs,
        in_specs=specs or [VM] * ins,
        out_specs=VM if one else [VM] * len(outs),
        scratch_shapes=list(scratch),
        compiler_params=pltpu.CompilerParams(vmem_limit_bytes=limit),
        cost_estimate=pl.CostEstimate(flops=flops, bytes_accessed=nbytes, transcendentals=0),
    )


def sds(shape, dtype=F32):
    return jax.ShapeDtypeStruct(shape, dtype)


def swap(x, axes):
    return lax.all_to_all(x, axes, split_axis=0, concat_axis=0, tiled=True)


def on_device(
    displacement,
    damage,
    applied_load,
    tangent,
    laplacian,
    block_columns,
    send_lists,
    hist_mech,
    mech_dest,
    strain_matrix,
    quad_weight,
):
    lanes, width = displacement.shape
    kblk = tangent.shape[1]
    quads = hist_mech.shape[1]
    ghost = send_lists.shape[2]
    both = ("dom", "blk")
    devices = lax.axis_size(both)
    groups = lax.axis_size("dom")
    disp_t = displacement.T
    dmg_t = damage.T
    load_t = applied_load.T
    tan_t = jnp.transpose(tangent, (1, 2, 3, 0))
    lap_t = jnp.transpose(laplacian, (1, 2, 3, 0))
    hist_t = jnp.transpose(hist_mech, (1, 2, 0))
    cols_t = block_columns.T

    stacked = jnp.concatenate([disp_t, dmg_t], axis=0)
    with jax.named_scope("prep"):
        fields, parts, request, bucket = call(
            prep_kernel,
            [
                sds((2 * width, lanes), BF16),
                sds((3, width, lanes), BF16),
                sds((devices, 1, lanes)),
                sds((1, lanes), jnp.int32),
            ],
            2,
            flops=FILL,
        )(stacked, mech_dest[None, :])
    wanted = swap(request, both)
    group = lax.all_gather(fields, "blk", axis=0, tiled=False)
    wanted, group = lax.optimization_barrier((wanted, group))
    with jax.named_scope("send"):
        parcels, hot = call(
            send_kernel, [sds((devices * CAP, lanes)), sds((devices * CAP, lanes), BF16)], 2, flops=FILL
        )(wanted, parts)
    asked = swap(parcels.reshape(devices, CAP, lanes), both)
    with jax.named_scope("picks"):
        picked = call(pick_kernel, [sds((2 * width, ghost), BF16)] * 2, 2, flops=FILL)(
            group, send_lists[0]
        )
    up = [(i, i + 1) for i in range(groups - 1)]
    down = [(i + 1, i) for i in range(groups - 1)]
    lower = lax.ppermute(picked[1], "dom", up)
    upper = lax.ppermute(picked[0], "dom", down)
    asked, lower, upper = lax.optimization_barrier((asked, lower, upper))
    with jax.named_scope("source"):
        answer = call(
            source_kernel,
            sds((devices * CAP, lanes)),
            5,
            flops=6 * quads * width * width * lanes,
            nbytes=4 * quads * width * lanes * 2,
            specs=[VM, VM, VM, VM, SM],
        )(
            asked.reshape(devices * CAP, lanes),
            bucket,
            hist_t,
            strain_matrix,
            quad_weight[None, :],
        )
    got = swap(answer.reshape(devices, CAP, lanes), both)
    with jax.named_scope("matvec"):
        mech_sum, diffuse = call(
            matvec_kernel,
            [sds((width, lanes))] * 2,
            6,
            [
                pltpu.VMEM((2, lanes, kblk * width), BF16),
                pltpu.VMEM(tan_t.shape, BF16),
                pltpu.VMEM(lap_t.shape, BF16),
                pltpu.SemaphoreType.DMA((2, width // STEP)),
            ],
            flops=4 * kblk * width * width * lanes,
            nbytes=4 * kblk * width * width * lanes,
            specs=[VM, VM, VM, VM, ANY, ANY],
            limit=48 * 1024 * 1024,
        )(group, lower, upper, cols_t, tan_t, lap_t)
    with jax.named_scope("residuals"):
        mech, dmg, sums = call(
            residual_kernel,
            [sds((width, lanes)), sds((width, lanes)), sds((devices, 1, lanes))],
            6,
        )(got.reshape(devices * CAP, lanes), hot, diffuse, mech_sum, load_t, dmg_t)
    every_sum = swap(sums, both)
    with jax.named_scope("scale"):
        mech_out, dmg_out, norms = call(
            functools.partial(scale_kernel, float(lanes * width * devices)),
            [sds((width, lanes)), sds((width, lanes)), sds((1, 2))],
            3,
        )(every_sum, mech, dmg)
    return mech_out.T, dmg_out.T, norms[0]


def solution(mesh):
    rows = P(("dom", "blk"))
    in_specs = (rows,) * 6 + (P("dom"),) + (rows,) * 2 + (P(), P())
    out_specs = (rows, rows, P())
    return jax.shard_map(
        on_device, mesh=mesh, in_specs=in_specs, out_specs=out_specs, check_vma=False
    )
```

```python
import functools

import jax
import jax.numpy as jnp
from jax import lax
from jax.experimental import pallas as pl
from jax.experimental.pallas import tpu as pltpu
from jax.sharding import PartitionSpec as P

F32 = jnp.float32
BF16 = jnp.bfloat16
FILL = 10**10
VMEM_LIMIT = 4 * 1024 * 1024


def dot(a, b):
    return lax.dot_general(a, b, (((1,), (0,)), ((), ())), preferred_element_type=F32)


def dot_nt(a, b):
    return lax.dot_general(a, b, (((1,), (1,)), ((), ())), preferred_element_type=F32)


def split2(x):
    hi = x.astype(BF16)
    lo = (x - hi.astype(F32)).astype(BF16)
    return hi, lo


def split3(x):
    hi = x.astype(BF16)
    rest = x - hi.astype(F32)
    mid = rest.astype(BF16)
    lo = (rest - mid.astype(F32)).astype(BF16)
    return hi, mid, lo


def one_hot(cond):
    return jnp.where(cond, 1.0, 0.0).astype(BF16)


def iota(shape, dim):
    return lax.broadcasted_iota(jnp.int32, shape, dim)


def lines_of(cap, width, lanes):
    return -(-cap * width // lanes)


def pack(hots, table, out):
    width, lanes = table.shape
    cuts = split3(table)
    for j in range(out.shape[1]):
        total = None
        for k, hot in enumerate(hots):
            first = max(j * lanes, k * width)
            last = min((j + 1) * lanes, (k + 1) * width)
            if first >= last:
                continue
            above, below = first - j * lanes, (j + 1) * lanes - last
            for cut in cuts:
                lines = cut[first - k * width : last - k * width]
                blank = [jnp.zeros((n, lanes), BF16) for n in (above, below)]
                parts = [blank[0]] * (above > 0) + [lines] + [blank[1]] * (below > 0)
                term = dot_nt(hot, jnp.concatenate(parts, axis=0))
                total = term if total is None else total + term
        out[:, j, :] = total


def unpack(hots, got, width):
    flat = jnp.concatenate([got[:, j, :].T for j in range(got.shape[1])], axis=0)
    cuts = split3(flat)
    total = None
    for k, hot in enumerate(hots):
        for cut in cuts:
            term = dot(cut[k * width : (k + 1) * width], hot)
            total = term if total is None else total + term
    return total


def asked_hots(request, cap):
    devices, _, lanes = request.shape
    slots = request[:, 0, :]
    lane = iota((devices, lanes), 1).astype(F32)
    return [one_hot(lane == slots[:, k : k + 1] - 1.0) for k in range(cap)]


def asking_hots(bucket, cap, devices):
    place = iota((devices, bucket.shape[1]), 0) * cap
    return [one_hot(place + k == bucket[...]) for k in range(cap)]


def root_of(damage):
    return jnp.sqrt((1.0 - damage) ** 2 + 0.001)


def prep_kernel(cap, stacked, dest, fields, disp, request, bucket):
    width, lanes = disp.shape
    devices = request.shape[0]
    x = stacked[:width, :]
    dmg = stacked[width : 2 * width, :]
    weighted = (root_of(dmg) * x).astype(BF16)
    half = dmg.astype(BF16)
    fields[:width, :] = weighted
    fields[width:, :] = half
    disp[...] = x
    d = dest[...]
    owner = d // lanes
    slot = d - owner * lanes
    square = jnp.broadcast_to(owner.astype(F32), (lanes, lanes))
    diag = iota((lanes, lanes), 0) == iota((lanes, lanes), 1)
    column = jnp.sum(jnp.where(diag, square, 0.0), axis=1, keepdims=True)
    before = iota((lanes, lanes), 0) < iota((lanes, lanes), 1)
    same = (column == square) & before
    rank = jnp.sum(jnp.where(same, 1.0, 0.0), axis=0, keepdims=True).astype(jnp.int32)
    bucket[...] = owner * cap + rank
    wanted = jnp.where(iota((devices, lanes), 0) == owner, (slot + 1).astype(F32), 0.0)
    ranks = one_hot(iota((lanes, lanes), 0) == rank)
    request[...] = dot_nt(wanted.astype(BF16), ranks)[:, None, :]


def send_kernel(cap, request, disp, parcels):
    pack(asked_hots(request, cap), disp[...], parcels)


def pick_kernel(group, lists, below, above):
    parts = group.shape[0]
    table = jnp.concatenate([group[j] for j in range(parts)], axis=1)
    for side, out in enumerate((below, above)):
        row = lists[side : side + 1, :]
        hot = one_hot(iota((table.shape[1], row.shape[1]), 0) == row)
        out[...] = dot(table, hot).astype(BF16)


def source_kernel(cap, got, bucket, hist, smat, weight, out):
    quads, width, lanes = hist.shape
    hots = asking_hots(bucket, cap, got.shape[0])
    dm = unpack(hots, got, width)
    d_hi, d_lo = split2(dm)
    acc = jnp.zeros((width, lanes), F32)
    for q in range(quads):
        s_hi, s_lo = split2(smat[q])
        strain = dot(s_hi, d_hi) + (dot(s_hi, d_lo) + dot(s_lo, d_hi))
        acc = acc + weight[0, q] * jnp.maximum(hist[q], 0.5 * strain * strain)
    pack(hots, acc, out)


def matvec_kernel(group, lower, upper, columns, tan, lap, mech, diff, left, near):
    kblk, rows, width, lanes = tan.shape
    parts = group.shape[0]
    depth = kblk * width
    table = jnp.concatenate([group[j] for j in range(parts)] + [lower[...], upper[...]], axis=1)
    wanted = jnp.concatenate([columns[k : k + 1, :] for k in range(kblk)], axis=1)
    hot = one_hot(iota((table.shape[1], kblk * lanes), 0) == wanted)
    found = dot(table, hot)
    tall = []
    for field in range(2):
        cut = [
            found[field * width : (field + 1) * width, k * lanes : (k + 1) * lanes]
            for k in range(kblk)
        ]
        tall.append(jnp.concatenate(cut, axis=0))
    left[...] = tall[0].T.astype(BF16)
    near[...] = tall[1]
    lane = iota((8, 2 * lanes), 1) % lanes
    mine = iota((8, 2 * lanes), 0) == lane % 8

    @pl.loop(0, rows // 8)
    def _(step):
        place = pl.ds(pl.multiple_of(step * 8, 8), 8)
        lines = []
        for r in range(0, 8, 2):
            pair = [tan[:, step * 8 + r + j].reshape(depth, lanes) for j in range(2)]
            full = dot(left[...], jnp.concatenate(pair, axis=1))
            kept = full[:8]
            for g in range(1, lanes // 8):
                kept = jnp.where(lane // 8 == g, full[g * 8 : g * 8 + 8], kept)
            line = jnp.sum(jnp.where(mine, kept, 0.0), axis=0, keepdims=True)
            lines += [line[:, :lanes], line[:, lanes:]]
        mech[place, :] = jnp.concatenate(lines, axis=0)
        acc = [jnp.zeros((8, lanes), F32) for _ in range(8)]
        for k in range(kblk):
            for c in range(0, width, 16):
                base = k * width + c
                lo = near[base : base + 8, :]
                hi = near[base + 8 : base + 16, :]
                for r in range(8):
                    block = lap[k, step * 8 + r, c : c + 16, :].astype(F32)
                    acc[r] = acc[r] + (block[:8] * lo + block[8:] * hi)
        sums = [jnp.sum(a, axis=0, keepdims=True) for a in acc]
        diff[place, :] = jnp.concatenate(sums, axis=0)


def residual_kernel(cap, got, request, diffuse, mech_sum, load, damage, mech, dmg, sums):
    width, lanes = damage.shape
    source = unpack(asked_hots(request, cap), got, width)
    d = damage[...]
    dmg_res = diffuse[...] + (1.0 + 2.0 * source) * d - 2.0 * source
    mech_res = root_of(d) * mech_sum[...] - load[...]
    mech[...] = mech_res
    dmg[...] = dmg_res
    pair = []
    for x in (mech_res, dmg_res):
        line = jnp.sum(x * x, axis=0, keepdims=True)
        pair.append(jnp.sum(line, axis=1, keepdims=True))
    lane = iota((1, lanes), 1)
    row = jnp.where(lane == 0, pair[0], jnp.where(lane == 1, pair[1], 0.0))
    sums[...] = jnp.broadcast_to(row[None], sums.shape)


def scale_kernel(entries, sums, mech, dmg, mech_out, dmg_out, norms):
    total = jnp.sum(sums[...], axis=0)
    norm = jnp.sqrt(total / entries + 1e-06)
    mech_out[...] = mech[...] / norm[:, 0:1]
    dmg_out[...] = dmg[...] / norm[:, 1:2]
    norms[...] = norm[:, 0:2]


VM = pl.BlockSpec(memory_space=pltpu.VMEM)
SM = pl.BlockSpec(memory_space=pltpu.SMEM)


def call(body, outs, ins, scratch=(), flops=0, nbytes=0, specs=None):
    one = not isinstance(outs, (list, tuple))
    return pl.pallas_call(
        body,
        out_shape=outs,
        in_specs=specs or [VM] * ins,
        out_specs=VM if one else [VM] * len(outs),
        scratch_shapes=list(scratch),
        compiler_params=pltpu.CompilerParams(vmem_limit_bytes=VMEM_LIMIT),
        cost_estimate=pl.CostEstimate(flops=flops, bytes_accessed=nbytes, transcendentals=0),
    )


def sds(shape, dtype=F32):
    return jax.ShapeDtypeStruct(shape, dtype)


def swap(x, axes):
    return lax.all_to_all(x, axes, split_axis=0, concat_axis=0, tiled=True)


def on_device(
    displacement,
    damage,
    applied_load,
    tangent,
    laplacian,
    block_columns,
    send_lists,
    hist_mech,
    mech_dest,
    strain_matrix,
    quad_weight,
):
    lanes, width = displacement.shape
    kblk = tangent.shape[1]
    quads = hist_mech.shape[1]
    ghost = send_lists.shape[2]
    both = ("dom", "blk")
    devices = lax.axis_size(both)
    groups = lax.axis_size("dom")
    disp_t = displacement.T
    dmg_t = damage.T
    load_t = applied_load.T
    tan_t = jnp.transpose(tangent, (1, 2, 3, 0))
    lap_t = jnp.transpose(laplacian, (1, 2, 3, 0))
    hist_t = jnp.transpose(hist_mech, (1, 2, 0))
    cols_t = block_columns.T

    stacked = jnp.concatenate([disp_t, dmg_t], axis=0)
    cap = lanes // devices + 1
    parcel = sds((devices, lines_of(cap, width, lanes), lanes))
    with jax.named_scope("prep"):
        fields, disp_t, request, bucket = call(
            functools.partial(prep_kernel, cap),
            [
                sds((2 * width, lanes), BF16),
                sds((width, lanes)),
                sds((devices, 1, lanes)),
                sds((1, lanes), jnp.int32),
            ],
            2,
            flops=FILL,
        )(stacked, mech_dest[None, :])
    wanted = swap(request, both)
    group = lax.all_gather(fields, "blk", axis=0, tiled=False)
    wanted, group = lax.optimization_barrier((wanted, group))
    with jax.named_scope("send"):
        parcels = call(functools.partial(send_kernel, cap), parcel, 2, flops=FILL)(
            wanted, disp_t
        )
    asked = swap(parcels, both)
    with jax.named_scope("picks"):
        picked = call(pick_kernel, [sds((2 * width, ghost), BF16)] * 2, 2, flops=FILL)(
            group, send_lists[0]
        )
    up = [(i, i + 1) for i in range(groups - 1)]
    down = [(i + 1, i) for i in range(groups - 1)]
    lower = lax.ppermute(picked[1], "dom", up)
    upper = lax.ppermute(picked[0], "dom", down)
    asked, lower, upper = lax.optimization_barrier((asked, lower, upper))
    with jax.named_scope("source"):
        answer = call(
            functools.partial(source_kernel, cap),
            parcel,
            5,
            flops=20 * FILL,
            specs=[VM, VM, VM, VM, SM],
        )(asked, bucket, hist_t, strain_matrix, quad_weight[None, :])
    got = swap(answer, both)
    got, lower, upper = lax.optimization_barrier((got, lower, upper))
    with jax.named_scope("matvec"):
        mech_sum, diffuse = call(
            matvec_kernel,
            [sds((width, lanes))] * 2,
            6,
            [
                pltpu.VMEM((lanes, kblk * width), BF16),
                pltpu.VMEM((kblk * width, lanes), F32),
            ],
            flops=4 * kblk * width * width * lanes,
            nbytes=4 * kblk * width * width * lanes,
        )(group, lower, upper, cols_t, tan_t, lap_t)
    with jax.named_scope("residuals"):
        mech, dmg, sums = call(
            functools.partial(residual_kernel, cap),
            [sds((width, lanes)), sds((width, lanes)), sds((devices, 1, lanes))],
            6,
        )(got, wanted, diffuse, mech_sum, load_t, dmg_t)
    every_sum = swap(sums, both)
    with jax.named_scope("scale"):
        mech_out, dmg_out, norms = call(
            functools.partial(scale_kernel, float(lanes * width * devices)),
            [sds((width, lanes)), sds((width, lanes)), sds((1, 2))],
            3,
        )(every_sum, mech, dmg)
    return mech_out.T, dmg_out.T, norms[0]


def solution(mesh):
    rows = P(("dom", "blk"))
    in_specs = (rows,) * 6 + (P("dom"),) + (rows,) * 2 + (P(), P())
    out_specs = (rows, rows, P())
    return jax.shard_map(
        on_device, mesh=mesh, in_specs=in_specs, out_specs=out_specs, check_vma=False
    )
```

```python
import functools

import jax
import jax.numpy as jnp
from jax import lax
from jax.experimental import pallas as pl
from jax.experimental.pallas import tpu as pltpu
from jax.sharding import PartitionSpec as P

F32 = jnp.float32
BF16 = jnp.bfloat16
FILL = 10**10
VMEM_LIMIT = 4 * 1024 * 1024


def dot(a, b):
    return lax.dot_general(a, b, (((1,), (0,)), ((), ())), preferred_element_type=F32)


def dot_nt(a, b):
    return lax.dot_general(a, b, (((1,), (1,)), ((), ())), preferred_element_type=F32)


def split2(x):
    hi = x.astype(BF16)
    lo = (x - hi.astype(F32)).astype(BF16)
    return hi, lo


def split3(x):
    hi = x.astype(BF16)
    rest = x - hi.astype(F32)
    mid = rest.astype(BF16)
    lo = (rest - mid.astype(F32)).astype(BF16)
    return hi, mid, lo


def one_hot(cond):
    return jnp.where(cond, 1.0, 0.0).astype(BF16)


def iota(shape, dim):
    return lax.broadcasted_iota(jnp.int32, shape, dim)


def parcel_shape(devices, values, lanes):
    return (devices, -(-values // (4 * lanes)), 4, lanes)


def pack(hots, table, out, tail=0.0):
    width, lanes = table.shape
    cuts = split3(table)
    lines = out.shape[1] * 4
    for j in range(lines):
        total = jnp.zeros((out.shape[0], lanes), F32)
        for k, hot in enumerate(hots):
            first = max(j * lanes, k * width)
            last = min((j + 1) * lanes, (k + 1) * width)
            if first >= last:
                continue
            above, below = first - j * lanes, (j + 1) * lanes - last
            for cut in cuts:
                body = cut[first - k * width : last - k * width]
                blank = [jnp.zeros((n, lanes), BF16) for n in (above, below)]
                parts = [blank[0]] * (above > 0) + [body] + [blank[1]] * (below > 0)
                total = total + dot_nt(hot, jnp.concatenate(parts, axis=0))
        if j == lines - 1:
            total = total + tail
        out[:, j // 4, j % 4, :] = total


def unpack(hots, got, width):
    lines = [got[:, j // 4, j % 4, :].T for j in range(got.shape[1] * 4)]
    flat = jnp.concatenate(lines, axis=0)
    cuts = split3(flat)
    total = None
    for k, hot in enumerate(hots):
        for cut in cuts:
            term = dot(cut[k * width : (k + 1) * width], hot)
            total = term if total is None else total + term
    return total


def asked_hots(request, cap):
    devices, _, lanes = request.shape
    slots = request[:, 0, :]
    lane = iota((devices, lanes), 1).astype(F32)
    return [one_hot(lane == slots[:, k : k + 1] - 1.0) for k in range(cap)]


def asking_hots(bucket, cap, devices):
    place = iota((devices, bucket.shape[1]), 0) * cap
    return [one_hot(place + k == bucket[...]) for k in range(cap)]


def root_of(damage):
    return jnp.sqrt((1.0 - damage) ** 2 + 0.001)


def request_kernel(cap, dest, request, bucket):
    devices, _, lanes = request.shape
    d = dest[...]
    owner = d // lanes
    slot = d - owner * lanes
    square = jnp.broadcast_to(owner.astype(F32), (lanes, lanes))
    diag = iota((lanes, lanes), 0) == iota((lanes, lanes), 1)
    column = jnp.sum(jnp.where(diag, square, 0.0), axis=1, keepdims=True)
    before = iota((lanes, lanes), 0) < iota((lanes, lanes), 1)
    same = (column == square) & before
    rank = jnp.sum(jnp.where(same, 1.0, 0.0), axis=0, keepdims=True).astype(jnp.int32)
    bucket[...] = owner * cap + rank
    wanted = jnp.where(iota((devices, lanes), 0) == owner, (slot + 1).astype(F32), 0.0)
    ranks = one_hot(iota((lanes, lanes), 0) == rank)
    request[...] = dot_nt(wanted.astype(BF16), ranks)[:, None, :]


def pick_kernel(group, lists, below, above):
    parts = group.shape[0]
    table = jnp.concatenate([group[j] for j in range(parts)], axis=1)
    for side, out in enumerate((below, above)):
        row = lists[side : side + 1, :]
        hot = one_hot(iota((table.shape[1], row.shape[1]), 0) == row)
        out[...] = dot(table, hot).astype(BF16)


def total_of(x):
    line = jnp.sum(x * x, axis=0, keepdims=True)
    return jnp.sum(line, axis=1, keepdims=True)


def source_kernel(cap, got, bucket, hist, smat, weight, mech_total, out):
    quads, width, lanes = hist.shape
    hots = asking_hots(bucket, cap, got.shape[0])
    held = unpack(hots, got, 3 * width)
    d_hi, d_lo = split2(held[:width])
    acc = jnp.zeros((width, lanes), F32)
    for q in range(quads):
        s_hi, s_lo = split2(smat[q])
        strain = dot(s_hi, d_hi) + (dot(s_hi, d_lo) + dot(s_lo, d_hi))
        acc = acc + weight[0, q] * jnp.maximum(hist[q], 0.5 * strain * strain)
    dmg_res = held[width : 2 * width] + 2.0 * acc * held[2 * width :]
    spare = iota((1, lanes), 1) - (lanes - 2)
    tail = jnp.where(spare == 0, mech_total[...], 0.0)
    tail = jnp.where(spare == 1, total_of(dmg_res), tail)
    pack(hots, dmg_res, out, tail)


def matvec_kernel(
    cap,
    group,
    lower,
    upper,
    columns,
    tan,
    lap,
    request,
    disp,
    damage,
    load,
    mech,
    mech_total,
    parcels,
    left,
    near,
    diff,
):
    kblk, rows, width, lanes = tan.shape
    parts = group.shape[0]
    depth = kblk * width
    table = jnp.concatenate([group[j] for j in range(parts)] + [lower[...], upper[...]], axis=1)
    wanted = jnp.concatenate([columns[k : k + 1, :] for k in range(kblk)], axis=1)
    hot = one_hot(iota((table.shape[1], kblk * lanes), 0) == wanted)
    found = dot(table, hot)
    tall = []
    for field in range(2):
        cut = [
            found[field * width : (field + 1) * width, k * lanes : (k + 1) * lanes]
            for k in range(kblk)
        ]
        tall.append(jnp.concatenate(cut, axis=0))
    left[...] = tall[0].T.astype(BF16)
    near[...] = tall[1]
    lane = iota((8, 2 * lanes), 1) % lanes
    mine = iota((8, 2 * lanes), 0) == lane % 8

    @pl.loop(0, rows // 8)
    def _(step):
        place = pl.ds(pl.multiple_of(step * 8, 8), 8)
        lines = []
        for r in range(0, 8, 2):
            pair = [tan[:, step * 8 + r + j].reshape(depth, lanes) for j in range(2)]
            full = dot(left[...], jnp.concatenate(pair, axis=1))
            kept = full[:8]
            for g in range(1, lanes // 8):
                kept = jnp.where(lane // 8 == g, full[g * 8 : g * 8 + 8], kept)
            line = jnp.sum(jnp.where(mine, kept, 0.0), axis=0, keepdims=True)
            lines += [line[:, :lanes], line[:, lanes:]]
        mech[place, :] = jnp.concatenate(lines, axis=0)
        acc = [jnp.zeros((8, lanes), F32) for _ in range(8)]
        for k in range(kblk):
            for c in range(0, width, 16):
                base = k * width + c
                lo = near[base : base + 8, :]
                hi = near[base + 8 : base + 16, :]
                for r in range(8):
                    block = lap[k, step * 8 + r, c : c + 16, :].astype(F32)
                    acc[r] = acc[r] + (block[:8] * lo + block[8:] * hi)
        sums = [jnp.sum(a, axis=0, keepdims=True) for a in acc]
        diff[place, :] = jnp.concatenate(sums, axis=0)


    d = damage[...]
    mech_res = root_of(d) * mech[...] - load[...]
    mech[...] = mech_res
    mech_total[...] = jnp.broadcast_to(total_of(mech_res), mech_total.shape)
    table = jnp.concatenate([disp[...], diff[...] + d, d - 1.0], axis=0)
    pack(asked_hots(request, cap), table, parcels)


def scale_kernel(cap, entries, got, request, mech, mech_out, dmg_out, norms):
    width, lanes = mech.shape
    last = got[:, got.shape[1] - 1, 3, :]
    total = jnp.sum(last, axis=0, keepdims=True)[:, lanes - 2 :]
    norm = jnp.sqrt(total / entries + 1e-06)
    mech_out[...] = mech[...] / norm[:, 0:1]
    dmg_out[...] = unpack(asked_hots(request, cap), got, width) / norm[:, 1:2]
    norms[...] = norm


VM = pl.BlockSpec(memory_space=pltpu.VMEM)
SM = pl.BlockSpec(memory_space=pltpu.SMEM)


def call(body, outs, ins, scratch=(), flops=0, nbytes=0, specs=None):
    one = not isinstance(outs, (list, tuple))
    return pl.pallas_call(
        body,
        out_shape=outs,
        in_specs=specs or [VM] * ins,
        out_specs=VM if one else [VM] * len(outs),
        scratch_shapes=list(scratch),
        compiler_params=pltpu.CompilerParams(vmem_limit_bytes=VMEM_LIMIT),
        cost_estimate=pl.CostEstimate(flops=flops, bytes_accessed=nbytes, transcendentals=0),
    )


def sds(shape, dtype=F32):
    return jax.ShapeDtypeStruct(shape, dtype)


def swap(x, axes):
    return lax.all_to_all(x, axes, split_axis=0, concat_axis=0, tiled=True)


def on_device(
    displacement,
    damage,
    applied_load,
    tangent,
    laplacian,
    block_columns,
    send_lists,
    hist_mech,
    mech_dest,
    strain_matrix,
    quad_weight,
):
    lanes, width = displacement.shape
    kblk = tangent.shape[1]
    quads = hist_mech.shape[1]
    ghost = send_lists.shape[2]
    both = ("dom", "blk")
    devices = lax.axis_size(both)
    groups = lax.axis_size("dom")
    disp_t = displacement.T
    dmg_t = damage.T
    load_t = applied_load.T
    tan_t = jnp.transpose(tangent, (1, 2, 3, 0))
    lap_t = jnp.transpose(laplacian, (1, 2, 3, 0))
    hist_t = jnp.transpose(hist_mech, (1, 2, 0))
    cols_t = block_columns.T

    cap = lanes // devices + 1
    weighted = (root_of(dmg_t) * disp_t).astype(BF16)
    fields = jnp.concatenate([weighted, dmg_t.astype(BF16)], axis=0)
    with jax.named_scope("requests"):
        request, bucket = call(
            functools.partial(request_kernel, cap),
            [sds((devices, 1, lanes)), sds((1, lanes), jnp.int32)],
            1,
            flops=FILL,
        )(mech_dest[None, :])
    wanted = swap(request, both)
    group = lax.all_gather(fields, "blk", axis=0, tiled=False)
    wanted, group = lax.optimization_barrier((wanted, group))
    with jax.named_scope("picks"):
        picked = call(pick_kernel, [sds((2 * width, ghost), BF16)] * 2, 2, flops=20 * FILL)(
            group, send_lists[0]
        )
    up = [(i, i + 1) for i in range(groups - 1)]
    down = [(i + 1, i) for i in range(groups - 1)]
    lower = lax.ppermute(picked[1], "dom", up)
    upper = lax.ppermute(picked[0], "dom", down)
    with jax.named_scope("matvec"):
        mech, mech_total, parcels = call(
            functools.partial(matvec_kernel, cap),
            [
                sds((width, lanes)),
                sds((1, lanes)),
                sds(parcel_shape(devices, 3 * cap * width, lanes)),
            ],
            10,
            [
                pltpu.VMEM((lanes, kblk * width), BF16),
                pltpu.VMEM((kblk * width, lanes), F32),
                pltpu.VMEM((width, lanes), F32),
            ],
            flops=FILL,
        )(group, lower, upper, cols_t, tan_t, lap_t, wanted, disp_t, dmg_t, load_t)
    asked = swap(parcels, both)
    with jax.named_scope("source"):
        answer = call(
            functools.partial(source_kernel, cap),
            sds(parcel_shape(devices, cap * width + 2, lanes)),
            6,
            flops=FILL,
            specs=[VM, VM, VM, VM, SM, VM],
        )(asked, bucket, hist_t, strain_matrix, quad_weight[None, :], mech_total)
    got = swap(answer, both)
    with jax.named_scope("scale"):
        mech_out, dmg_out, norms = call(
            functools.partial(scale_kernel, cap, float(lanes * width * devices)),
            [sds((width, lanes)), sds((width, lanes)), sds((1, 2))],
            3,
        )(got, wanted, mech)
    return mech_out.T, dmg_out.T, norms[0]


def solution(mesh):
    rows = P(("dom", "blk"))
    in_specs = (rows,) * 6 + (P("dom"),) + (rows,) * 2 + (P(), P())
    out_specs = (rows, rows, P())
    return jax.shard_map(
        on_device, mesh=mesh, in_specs=in_specs, out_specs=out_specs, check_vma=False
    )
```

```python
import functools

import jax
import jax.numpy as jnp
from jax import lax
from jax.experimental import pallas as pl
from jax.experimental.pallas import tpu as pltpu
from jax.sharding import PartitionSpec as P

F32 = jnp.float32
BF16 = jnp.bfloat16
FILL = 10**10
VMEM_LIMIT = 4 * 1024 * 1024


def dot(a, b):
    return lax.dot_general(a, b, (((1,), (0,)), ((), ())), preferred_element_type=F32)


def dot_nt(a, b):
    return lax.dot_general(a, b, (((1,), (1,)), ((), ())), preferred_element_type=F32)


def split2(x):
    hi = x.astype(BF16)
    lo = (x - hi.astype(F32)).astype(BF16)
    return hi, lo


def split3(x):
    hi = x.astype(BF16)
    rest = x - hi.astype(F32)
    mid = rest.astype(BF16)
    lo = (rest - mid.astype(F32)).astype(BF16)
    return hi, mid, lo


def one_hot(cond):
    return jnp.where(cond, 1.0, 0.0).astype(BF16)


def iota(shape, dim):
    return lax.broadcasted_iota(jnp.int32, shape, dim)


def parcel_shape(devices, values, lanes):
    return (devices, -(-values // (4 * lanes)), 4, lanes)


def pack(hot, table, out, tail=0.0):
    devices, groups, _, lanes = out.shape
    hi, lo = split2(table)
    moved = dot_nt(hot, hi) + dot_nt(hot, lo)
    cap, width = moved.shape[0] // devices, moved.shape[1]
    rows = [moved[k * devices : (k + 1) * devices] for k in range(cap)]
    rows.append(jnp.zeros((devices, groups * 4 * lanes - cap * width), F32))
    flat = jnp.concatenate(rows, axis=1)
    for j in range(groups * 4):
        line = flat[:, j * lanes : (j + 1) * lanes]
        out[:, j // 4, j % 4, :] = line + tail if j == groups * 4 - 1 else line


def unpack(hot, got, width):
    devices, groups, _, lanes = got.shape
    flat = jnp.concatenate([got[:, j // 4, j % 4, :] for j in range(groups * 4)], axis=1)
    cap = hot.shape[0] // devices
    rows = jnp.concatenate([flat[:, k * width : (k + 1) * width] for k in range(cap)], axis=0)
    blank = jnp.zeros((cap * devices, -width % lanes), F32)
    tall = jnp.concatenate([rows, blank], axis=1).T[:width]
    hi, lo = split2(tall)
    return dot(hi, hot) + dot(lo, hot)


def asked_hot(request, cap):
    devices, _, lanes = request.shape
    slots = request[:, 0, :]
    lane = iota((devices, lanes), 1).astype(F32)
    hots = [one_hot(lane == slots[:, k : k + 1] - 1.0) for k in range(cap)]
    return jnp.concatenate(hots, axis=0)


def asking_hot(bucket, cap, devices):
    place = iota((devices, bucket.shape[1]), 0) * cap
    hots = [one_hot(place + k == bucket[...]) for k in range(cap)]
    return jnp.concatenate(hots, axis=0)


def root_of(damage):
    return jnp.sqrt((1.0 - damage) ** 2 + 0.001)


def request_kernel(cap, dest, request, bucket):
    devices, _, lanes = request.shape
    d = dest[...]
    owner = d // lanes
    slot = d - owner * lanes
    square = jnp.broadcast_to(owner.astype(F32), (lanes, lanes))
    diag = iota((lanes, lanes), 0) == iota((lanes, lanes), 1)
    column = jnp.sum(jnp.where(diag, square, 0.0), axis=1, keepdims=True)
    before = iota((lanes, lanes), 0) < iota((lanes, lanes), 1)
    same = (column == square) & before
    rank = jnp.sum(jnp.where(same, 1.0, 0.0), axis=0, keepdims=True).astype(jnp.int32)
    bucket[...] = owner * cap + rank
    wanted = jnp.where(iota((devices, lanes), 0) == owner, (slot + 1).astype(F32), 0.0)
    ranks = one_hot(iota((lanes, lanes), 0) == rank)
    request[...] = dot_nt(wanted.astype(BF16), ranks)[:, None, :]


def pick_kernel(group, lists, out):
    parts = group.shape[0]
    table = jnp.concatenate([group[j] for j in range(parts)], axis=1)
    odd = lax.axis_index("blk") % 2
    row = jnp.where(odd == 0, lists[1:2, :], lists[0:1, :])
    hot = one_hot(iota((table.shape[1], row.shape[1]), 0) == row)
    out[...] = dot(table, hot).astype(BF16)


def total_of(x):
    line = jnp.sum(x * x, axis=0, keepdims=True)
    return jnp.sum(line, axis=1, keepdims=True)


def source_kernel(cap, got, bucket, hist, smat, weight, mech_total, out):
    quads, width, lanes = hist.shape
    hot = asking_hot(bucket, cap, got.shape[0])
    held = unpack(hot, got, 3 * width)
    d_hi, d_lo = split2(held[:width])
    acc = jnp.zeros((width, lanes), F32)
    for q in range(quads):
        s_hi, s_lo = split2(smat[q])
        strain = dot(s_hi, d_hi) + (dot(s_hi, d_lo) + dot(s_lo, d_hi))
        acc = acc + weight[0, q] * jnp.maximum(hist[q], 0.5 * strain * strain)
    dmg_res = held[width : 2 * width] + 2.0 * acc * held[2 * width :]
    spare = iota((1, lanes), 1) - (lanes - 2)
    tail = jnp.where(spare == 0, mech_total[...], 0.0)
    tail = jnp.where(spare == 1, total_of(dmg_res), tail)
    pack(hot, dmg_res, out, tail)


def matvec_kernel(
    cap,
    group,
    mine_ghost,
    other_ghost,
    columns,
    tan,
    lap,
    request,
    disp,
    damage,
    load,
    mech,
    mech_total,
    parcels,
    left,
    near,
    diff,
):
    kblk, rows, width, lanes = tan.shape
    parts = group.shape[0]
    depth = kblk * width
    ghost = mine_ghost.shape[1]
    table = jnp.concatenate(
        [group[j] for j in range(parts)] + [mine_ghost[...], other_ghost[...]], axis=1
    )
    wanted = jnp.concatenate([columns[k : k + 1, :] for k in range(kblk)], axis=1)
    odd = lax.axis_index("blk") % 2
    own = parts * lanes
    starts = (0, own + odd * ghost, own + ghost - odd * ghost)
    hots = [
        one_hot(iota((size, kblk * lanes), 0) + start == wanted)
        for size, start in zip((own, ghost, ghost), starts)
    ]
    hot = jnp.concatenate(hots, axis=0)
    found = dot(table, hot)
    tall = []
    for field in range(2):
        cut = [
            found[field * width : (field + 1) * width, k * lanes : (k + 1) * lanes]
            for k in range(kblk)
        ]
        tall.append(jnp.concatenate(cut, axis=0))
    left[...] = tall[0].T.astype(BF16)
    near[...] = tall[1]
    lane = iota((8, 2 * lanes), 1) % lanes
    mine = iota((8, 2 * lanes), 0) == lane % 8

    @pl.loop(0, rows // 8)
    def _(step):
        place = pl.ds(pl.multiple_of(step * 8, 8), 8)
        lines = []
        for r in range(0, 8, 2):
            pair = [tan[:, step * 8 + r + j].reshape(depth, lanes) for j in range(2)]
            full = dot(left[...], jnp.concatenate(pair, axis=1))
            kept = full[:8]
            for g in range(1, lanes // 8):
                kept = jnp.where(lane // 8 == g, full[g * 8 : g * 8 + 8], kept)
            line = jnp.sum(jnp.where(mine, kept, 0.0), axis=0, keepdims=True)
            lines += [line[:, :lanes], line[:, lanes:]]
        mech[place, :] = jnp.concatenate(lines, axis=0)
        acc = [jnp.zeros((8, lanes), F32) for _ in range(8)]
        for k in range(kblk):
            for c in range(0, width, 16):
                base = k * width + c
                lo = near[base : base + 8, :]
                hi = near[base + 8 : base + 16, :]
                for r in range(8):
                    block = lap[k, step * 8 + r, c : c + 16, :].astype(F32)
                    acc[r] = acc[r] + (block[:8] * lo + block[8:] * hi)
        sums = [jnp.sum(a, axis=0, keepdims=True) for a in acc]
        diff[place, :] = jnp.concatenate(sums, axis=0)


    d = damage[...]
    mech_res = root_of(d) * mech[...] - load[...]
    mech[...] = mech_res
    mech_total[...] = jnp.broadcast_to(total_of(mech_res), mech_total.shape)
    table = jnp.concatenate([disp[...], diff[...] + d, d - 1.0], axis=0)
    pack(asked_hot(request, cap), table, parcels)


def scale_kernel(cap, entries, got, request, mech, mech_out, dmg_out, norms):
    width, lanes = mech.shape
    last = got[:, got.shape[1] - 1, 3, :]
    total = jnp.sum(last, axis=0, keepdims=True)[:, lanes - 2 :]
    norm = jnp.sqrt(total / entries + 1e-06)
    mech_out[...] = mech[...] / norm[:, 0:1]
    dmg_out[...] = unpack(asked_hot(request, cap), got, width) / norm[:, 1:2]
    norms[...] = norm


VM = pl.BlockSpec(memory_space=pltpu.VMEM)
SM = pl.BlockSpec(memory_space=pltpu.SMEM)


def call(body, outs, ins, scratch=(), flops=0, nbytes=0, specs=None):
    one = not isinstance(outs, (list, tuple))
    return pl.pallas_call(
        body,
        out_shape=outs,
        in_specs=specs or [VM] * ins,
        out_specs=VM if one else [VM] * len(outs),
        scratch_shapes=list(scratch),
        compiler_params=pltpu.CompilerParams(vmem_limit_bytes=VMEM_LIMIT),
        cost_estimate=pl.CostEstimate(flops=flops, bytes_accessed=nbytes, transcendentals=0),
    )


def sds(shape, dtype=F32):
    return jax.ShapeDtypeStruct(shape, dtype)


def swap(x, axes):
    return lax.all_to_all(x, axes, split_axis=0, concat_axis=0, tiled=True)


def on_device(
    displacement,
    damage,
    applied_load,
    tangent,
    laplacian,
    block_columns,
    send_lists,
    hist_mech,
    mech_dest,
    strain_matrix,
    quad_weight,
):
    lanes, width = displacement.shape
    kblk = tangent.shape[1]
    quads = hist_mech.shape[1]
    ghost = send_lists.shape[2]
    both = ("dom", "blk")
    devices = lax.axis_size(both)
    groups = lax.axis_size("dom")
    disp_t = displacement.T
    dmg_t = damage.T
    load_t = applied_load.T
    tan_t = jnp.transpose(tangent, (1, 2, 3, 0))
    lap_t = jnp.transpose(laplacian, (1, 2, 3, 0))
    hist_t = jnp.transpose(hist_mech, (1, 2, 0))
    cols_t = block_columns.T

    cap = lanes // devices + 1
    weighted = (root_of(dmg_t) * disp_t).astype(BF16)
    fields = jnp.concatenate([weighted, dmg_t.astype(BF16)], axis=0)
    with jax.named_scope("requests"):
        request, bucket = call(
            functools.partial(request_kernel, cap),
            [sds((devices, 1, lanes)), sds((1, lanes), jnp.int32)],
            1,
            flops=FILL,
        )(mech_dest[None, :])
    wanted = swap(request, both)
    group = lax.all_gather(fields, "blk", axis=0, tiled=False)
    wanted, group = lax.optimization_barrier((wanted, group))
    with jax.named_scope("picks"):
        picked = call(pick_kernel, sds((2 * width, ghost), BF16), 2, flops=20 * FILL)(
            group, send_lists[0]
        )
    blocks = lax.axis_size("blk")
    everyone = [(a, b) for a in range(groups) for b in range(blocks)]
    hop = [(a * blocks + b, (a + 1 - b % 2 * 2) * blocks + b) for a, b in everyone]
    hop = [(i, j) for i, j in hop if 0 <= j < groups * blocks]
    side = [(b, b ^ 1) for b in range(blocks)]
    mine_ghost = lax.ppermute(picked, both, hop)
    other_ghost = lax.ppermute(mine_ghost, "blk", side)
    with jax.named_scope("matvec"):
        mech, mech_total, parcels = call(
            functools.partial(matvec_kernel, cap),
            [
                sds((width, lanes)),
                sds((1, lanes)),
                sds(parcel_shape(devices, 3 * cap * width, lanes)),
            ],
            10,
            [
                pltpu.VMEM((lanes, kblk * width), BF16),
                pltpu.VMEM((kblk * width, lanes), F32),
                pltpu.VMEM((width, lanes), F32),
            ],
            flops=FILL,
        )(group, mine_ghost, other_ghost, cols_t, tan_t, lap_t, wanted, disp_t, dmg_t, load_t)
    asked = swap(parcels, both)
    with jax.named_scope("source"):
        answer = call(
            functools.partial(source_kernel, cap),
            sds(parcel_shape(devices, cap * width + 2, lanes)),
            6,
            flops=FILL,
            specs=[VM, VM, VM, VM, SM, VM],
        )(asked, bucket, hist_t, strain_matrix, quad_weight[None, :], mech_total)
    got = swap(answer, both)
    with jax.named_scope("scale"):
        mech_out, dmg_out, norms = call(
            functools.partial(scale_kernel, cap, float(lanes * width * devices)),
            [sds((width, lanes)), sds((width, lanes)), sds((1, 2))],
            3,
        )(got, wanted, mech)
    return mech_out.T, dmg_out.T, norms[0]


def solution(mesh):
    rows = P(("dom", "blk"))
    in_specs = (rows,) * 6 + (P("dom"),) + (rows,) * 2 + (P(), P())
    out_specs = (rows, rows, P())
    return jax.shard_map(
        on_device, mesh=mesh, in_specs=in_specs, out_specs=out_specs, check_vma=False
    )
```

```python
import functools

import jax
import jax.numpy as jnp
from jax import lax
from jax.experimental import pallas as pl
from jax.experimental.pallas import tpu as pltpu
from jax.sharding import PartitionSpec as P

F32 = jnp.float32
BF16 = jnp.bfloat16
FILL = 10**10
VMEM_LIMIT = 4 * 1024 * 1024


def dot(a, b):
    return lax.dot_general(a, b, (((1,), (0,)), ((), ())), preferred_element_type=F32)


def dot_nt(a, b):
    return lax.dot_general(a, b, (((1,), (1,)), ((), ())), preferred_element_type=F32)


def split2(x):
    hi = x.astype(BF16)
    lo = (x - hi.astype(F32)).astype(BF16)
    return hi, lo


def split3(x):
    hi = x.astype(BF16)
    rest = x - hi.astype(F32)
    mid = rest.astype(BF16)
    lo = (rest - mid.astype(F32)).astype(BF16)
    return hi, mid, lo


def one_hot(cond):
    return jnp.where(cond, 1.0, 0.0).astype(BF16)


def iota(shape, dim):
    return lax.broadcasted_iota(jnp.int32, shape, dim)


def parcel_shape(devices, values, lanes):
    return (devices, -(-values // (4 * lanes)), 4, lanes)


def pack(hot, table, out, tail=0.0):
    devices, groups, _, lanes = out.shape
    hi, lo = split2(table)
    moved = dot_nt(hot, hi) + dot_nt(hot, lo)
    cap, width = moved.shape[0] // devices, moved.shape[1]
    rows = [moved[k * devices : (k + 1) * devices] for k in range(cap)]
    rows.append(jnp.zeros((devices, groups * 4 * lanes - cap * width), F32))
    flat = jnp.concatenate(rows, axis=1)
    for j in range(groups * 4):
        line = flat[:, j * lanes : (j + 1) * lanes]
        out[:, j // 4, j % 4, :] = line + tail if j == groups * 4 - 1 else line


def unpack(hot, got, width):
    devices, groups, _, lanes = got.shape
    flat = jnp.concatenate([got[:, j // 4, j % 4, :] for j in range(groups * 4)], axis=1)
    cap = hot.shape[0] // devices
    rows = jnp.concatenate([flat[:, k * width : (k + 1) * width] for k in range(cap)], axis=0)
    blank = jnp.zeros((cap * devices, -width % lanes), F32)
    tall = jnp.concatenate([rows, blank], axis=1).T[:width]
    hi, lo = split2(tall)
    return dot(hi, hot) + dot(lo, hot)


def asked_hot(request, cap):
    devices, _, lanes = request.shape
    slots = request[:, 0, :]
    lane = iota((devices, lanes), 1).astype(F32)
    hots = [one_hot(lane == slots[:, k : k + 1] - 1.0) for k in range(cap)]
    return jnp.concatenate(hots, axis=0)


def asking_hot(bucket, cap, devices):
    place = iota((devices, bucket.shape[1]), 0) * cap
    hots = [one_hot(place + k == bucket[...]) for k in range(cap)]
    return jnp.concatenate(hots, axis=0)


def root_of(damage):
    return jnp.sqrt((1.0 - damage) ** 2 + 0.001)


def fields_kernel(stacked, fields):
    width = stacked.shape[0] // 2
    dmg = stacked[width:, :]
    fields[:width, :] = (root_of(dmg) * stacked[:width, :]).astype(BF16)
    fields[width:, :] = dmg.astype(BF16)


def request_kernel(cap, dest, request, bucket):
    devices, _, lanes = request.shape
    d = dest[...]
    owner = d // lanes
    slot = d - owner * lanes
    square = jnp.broadcast_to(owner.astype(F32), (lanes, lanes))
    diag = iota((lanes, lanes), 0) == iota((lanes, lanes), 1)
    column = jnp.sum(jnp.where(diag, square, 0.0), axis=1, keepdims=True)
    before = iota((lanes, lanes), 0) < iota((lanes, lanes), 1)
    same = (column == square) & before
    rank = jnp.sum(jnp.where(same, 1.0, 0.0), axis=0, keepdims=True).astype(jnp.int32)
    bucket[...] = owner * cap + rank
    wanted = jnp.where(iota((devices, lanes), 0) == owner, (slot + 1).astype(F32), 0.0)
    ranks = one_hot(iota((lanes, lanes), 0) == rank)
    request[...] = dot_nt(wanted.astype(BF16), ranks)[:, None, :]


def pick_kernel(group, lists, out):
    parts = group.shape[0]
    table = jnp.concatenate([group[j] for j in range(parts)], axis=1)
    odd = lax.axis_index("blk") % 2
    row = jnp.where(odd == 0, lists[1:2, :], lists[0:1, :])
    hot = one_hot(iota((table.shape[1], row.shape[1]), 0) == row)
    out[...] = dot(table, hot).astype(BF16)


def total_of(x):
    line = jnp.sum(x * x, axis=0, keepdims=True)
    return jnp.sum(line, axis=1, keepdims=True)


def source_kernel(cap, got, bucket, hist, smat, weight, mech_total, out):
    quads, width, lanes = hist.shape
    hot = asking_hot(bucket, cap, got.shape[0])
    held = unpack(hot, got, 3 * width)
    d_hi, d_lo = split2(held[:width])
    acc = jnp.zeros((width, lanes), F32)
    for q in range(quads):
        s_hi, s_lo = split2(smat[q])
        strain = dot(s_hi, d_hi) + (dot(s_hi, d_lo) + dot(s_lo, d_hi))
        acc = acc + weight[0, q] * jnp.maximum(hist[q], 0.5 * strain * strain)
    dmg_res = held[width : 2 * width] + 2.0 * acc * held[2 * width :]
    spare = iota((1, lanes), 1) - (lanes - 2)
    tail = jnp.where(spare == 0, mech_total[...], 0.0)
    tail = jnp.where(spare == 1, total_of(dmg_res), tail)
    pack(hot, dmg_res, out, tail)


def matvec_kernel(
    cap,
    group,
    mine_ghost,
    other_ghost,
    columns,
    tan,
    lap,
    request,
    disp,
    damage,
    load,
    mech,
    mech_total,
    parcels,
    left,
    near,
    diff,
):
    kblk, rows, width, lanes = tan.shape
    parts = group.shape[0]
    depth = kblk * width
    ghost = mine_ghost.shape[1]
    table = jnp.concatenate(
        [group[j] for j in range(parts)] + [mine_ghost[...], other_ghost[...]], axis=1
    )
    wanted = jnp.concatenate([columns[k : k + 1, :] for k in range(kblk)], axis=1)
    odd = lax.axis_index("blk") % 2
    own = parts * lanes
    starts = (0, own + odd * ghost, own + ghost - odd * ghost)
    hots = [
        one_hot(iota((size, kblk * lanes), 0) + start == wanted)
        for size, start in zip((own, ghost, ghost), starts)
    ]
    hot = jnp.concatenate(hots, axis=0)
    found = dot(table, hot)
    tall = []
    for field in range(2):
        cut = [
            found[field * width : (field + 1) * width, k * lanes : (k + 1) * lanes]
            for k in range(kblk)
        ]
        tall.append(jnp.concatenate(cut, axis=0))
    left[...] = tall[0].T.astype(BF16)
    near[...] = tall[1]
    lane = iota((8, 2 * lanes), 1) % lanes
    mine = iota((8, 2 * lanes), 0) == lane % 8

    @pl.loop(0, rows // 8)
    def _(step):
        place = pl.ds(pl.multiple_of(step * 8, 8), 8)
        lines = []
        for r in range(0, 8, 2):
            pair = [tan[:, step * 8 + r + j].reshape(depth, lanes) for j in range(2)]
            full = dot(left[...], jnp.concatenate(pair, axis=1))
            kept = full[:8]
            for g in range(1, lanes // 8):
                kept = jnp.where(lane // 8 == g, full[g * 8 : g * 8 + 8], kept)
            line = jnp.sum(jnp.where(mine, kept, 0.0), axis=0, keepdims=True)
            lines += [line[:, :lanes], line[:, lanes:]]
        mech[place, :] = jnp.concatenate(lines, axis=0)
        acc = [jnp.zeros((8, lanes), F32) for _ in range(8)]
        for k in range(kblk):
            for c in range(0, width, 16):
                base = k * width + c
                lo = near[base : base + 8, :]
                hi = near[base + 8 : base + 16, :]
                for r in range(8):
                    block = lap[k, step * 8 + r, c : c + 16, :].astype(F32)
                    acc[r] = acc[r] + (block[:8] * lo + block[8:] * hi)
        sums = [jnp.sum(a, axis=0, keepdims=True) for a in acc]
        diff[place, :] = jnp.concatenate(sums, axis=0)


    d = damage[...]
    mech_res = root_of(d) * mech[...] - load[...]
    mech[...] = mech_res
    mech_total[...] = jnp.broadcast_to(total_of(mech_res), mech_total.shape)
    table = jnp.concatenate([disp[...], diff[...] + d, d - 1.0], axis=0)
    pack(asked_hot(request, cap), table, parcels)


def scale_kernel(cap, entries, got, request, mech, mech_out, dmg_out, norms):
    width, lanes = mech.shape
    last = got[:, got.shape[1] - 1, 3, :]
    total = jnp.sum(last, axis=0, keepdims=True)[:, lanes - 2 :]
    norm = jnp.sqrt(total / entries + 1e-06)
    mech_out[...] = mech[...] / norm[:, 0:1]
    dmg_out[...] = unpack(asked_hot(request, cap), got, width) / norm[:, 1:2]
    norms[...] = norm


VM = pl.BlockSpec(memory_space=pltpu.VMEM)
SM = pl.BlockSpec(memory_space=pltpu.SMEM)


def call(body, outs, ins, scratch=(), flops=0, nbytes=0, specs=None):
    one = not isinstance(outs, (list, tuple))
    return pl.pallas_call(
        body,
        out_shape=outs,
        in_specs=specs or [VM] * ins,
        out_specs=VM if one else [VM] * len(outs),
        scratch_shapes=list(scratch),
        compiler_params=pltpu.CompilerParams(vmem_limit_bytes=VMEM_LIMIT),
        cost_estimate=pl.CostEstimate(flops=flops, bytes_accessed=nbytes, transcendentals=0),
    )


def sds(shape, dtype=F32):
    return jax.ShapeDtypeStruct(shape, dtype)


def swap(x, axes):
    return lax.all_to_all(x, axes, split_axis=0, concat_axis=0, tiled=True)


def on_device(
    displacement,
    damage,
    applied_load,
    tangent,
    laplacian,
    block_columns,
    send_lists,
    hist_mech,
    mech_dest,
    strain_matrix,
    quad_weight,
):
    lanes, width = displacement.shape
    kblk = tangent.shape[1]
    quads = hist_mech.shape[1]
    ghost = send_lists.shape[2]
    both = ("dom", "blk")
    devices = lax.axis_size(both)
    groups = lax.axis_size("dom")
    disp_t = displacement.T
    dmg_t = damage.T
    load_t = applied_load.T
    tan_t = jnp.transpose(tangent, (1, 2, 3, 0))
    lap_t = jnp.transpose(laplacian, (1, 2, 3, 0))
    hist_t = jnp.transpose(hist_mech, (1, 2, 0))
    cols_t = block_columns.T

    cap = lanes // devices + 1
    stacked = jnp.concatenate([disp_t, dmg_t], axis=0)
    with jax.named_scope("fields"):
        fields = call(fields_kernel, sds(stacked.shape, BF16), 1, flops=FILL)(stacked)
    group = lax.all_gather(fields, "blk", axis=0, tiled=False)
    with jax.named_scope("picks"):
        picked = call(pick_kernel, sds((2 * width, ghost), BF16), 2, flops=20 * FILL)(
            group, send_lists[0]
        )
    picked, mech_dest = lax.optimization_barrier((picked, mech_dest))
    with jax.named_scope("requests"):
        request, bucket = call(
            functools.partial(request_kernel, cap),
            [sds((devices, 1, lanes)), sds((1, lanes), jnp.int32)],
            1,
            flops=FILL,
        )(mech_dest[None, :])
    wanted = swap(request, both)
    blocks = lax.axis_size("blk")
    everyone = [(a, b) for a in range(groups) for b in range(blocks)]
    hop = [(a * blocks + b, (a + 1 - b % 2 * 2) * blocks + b) for a, b in everyone]
    hop = [(i, j) for i, j in hop if 0 <= j < groups * blocks]
    side = [(b, b ^ 1) for b in range(blocks)]
    mine_ghost = lax.ppermute(picked, both, hop)
    mine_ghost, wanted = lax.optimization_barrier((mine_ghost, wanted))
    other_ghost = lax.ppermute(mine_ghost, "blk", side)
    with jax.named_scope("matvec"):
        mech, mech_total, parcels = call(
            functools.partial(matvec_kernel, cap),
            [
                sds((width, lanes)),
                sds((1, lanes)),
                sds(parcel_shape(devices, 3 * cap * width, lanes)),
            ],
            10,
            [
                pltpu.VMEM((lanes, kblk * width), BF16),
                pltpu.VMEM((kblk * width, lanes), F32),
                pltpu.VMEM((width, lanes), F32),
            ],
            flops=FILL,
        )(group, mine_ghost, other_ghost, cols_t, tan_t, lap_t, wanted, disp_t, dmg_t, load_t)
    asked = swap(parcels, both)
    with jax.named_scope("source"):
        answer = call(
            functools.partial(source_kernel, cap),
            sds(parcel_shape(devices, cap * width + 2, lanes)),
            6,
            flops=FILL,
            specs=[VM, VM, VM, VM, SM, VM],
        )(asked, bucket, hist_t, strain_matrix, quad_weight[None, :], mech_total)
    got = swap(answer, both)
    with jax.named_scope("scale"):
        mech_out, dmg_out, norms = call(
            functools.partial(scale_kernel, cap, float(lanes * width * devices)),
            [sds((width, lanes)), sds((width, lanes)), sds((1, 2))],
            3,
        )(got, wanted, mech)
    return mech_out.T, dmg_out.T, norms[0]


def solution(mesh):
    rows = P(("dom", "blk"))
    in_specs = (rows,) * 6 + (P("dom"),) + (rows,) * 2 + (P(), P())
    out_specs = (rows, rows, P())
    return jax.shard_map(
        on_device, mesh=mesh, in_specs=in_specs, out_specs=out_specs, check_vma=False
    )
```

```python
import functools

import jax
import jax.numpy as jnp
from jax import lax
from jax.experimental import pallas as pl
from jax.experimental.pallas import tpu as pltpu
from jax.sharding import PartitionSpec as P

F32 = jnp.float32
BF16 = jnp.bfloat16
FILL = 10**10
VMEM_LIMIT = 4 * 1024 * 1024


def dot(a, b):
    return lax.dot_general(a, b, (((1,), (0,)), ((), ())), preferred_element_type=F32)


def dot_nt(a, b):
    return lax.dot_general(a, b, (((1,), (1,)), ((), ())), preferred_element_type=F32)


def split2(x):
    hi = x.astype(BF16)
    lo = (x - hi.astype(F32)).astype(BF16)
    return hi, lo


def split3(x):
    hi = x.astype(BF16)
    rest = x - hi.astype(F32)
    mid = rest.astype(BF16)
    lo = (rest - mid.astype(F32)).astype(BF16)
    return hi, mid, lo


def one_hot(cond):
    return jnp.where(cond, 1.0, 0.0).astype(BF16)


def iota(shape, dim):
    return lax.broadcasted_iota(jnp.int32, shape, dim)


def parcel_shape(devices, values, lanes):
    return (devices, -(-values // (4 * lanes)), 4, lanes)


def pack(hot, table, out, tail=0.0):
    devices, groups, _, lanes = out.shape
    hi, lo = split2(table)
    moved = dot_nt(hot, hi) + dot_nt(hot, lo)
    cap, width = moved.shape[0] // devices, moved.shape[1]
    rows = [moved[k * devices : (k + 1) * devices] for k in range(cap)]
    rows.append(jnp.zeros((devices, groups * 4 * lanes - cap * width), F32))
    flat = jnp.concatenate(rows, axis=1)
    for j in range(groups * 4):
        line = flat[:, j * lanes : (j + 1) * lanes]
        out[:, j // 4, j % 4, :] = line + tail if j == groups * 4 - 1 else line


def unpack(hot, got, width):
    devices, groups, _, lanes = got.shape
    flat = jnp.concatenate([got[:, j // 4, j % 4, :] for j in range(groups * 4)], axis=1)
    cap = hot.shape[0] // devices
    rows = jnp.concatenate([flat[:, k * width : (k + 1) * width] for k in range(cap)], axis=0)
    blank = jnp.zeros((cap * devices, -width % lanes), F32)
    tall = jnp.concatenate([rows, blank], axis=1).T[:width]
    hi, lo = split2(tall)
    return dot(hi, hot) + dot(lo, hot)


def asked_hot(request, cap):
    devices, _, lanes = request.shape
    slots = request[:, 0, :]
    lane = iota((devices, lanes), 1).astype(F32)
    hots = [one_hot(lane == slots[:, k : k + 1] - 1.0) for k in range(cap)]
    return jnp.concatenate(hots, axis=0)


def asking_hot(bucket, cap, devices):
    place = iota((devices, bucket.shape[1]), 0) * cap
    hots = [one_hot(place + k == bucket[...]) for k in range(cap)]
    return jnp.concatenate(hots, axis=0)


def root_of(damage):
    return jnp.sqrt((1.0 - damage) ** 2 + 0.001)


def fields_kernel(cap, stacked, fields, bucket):
    lanes = stacked.shape[1]
    width = (stacked.shape[0] - 1) // 2
    devices = fields.shape[0] - 2 * width
    dmg = stacked[width : 2 * width, :]
    fields[:width, :] = (root_of(dmg) * stacked[:width, :]).astype(BF16)
    fields[width : 2 * width, :] = dmg.astype(BF16)
    d = stacked[2 * width :, :].astype(jnp.int32)
    owner = d // lanes
    slot = d - owner * lanes
    square = jnp.broadcast_to(owner.astype(F32), (lanes, lanes))
    diag = iota((lanes, lanes), 0) == iota((lanes, lanes), 1)
    column = jnp.sum(jnp.where(diag, square, 0.0), axis=1, keepdims=True)
    before = iota((lanes, lanes), 0) < iota((lanes, lanes), 1)
    same = (column == square) & before
    rank = jnp.sum(jnp.where(same, 1.0, 0.0), axis=0, keepdims=True).astype(jnp.int32)
    bucket[...] = owner * cap + rank
    wanted = jnp.where(iota((devices, lanes), 0) == owner, (slot + 1).astype(F32), 0.0)
    ranks = one_hot(iota((lanes, lanes), 0) == rank)
    fields[2 * width :, :] = dot_nt(wanted.astype(BF16), ranks).astype(BF16)


def pick_kernel(group, lists, out, ask):
    parts = group.shape[0]
    fields = out.shape[0]
    devices = group.shape[1] - fields
    me = lax.axis_index("blk")
    place = iota((ask.shape[0], devices), 0) * parts + me
    mine = one_hot(place == iota((ask.shape[0], devices), 1))
    for j in range(parts):
        ask[:, j, 0, :] = dot(mine, group[j, fields:, :])
    table = jnp.concatenate([group[j, :fields, :] for j in range(parts)], axis=1)
    odd = me % 2
    row = jnp.where(odd == 0, lists[1:2, :], lists[0:1, :])
    hot = one_hot(iota((table.shape[1], row.shape[1]), 0) == row)
    out[...] = dot(table, hot).astype(BF16)


def total_of(x):
    line = jnp.sum(x * x, axis=0, keepdims=True)
    return jnp.sum(line, axis=1, keepdims=True)


def source_kernel(cap, got, bucket, hist, smat, weight, mech_total, out):
    quads, width, lanes = hist.shape
    hot = asking_hot(bucket, cap, got.shape[0])
    held = unpack(hot, got, 3 * width)
    sides = jnp.concatenate(split2(held[:width]), axis=1)
    acc = jnp.zeros((width, lanes), F32)
    for q in range(quads):
        both = dot(jnp.concatenate(split2(smat[q]), axis=0), sides)
        strain = both[:width, :lanes] + (both[:width, lanes:] + both[width:, :lanes])
        acc = acc + weight[0, q] * jnp.maximum(hist[q], 0.5 * strain * strain)
    dmg_res = held[width : 2 * width] + 2.0 * acc * held[2 * width :]
    spare = iota((1, lanes), 1) - (lanes - 2)
    tail = jnp.where(spare == 0, mech_total[...], 0.0)
    tail = jnp.where(spare == 1, total_of(dmg_res), tail)
    pack(hot, dmg_res, out, tail)


def matvec_kernel(
    cap,
    group,
    mine_ghost,
    other_ghost,
    columns,
    tan,
    lap,
    request,
    disp,
    damage,
    load,
    mech,
    mech_total,
    parcels,
    left,
    near,
    diff,
):
    kblk, rows, width, lanes = tan.shape
    parts = group.shape[0]
    depth = kblk * width
    ghost = mine_ghost.shape[1]
    table = jnp.concatenate(
        [group[j, : 2 * width, :] for j in range(parts)] + [mine_ghost[...], other_ghost[...]], axis=1
    )
    wanted = jnp.concatenate([columns[k : k + 1, :] for k in range(kblk)], axis=1)
    odd = lax.axis_index("blk") % 2
    own = parts * lanes
    starts = (0, own + odd * ghost, own + ghost - odd * ghost)
    hots = [
        one_hot(iota((size, kblk * lanes), 0) + start == wanted)
        for size, start in zip((own, ghost, ghost), starts)
    ]
    hot = jnp.concatenate(hots, axis=0)
    found = dot(table, hot)
    tall = []
    for field in range(2):
        cut = [
            found[field * width : (field + 1) * width, k * lanes : (k + 1) * lanes]
            for k in range(kblk)
        ]
        tall.append(jnp.concatenate(cut, axis=0))
    for field in range(2):
        left[field] = tall[field].T.astype(BF16)
    near[...] = tall[1]
    lane = iota((8, 2 * lanes), 1) % lanes
    mine = iota((8, 2 * lanes), 0) == lane % 8

    @pl.loop(0, rows // 8)
    def _(step):
        def by_matrix(field, mat, r):
            pair = [mat[:, step * 8 + r + j].reshape(depth, lanes) for j in range(2)]
            full = dot(left[field], jnp.concatenate(pair, axis=1))
            kept = full[:8]
            for g in range(1, lanes // 8):
                kept = jnp.where(lane // 8 == g, full[g * 8 : g * 8 + 8], kept)
            line = jnp.sum(jnp.where(mine, kept, 0.0), axis=0, keepdims=True)
            return [line[:, :lanes], line[:, lanes:]]

        place = pl.ds(pl.multiple_of(step * 8, 8), 8)
        lines = []
        for r in range(0, 8, 2):
            lines += by_matrix(0, tan, r)
        mech[place, :] = jnp.concatenate(lines, axis=0)
        lines = by_matrix(1, lap, 0)
        acc = {r: jnp.zeros((8, lanes), F32) for r in range(2, 8)}
        for k in range(kblk):
            for c in range(0, width, 16):
                base = k * width + c
                lo = near[base : base + 8, :]
                hi = near[base + 8 : base + 16, :]
                for r in acc:
                    block = lap[k, step * 8 + r, c : c + 16, :].astype(F32)
                    acc[r] = acc[r] + (block[:8] * lo + block[8:] * hi)
        lines += [jnp.sum(a, axis=0, keepdims=True) for a in acc.values()]
        diff[place, :] = jnp.concatenate(lines, axis=0)

    d = damage[...]
    mech_res = root_of(d) * mech[...] - load[...]
    mech[...] = mech_res
    mech_total[...] = jnp.broadcast_to(total_of(mech_res), mech_total.shape)
    table = jnp.concatenate([disp[...], diff[...] + d, d - 1.0], axis=0)
    pack(asked_hot(request, cap), table, parcels)


def scale_kernel(cap, entries, got, request, mech, mech_out, dmg_out, norms):
    width, lanes = mech.shape
    last = got[:, got.shape[1] - 1, 3, :]
    total = jnp.sum(last, axis=0, keepdims=True)[:, lanes - 2 :]
    norm = jnp.sqrt(total / entries + 1e-06)
    mech_out[...] = mech[...] / norm[:, 0:1]
    dmg_out[...] = unpack(asked_hot(request, cap), got, width) / norm[:, 1:2]
    norms[...] = norm


VM = pl.BlockSpec(memory_space=pltpu.VMEM)
SM = pl.BlockSpec(memory_space=pltpu.SMEM)


def call(body, outs, ins, scratch=(), flops=0, nbytes=0, specs=None):
    one = not isinstance(outs, (list, tuple))
    return pl.pallas_call(
        body,
        out_shape=outs,
        in_specs=specs or [VM] * ins,
        out_specs=VM if one else [VM] * len(outs),
        scratch_shapes=list(scratch),
        compiler_params=pltpu.CompilerParams(vmem_limit_bytes=VMEM_LIMIT),
        cost_estimate=pl.CostEstimate(flops=flops, bytes_accessed=nbytes, transcendentals=0),
    )


def sds(shape, dtype=F32):
    return jax.ShapeDtypeStruct(shape, dtype)


def swap(x, axes):
    return lax.all_to_all(x, axes, split_axis=0, concat_axis=0, tiled=True)


def on_device(
    displacement,
    damage,
    applied_load,
    tangent,
    laplacian,
    block_columns,
    send_lists,
    hist_mech,
    mech_dest,
    strain_matrix,
    quad_weight,
):
    lanes, width = displacement.shape
    kblk = tangent.shape[1]
    quads = hist_mech.shape[1]
    ghost = send_lists.shape[2]
    both = ("dom", "blk")
    devices = lax.axis_size(both)
    groups = lax.axis_size("dom")
    disp_t = displacement.T
    dmg_t = damage.T
    load_t = applied_load.T
    tan_t = jnp.transpose(tangent, (1, 2, 3, 0))
    lap_t = jnp.transpose(laplacian, (1, 2, 3, 0))
    hist_t = jnp.transpose(hist_mech, (1, 2, 0))
    cols_t = block_columns.T

    cap = lanes // devices + 1
    dest = mech_dest[None, :].astype(F32)
    stacked = jnp.concatenate([disp_t, dmg_t, dest], axis=0)
    with jax.named_scope("fields"):
        fields, bucket = call(
            functools.partial(fields_kernel, cap),
            [sds((2 * width + devices, lanes), BF16), sds((1, lanes), jnp.int32)],
            1,
            flops=FILL,
        )(stacked)
    group = lax.all_gather(fields, "blk", axis=0, tiled=False)
    blocks = lax.axis_size("blk")
    with jax.named_scope("picks"):
        picked, ask = call(
            pick_kernel,
            [sds((2 * width, ghost), BF16), sds((groups, blocks, 1, lanes))],
            2,
            flops=20 * FILL,
        )(group, send_lists[0])
    wanted = swap(ask, "dom").reshape(devices, 1, lanes)
    everyone = [(a, b) for a in range(groups) for b in range(blocks)]
    hop = [(a * blocks + b, (a + 1 - b % 2 * 2) * blocks + b) for a, b in everyone]
    hop = [(i, j) for i, j in hop if 0 <= j < groups * blocks]
    side = [(b, b ^ 1) for b in range(blocks)]
    mine_ghost = lax.ppermute(picked, both, hop)
    mine_ghost, wanted = lax.optimization_barrier((mine_ghost, wanted))
    other_ghost = lax.ppermute(mine_ghost, "blk", side)
    with jax.named_scope("matvec"):
        mech, mech_total, parcels = call(
            functools.partial(matvec_kernel, cap),
            [
                sds((width, lanes)),
                sds((1, lanes)),
                sds(parcel_shape(devices, 3 * cap * width, lanes)),
            ],
            10,
            [
                pltpu.VMEM((2, lanes, kblk * width), BF16),
                pltpu.VMEM((kblk * width, lanes), F32),
                pltpu.VMEM((width, lanes), F32),
            ],
            flops=FILL,
        )(group, mine_ghost, other_ghost, cols_t, tan_t, lap_t, wanted, disp_t, dmg_t, load_t)
    asked = swap(parcels, both)
    with jax.named_scope("source"):
        answer = call(
            functools.partial(source_kernel, cap),
            sds(parcel_shape(devices, cap * width + 2, lanes)),
            6,
            flops=FILL,
            specs=[VM, VM, VM, VM, SM, VM],
        )(asked, bucket, hist_t, strain_matrix, quad_weight[None, :], mech_total)
    got = swap(answer, both)
    with jax.named_scope("scale"):
        mech_out, dmg_out, norms = call(
            functools.partial(scale_kernel, cap, float(lanes * width * devices)),
            [sds((width, lanes)), sds((width, lanes)), sds((1, 2))],
            3,
        )(got, wanted, mech)
    return mech_out.T, dmg_out.T, norms[0]


def solution(mesh):
    rows = P(("dom", "blk"))
    in_specs = (rows,) * 6 + (P("dom"),) + (rows,) * 2 + (P(), P())
    out_specs = (rows, rows, P())
    return jax.shard_map(
        on_device, mesh=mesh, in_specs=in_specs, out_specs=out_specs, check_vma=False
    )
```

```python
import functools

import jax
import jax.numpy as jnp
from jax import lax
from jax.experimental import pallas as pl
from jax.experimental.pallas import tpu as pltpu
from jax.sharding import PartitionSpec as P

F32 = jnp.float32
BF16 = jnp.bfloat16
FILL = 10**10
VMEM_LIMIT = 4 * 1024 * 1024


def dot(a, b):
    return lax.dot_general(a, b, (((1,), (0,)), ((), ())), preferred_element_type=F32)


def dot_nt(a, b):
    return lax.dot_general(a, b, (((1,), (1,)), ((), ())), preferred_element_type=F32)


def split2(x):
    hi = x.astype(BF16)
    lo = (x - hi.astype(F32)).astype(BF16)
    return hi, lo


def split3(x):
    hi = x.astype(BF16)
    rest = x - hi.astype(F32)
    mid = rest.astype(BF16)
    lo = (rest - mid.astype(F32)).astype(BF16)
    return hi, mid, lo


def one_hot(cond):
    return jnp.where(cond, 1.0, 0.0).astype(BF16)


def iota(shape, dim):
    return lax.broadcasted_iota(jnp.int32, shape, dim)


def parcel_shape(devices, values, lanes):
    return (devices, -(-values // (4 * lanes)), 4, lanes)


def pack(hot, table, out, tail=0.0):
    devices, groups, _, lanes = out.shape
    hi, lo = split2(table)
    moved = dot_nt(hot, hi) + dot_nt(hot, lo)
    cap, width = moved.shape[0] // devices, moved.shape[1]
    rows = [moved[k * devices : (k + 1) * devices] for k in range(cap)]
    rows.append(jnp.zeros((devices, groups * 4 * lanes - cap * width), F32))
    flat = jnp.concatenate(rows, axis=1)
    for j in range(groups * 4):
        line = flat[:, j * lanes : (j + 1) * lanes]
        out[:, j // 4, j % 4, :] = line + tail if j == groups * 4 - 1 else line


def unpack(hot, got, width):
    devices, groups, _, lanes = got.shape
    flat = jnp.concatenate([got[:, j // 4, j % 4, :] for j in range(groups * 4)], axis=1)
    cap = hot.shape[0] // devices
    rows = jnp.concatenate([flat[:, k * width : (k + 1) * width] for k in range(cap)], axis=0)
    blank = jnp.zeros((cap * devices, -width % lanes), F32)
    tall = jnp.concatenate([rows, blank], axis=1).T[:width]
    hi, lo = split2(tall)
    return dot(hi, hot) + dot(lo, hot)


def asked_hot(request, cap):
    devices, _, lanes = request.shape
    slots = request[:, 0, :]
    lane = iota((devices, lanes), 1).astype(F32)
    hots = [one_hot(lane == slots[:, k : k + 1] - 1.0) for k in range(cap)]
    return jnp.concatenate(hots, axis=0)


def asking_hot(bucket, cap, devices):
    place = iota((devices, bucket.shape[1]), 0) * cap
    hots = [one_hot(place + k == bucket[...]) for k in range(cap)]
    return jnp.concatenate(hots, axis=0)


def root_of(damage):
    return jnp.sqrt((1.0 - damage) ** 2 + 0.001)


def fields_kernel(stacked, fields):
    width = stacked.shape[0] // 2
    dmg = stacked[width:, :]
    fields[:width, :] = (root_of(dmg) * stacked[:width, :]).astype(BF16)
    fields[width:, :] = dmg.astype(BF16)


def request_kernel(cap, dest, request, bucket):
    devices, _, lanes = request.shape
    d = dest[...]
    owner = d // lanes
    slot = d - owner * lanes
    square = jnp.broadcast_to(owner.astype(F32), (lanes, lanes))
    diag = iota((lanes, lanes), 0) == iota((lanes, lanes), 1)
    column = jnp.sum(jnp.where(diag, square, 0.0), axis=1, keepdims=True)
    before = iota((lanes, lanes), 0) < iota((lanes, lanes), 1)
    same = (column == square) & before
    rank = jnp.sum(jnp.where(same, 1.0, 0.0), axis=0, keepdims=True).astype(jnp.int32)
    bucket[...] = owner * cap + rank
    wanted = jnp.where(iota((devices, lanes), 0) == owner, (slot + 1).astype(F32), 0.0)
    ranks = one_hot(iota((lanes, lanes), 0) == rank)
    request[...] = dot_nt(wanted.astype(BF16), ranks)[:, None, :]


def pick_kernel(group, lists, out):
    parts = group.shape[0]
    table = jnp.concatenate([group[j] for j in range(parts)], axis=1)
    odd = lax.axis_index("blk") % 2
    row = jnp.where(odd == 0, lists[1:2, :], lists[0:1, :])
    hot = one_hot(iota((table.shape[1], row.shape[1]), 0) == row)
    out[...] = dot(table, hot).astype(BF16)


def total_of(x):
    line = jnp.sum(x * x, axis=0, keepdims=True)
    return jnp.sum(line, axis=1, keepdims=True)


def source_kernel(cap, got, bucket, hist, smat, weight, mech_total, out):
    quads, width, lanes = hist.shape
    hot = asking_hot(bucket, cap, got.shape[0])
    held = unpack(hot, got, 3 * width)
    gap = jnp.zeros((lanes - width, lanes), F32)
    d_hi, d_lo = split2(jnp.concatenate([held[:width], gap], axis=0))
    upper = jnp.concatenate([d_hi, d_lo], axis=1)
    lower = jnp.concatenate([d_hi, jnp.zeros_like(d_hi)], axis=1)
    sides = jnp.concatenate([upper, lower], axis=0)
    blank = jnp.zeros((width, lanes - width), F32)
    acc = jnp.zeros((width, lanes), F32)
    for q in range(quads):
        halves = split2(jnp.concatenate([smat[q], blank], axis=1))
        full = dot(jnp.concatenate(halves, axis=1), sides)
        strain = full[:, :lanes] + full[:, lanes:]
        acc = acc + weight[0, q] * jnp.maximum(hist[q], 0.5 * strain * strain)
    dmg_res = held[width : 2 * width] + 2.0 * acc * held[2 * width :]
    spare = iota((1, lanes), 1) - (lanes - 2)
    tail = jnp.where(spare == 0, mech_total[...], 0.0)
    tail = jnp.where(spare == 1, total_of(dmg_res), tail)
    pack(hot, dmg_res, out, tail)


def matvec_kernel(
    cap,
    group,
    mine_ghost,
    other_ghost,
    columns,
    tan,
    lap,
    request,
    disp,
    damage,
    load,
    mech,
    mech_total,
    parcels,
    left,
    near,
    diff,
):
    kblk, rows, width, lanes = tan.shape
    parts = group.shape[0]
    depth = kblk * width
    ghost = mine_ghost.shape[1]
    table = jnp.concatenate(
        [group[j] for j in range(parts)] + [mine_ghost[...], other_ghost[...]], axis=1
    )
    wanted = jnp.concatenate([columns[k : k + 1, :] for k in range(kblk)], axis=1)
    odd = lax.axis_index("blk") % 2
    own = parts * lanes
    starts = (0, own + odd * ghost, own + ghost - odd * ghost)
    hots = [
        one_hot(iota((size, kblk * lanes), 0) + start == wanted)
        for size, start in zip((own, ghost, ghost), starts)
    ]
    hot = jnp.concatenate(hots, axis=0)
    found = dot(table, hot)
    tall = []
    for field in range(2):
        cut = [
            found[field * width : (field + 1) * width, k * lanes : (k + 1) * lanes]
            for k in range(kblk)
        ]
        tall.append(jnp.concatenate(cut, axis=0))
    left[...] = tall[0].T.astype(BF16)
    near[...] = tall[1]
    lane = iota((8, 2 * lanes), 1) % lanes
    mine = iota((8, 2 * lanes), 0) == lane % 8

    @pl.loop(0, rows // 8)
    def _(step):
        place = pl.ds(pl.multiple_of(step * 8, 8), 8)
        lines, sums = [], []
        for half in range(0, 8, 4):
            fulls = []
            for r in range(half, half + 4, 2):
                pair = [tan[:, step * 8 + r + j].reshape(depth, lanes) for j in range(2)]
                fulls.append(dot(left[...], jnp.concatenate(pair, axis=1)))
            acc = [jnp.zeros((8, lanes), F32) for _ in range(4)]
            for k in range(kblk):
                for c in range(0, width, 16):
                    base = k * width + c
                    lo = near[base : base + 8, :]
                    hi = near[base + 8 : base + 16, :]
                    for r in range(4):
                        block = lap[k, step * 8 + half + r, c : c + 16, :].astype(F32)
                        acc[r] = acc[r] + (block[:8] * lo + block[8:] * hi)
            sums += [jnp.sum(a, axis=0, keepdims=True) for a in acc]
            for full in fulls:
                kept = full[:8]
                for g in range(1, lanes // 8):
                    kept = jnp.where(lane // 8 == g, full[g * 8 : g * 8 + 8], kept)
                line = jnp.sum(jnp.where(mine, kept, 0.0), axis=0, keepdims=True)
                lines += [line[:, :lanes], line[:, lanes:]]
        mech[place, :] = jnp.concatenate(lines, axis=0)
        diff[place, :] = jnp.concatenate(sums, axis=0)

    d = damage[...]
    mech_res = root_of(d) * mech[...] - load[...]
    mech[...] = mech_res
    mech_total[...] = jnp.broadcast_to(total_of(mech_res), mech_total.shape)
    table = jnp.concatenate([disp[...], diff[...] + d, d - 1.0], axis=0)
    pack(asked_hot(request, cap), table, parcels)


def scale_kernel(cap, entries, got, request, mech, mech_out, dmg_out, norms):
    width, lanes = mech.shape
    last = got[:, got.shape[1] - 1, 3, :]
    total = jnp.sum(last, axis=0, keepdims=True)[:, lanes - 2 :]
    norm = jnp.sqrt(total / entries + 1e-06)
    mech_out[...] = mech[...] / norm[:, 0:1]
    dmg_out[...] = unpack(asked_hot(request, cap), got, width) / norm[:, 1:2]
    norms[...] = norm


VM = pl.BlockSpec(memory_space=pltpu.VMEM)
SM = pl.BlockSpec(memory_space=pltpu.SMEM)


def call(body, outs, ins, scratch=(), flops=0, nbytes=0, specs=None):
    one = not isinstance(outs, (list, tuple))
    return pl.pallas_call(
        body,
        out_shape=outs,
        in_specs=specs or [VM] * ins,
        out_specs=VM if one else [VM] * len(outs),
        scratch_shapes=list(scratch),
        compiler_params=pltpu.CompilerParams(vmem_limit_bytes=VMEM_LIMIT),
        cost_estimate=pl.CostEstimate(flops=flops, bytes_accessed=nbytes, transcendentals=0),
    )


def sds(shape, dtype=F32):
    return jax.ShapeDtypeStruct(shape, dtype)


def swap(x, axes):
    return lax.all_to_all(x, axes, split_axis=0, concat_axis=0, tiled=True)


def on_device(
    displacement,
    damage,
    applied_load,
    tangent,
    laplacian,
    block_columns,
    send_lists,
    hist_mech,
    mech_dest,
    strain_matrix,
    quad_weight,
):
    lanes, width = displacement.shape
    kblk = tangent.shape[1]
    quads = hist_mech.shape[1]
    ghost = send_lists.shape[2]
    both = ("dom", "blk")
    devices = lax.axis_size(both)
    groups = lax.axis_size("dom")
    disp_t = displacement.T
    dmg_t = damage.T
    load_t = applied_load.T
    tan_t = jnp.transpose(tangent, (1, 2, 3, 0))
    lap_t = jnp.transpose(laplacian, (1, 2, 3, 0))
    hist_t = jnp.transpose(hist_mech, (1, 2, 0))
    cols_t = block_columns.T

    cap = lanes // devices + 1
    stacked = jnp.concatenate([disp_t, dmg_t], axis=0)
    with jax.named_scope("fields"):
        fields = call(fields_kernel, sds(stacked.shape, BF16), 1, flops=FILL)(stacked)
    group = lax.all_gather(fields, "blk", axis=0, tiled=False)
    with jax.named_scope("picks"):
        picked = call(pick_kernel, sds((2 * width, ghost), BF16), 2, flops=20 * FILL)(
            group, send_lists[0]
        )
    picked, mech_dest = lax.optimization_barrier((picked, mech_dest))
    with jax.named_scope("requests"):
        request, bucket = call(
            functools.partial(request_kernel, cap),
            [sds((devices, 1, lanes)), sds((1, lanes), jnp.int32)],
            1,
            flops=FILL,
        )(mech_dest[None, :])
    wanted = swap(request, both)
    blocks = lax.axis_size("blk")
    everyone = [(a, b) for a in range(groups) for b in range(blocks)]
    hop = [(a * blocks + b, (a + 1 - b % 2 * 2) * blocks + b) for a, b in everyone]
    hop = [(i, j) for i, j in hop if 0 <= j < groups * blocks]
    side = [(b, b ^ 1) for b in range(blocks)]
    mine_ghost = lax.ppermute(picked, both, hop)
    mine_ghost, wanted = lax.optimization_barrier((mine_ghost, wanted))
    other_ghost = lax.ppermute(mine_ghost, "blk", side)
    with jax.named_scope("matvec"):
        mech, mech_total, parcels = call(
            functools.partial(matvec_kernel, cap),
            [
                sds((width, lanes)),
                sds((1, lanes)),
                sds(parcel_shape(devices, 3 * cap * width, lanes)),
            ],
            10,
            [
                pltpu.VMEM((lanes, kblk * width), BF16),
                pltpu.VMEM((kblk * width, lanes), F32),
                pltpu.VMEM((width, lanes), F32),
            ],
            flops=FILL,
        )(group, mine_ghost, other_ghost, cols_t, tan_t, lap_t, wanted, disp_t, dmg_t, load_t)
    asked = swap(parcels, both)
    with jax.named_scope("source"):
        answer = call(
            functools.partial(source_kernel, cap),
            sds(parcel_shape(devices, cap * width + 2, lanes)),
            6,
            flops=FILL,
            specs=[VM, VM, VM, VM, SM, VM],
        )(asked, bucket, hist_t, strain_matrix, quad_weight[None, :], mech_total)
    got = swap(answer, both)
    with jax.named_scope("scale"):
        mech_out, dmg_out, norms = call(
            functools.partial(scale_kernel, cap, float(lanes * width * devices)),
            [sds((width, lanes)), sds((width, lanes)), sds((1, 2))],
            3,
        )(got, wanted, mech)
    return mech_out.T, dmg_out.T, norms[0]


def solution(mesh):
    rows = P(("dom", "blk"))
    in_specs = (rows,) * 6 + (P("dom"),) + (rows,) * 2 + (P(), P())
    out_specs = (rows, rows, P())
    return jax.shard_map(
        on_device, mesh=mesh, in_specs=in_specs, out_specs=out_specs, check_vma=False
    )
```

```python
import functools

import jax
import jax.numpy as jnp
from jax import lax
from jax.experimental import pallas as pl
from jax.experimental.pallas import tpu as pltpu
from jax.sharding import PartitionSpec as P

F32 = jnp.float32
BF16 = jnp.bfloat16
FILL = 10**10
VMEM_LIMIT = 4 * 1024 * 1024


def dot(a, b):
    return lax.dot_general(a, b, (((1,), (0,)), ((), ())), preferred_element_type=F32)


def dot_nt(a, b):
    return lax.dot_general(a, b, (((1,), (1,)), ((), ())), preferred_element_type=F32)


def split2(x):
    hi = x.astype(BF16)
    lo = (x - hi.astype(F32)).astype(BF16)
    return hi, lo


def split3(x):
    hi = x.astype(BF16)
    rest = x - hi.astype(F32)
    mid = rest.astype(BF16)
    lo = (rest - mid.astype(F32)).astype(BF16)
    return hi, mid, lo


def one_hot(cond):
    return jnp.where(cond, 1.0, 0.0).astype(BF16)


def iota(shape, dim):
    return lax.broadcasted_iota(jnp.int32, shape, dim)


def parcel_shape(devices, values, lanes):
    return (devices, -(-values // (4 * lanes)), 4, lanes)


def pack(hot, table, out, tail=0.0):
    devices, groups, _, lanes = out.shape
    hi, lo = split2(table)
    moved = dot_nt(hot, hi) + dot_nt(hot, lo)
    cap, width = moved.shape[0] // devices, moved.shape[1]
    rows = [moved[k * devices : (k + 1) * devices] for k in range(cap)]
    rows.append(jnp.zeros((devices, groups * 4 * lanes - cap * width), F32))
    flat = jnp.concatenate(rows, axis=1)
    for j in range(groups * 4):
        line = flat[:, j * lanes : (j + 1) * lanes]
        out[:, j // 4, j % 4, :] = line + tail if j == groups * 4 - 1 else line


def unpack(hot, got, width):
    devices, groups, _, lanes = got.shape
    flat = jnp.concatenate([got[:, j // 4, j % 4, :] for j in range(groups * 4)], axis=1)
    cap = hot.shape[0] // devices
    rows = jnp.concatenate([flat[:, k * width : (k + 1) * width] for k in range(cap)], axis=0)
    blank = jnp.zeros((cap * devices, -width % lanes), F32)
    tall = jnp.concatenate([rows, blank], axis=1).T[:width]
    hi, lo = split2(tall)
    return dot(hi, hot) + dot(lo, hot)


def asked_hot(request, cap):
    devices, _, lanes = request.shape
    slots = request[:, 0, :]
    lane = iota((devices, lanes), 1).astype(F32)
    hots = [one_hot(lane == slots[:, k : k + 1] - 1.0) for k in range(cap)]
    return jnp.concatenate(hots, axis=0)


def asking_hot(bucket, cap, devices):
    place = iota((devices, bucket.shape[1]), 0) * cap
    hots = [one_hot(place + k == bucket[...]) for k in range(cap)]
    return jnp.concatenate(hots, axis=0)


def root_of(damage):
    return jnp.sqrt((1.0 - damage) ** 2 + 0.001)


def fields_kernel(stacked, fields):
    width = stacked.shape[0] // 2
    dmg = stacked[width:, :]
    fields[:width, :] = (root_of(dmg) * stacked[:width, :]).astype(BF16)
    fields[width:, :] = dmg.astype(BF16)


def request_kernel(cap, dest, request, bucket):
    devices, _, lanes = request.shape
    d = dest[...]
    owner = d // lanes
    slot = d - owner * lanes
    square = jnp.broadcast_to(owner.astype(F32), (lanes, lanes))
    diag = iota((lanes, lanes), 0) == iota((lanes, lanes), 1)
    column = jnp.sum(jnp.where(diag, square, 0.0), axis=1, keepdims=True)
    before = iota((lanes, lanes), 0) < iota((lanes, lanes), 1)
    same = (column == square) & before
    rank = jnp.sum(jnp.where(same, 1.0, 0.0), axis=0, keepdims=True).astype(jnp.int32)
    bucket[...] = owner * cap + rank
    wanted = jnp.where(iota((devices, lanes), 0) == owner, (slot + 1).astype(F32), 0.0)
    ranks = one_hot(iota((lanes, lanes), 0) == rank)
    request[...] = dot_nt(wanted.astype(BF16), ranks)[:, None, :]


def pick_kernel(group, lists, out):
    parts = group.shape[0]
    table = jnp.concatenate([group[j] for j in range(parts)], axis=1)
    odd = lax.axis_index("blk") % 2
    row = jnp.where(odd == 0, lists[1:2, :], lists[0:1, :])
    hot = one_hot(iota((table.shape[1], row.shape[1]), 0) == row)
    out[...] = dot(table, hot).astype(BF16)


def total_of(x):
    line = jnp.sum(x * x, axis=0, keepdims=True)
    return jnp.sum(line, axis=1, keepdims=True)


def source_kernel(cap, got, bucket, hist, smat, weight, mech_total, out):
    quads, width, lanes = hist.shape
    hot = asking_hot(bucket, cap, got.shape[0])
    held = unpack(hot, got, 3 * width)
    gap = jnp.zeros((lanes - width, lanes), F32)
    d_hi, d_lo = split2(jnp.concatenate([held[:width], gap], axis=0))
    upper = jnp.concatenate([d_hi, d_lo], axis=1)
    lower = jnp.concatenate([d_hi, jnp.zeros_like(d_hi)], axis=1)
    sides = jnp.concatenate([upper, lower], axis=0)
    blank = jnp.zeros((width, lanes - width), F32)
    acc = jnp.zeros((width, lanes), F32)
    for q in range(quads):
        halves = split2(jnp.concatenate([smat[q], blank], axis=1))
        full = dot(jnp.concatenate(halves, axis=1), sides)
        strain = full[:, :lanes] + full[:, lanes:]
        acc = acc + weight[0, q] * jnp.maximum(hist[q], 0.5 * strain * strain)
    dmg_res = held[width : 2 * width] + 2.0 * acc * held[2 * width :]
    spare = iota((1, lanes), 1) - (lanes - 2)
    tail = jnp.where(spare == 0, mech_total[...], 0.0)
    tail = jnp.where(spare == 1, total_of(dmg_res), tail)
    pack(hot, dmg_res, out, tail)


def laplacian_kernel(
    cap,
    group,
    mine_ghost,
    other_ghost,
    columns,
    lap,
    request,
    disp,
    damage,
    parcels,
    left,
    near,
    diff,
):
    kblk, rows, width, lanes = lap.shape
    parts = group.shape[0]
    ghost = mine_ghost.shape[1]
    table = jnp.concatenate(
        [group[j] for j in range(parts)] + [mine_ghost[...], other_ghost[...]], axis=1
    )
    wanted = jnp.concatenate([columns[k : k + 1, :] for k in range(kblk)], axis=1)
    odd = lax.axis_index("blk") % 2
    own = parts * lanes
    starts = (0, own + odd * ghost, own + ghost - odd * ghost)
    hots = [
        one_hot(iota((size, kblk * lanes), 0) + start == wanted)
        for size, start in zip((own, ghost, ghost), starts)
    ]
    found = dot(table, jnp.concatenate(hots, axis=0))
    tall = []
    for field in range(2):
        cut = [
            found[field * width : (field + 1) * width, k * lanes : (k + 1) * lanes]
            for k in range(kblk)
        ]
        tall.append(jnp.concatenate(cut, axis=0))
    left[...] = tall[0].T.astype(BF16)
    near[...] = tall[1]

    @pl.loop(0, rows // 8)
    def _(step):
        acc = [jnp.zeros((8, lanes), F32) for _ in range(8)]
        for k in range(kblk):
            for c in range(0, width, 16):
                base = k * width + c
                lo = near[base : base + 8, :]
                hi = near[base + 8 : base + 16, :]
                for r in range(8):
                    block = lap[k, step * 8 + r, c : c + 16, :].astype(F32)
                    acc[r] = acc[r] + (block[:8] * lo + block[8:] * hi)
        sums = [jnp.sum(a, axis=0, keepdims=True) for a in acc]
        diff[pl.ds(pl.multiple_of(step * 8, 8), 8), :] = jnp.concatenate(sums, axis=0)

    d = damage[...]
    values = jnp.concatenate([disp[...], diff[...] + d, d - 1.0], axis=0)
    pack(asked_hot(request, cap), values, parcels)


def tangent_kernel(left, tan_hbm, damage, load, mech, mech_total, tan, sems):
    kblk, rows, width, lanes = tan.shape
    depth = kblk * width
    steps = rows // 8

    def piece(step):
        place = pl.ds(pl.multiple_of(step * 8, 8), 8)
        return pltpu.make_async_copy(tan_hbm.at[:, place], tan.at[:, place], sems.at[step])

    @pl.loop(0, steps)
    def _(step):
        piece(step).start()

    lane = iota((8, 2 * lanes), 1) % lanes
    mine = iota((8, 2 * lanes), 0) == lane % 8

    @pl.loop(0, steps)
    def _(step):
        piece(step).wait()
        lines = []
        for r in range(0, 8, 2):
            pair = [tan[:, step * 8 + r + j].reshape(depth, lanes) for j in range(2)]
            full = dot(left[...], jnp.concatenate(pair, axis=1))
            kept = full[:8]
            for g in range(1, lanes // 8):
                kept = jnp.where(lane // 8 == g, full[g * 8 : g * 8 + 8], kept)
            line = jnp.sum(jnp.where(mine, kept, 0.0), axis=0, keepdims=True)
            lines += [line[:, :lanes], line[:, lanes:]]
        mech[pl.ds(pl.multiple_of(step * 8, 8), 8), :] = jnp.concatenate(lines, axis=0)

    mech_res = root_of(damage[...]) * mech[...] - load[...]
    mech[...] = mech_res
    mech_total[...] = jnp.broadcast_to(total_of(mech_res), mech_total.shape)


def scale_kernel(cap, entries, got, request, mech, mech_out, dmg_out, norms):
    width, lanes = mech.shape
    last = got[:, got.shape[1] - 1, 3, :]
    total = jnp.sum(last, axis=0, keepdims=True)[:, lanes - 2 :]
    norm = jnp.sqrt(total / entries + 1e-06)
    mech_out[...] = mech[...] / norm[:, 0:1]
    dmg_out[...] = unpack(asked_hot(request, cap), got, width) / norm[:, 1:2]
    norms[...] = norm


VM = pl.BlockSpec(memory_space=pltpu.VMEM)
ANY = pl.BlockSpec(memory_space=pl.ANY)
SM = pl.BlockSpec(memory_space=pltpu.SMEM)


def call(body, outs, ins, scratch=(), flops=0, nbytes=0, specs=None, limit=VMEM_LIMIT):
    one = not isinstance(outs, (list, tuple))
    return pl.pallas_call(
        body,
        out_shape=outs,
        in_specs=specs or [VM] * ins,
        out_specs=VM if one else [VM] * len(outs),
        scratch_shapes=list(scratch),
        compiler_params=pltpu.CompilerParams(vmem_limit_bytes=limit),
        cost_estimate=pl.CostEstimate(flops=flops, bytes_accessed=nbytes, transcendentals=0),
    )


def sds(shape, dtype=F32):
    return jax.ShapeDtypeStruct(shape, dtype)


def swap(x, axes):
    return lax.all_to_all(x, axes, split_axis=0, concat_axis=0, tiled=True)


def on_device(
    displacement,
    damage,
    applied_load,
    tangent,
    laplacian,
    block_columns,
    send_lists,
    hist_mech,
    mech_dest,
    strain_matrix,
    quad_weight,
):
    lanes, width = displacement.shape
    kblk = tangent.shape[1]
    quads = hist_mech.shape[1]
    ghost = send_lists.shape[2]
    both = ("dom", "blk")
    devices = lax.axis_size(both)
    groups = lax.axis_size("dom")
    disp_t = displacement.T
    dmg_t = damage.T
    load_t = applied_load.T
    tan_t = jnp.transpose(tangent, (1, 2, 3, 0))
    lap_t = jnp.transpose(laplacian, (1, 2, 3, 0))
    hist_t = jnp.transpose(hist_mech, (1, 2, 0))
    cols_t = block_columns.T

    cap = lanes // devices + 1
    stacked = jnp.concatenate([disp_t, dmg_t], axis=0)
    with jax.named_scope("fields"):
        fields = call(fields_kernel, sds(stacked.shape, BF16), 1, flops=FILL)(stacked)
    group = lax.all_gather(fields, "blk", axis=0, tiled=False)
    with jax.named_scope("picks"):
        picked = call(pick_kernel, sds((2 * width, ghost), BF16), 2, flops=20 * FILL)(
            group, send_lists[0]
        )
    picked, mech_dest = lax.optimization_barrier((picked, mech_dest))
    with jax.named_scope("requests"):
        request, bucket = call(
            functools.partial(request_kernel, cap),
            [sds((devices, 1, lanes)), sds((1, lanes), jnp.int32)],
            1,
            flops=FILL,
        )(mech_dest[None, :])
    wanted = swap(request, both)
    blocks = lax.axis_size("blk")
    everyone = [(a, b) for a in range(groups) for b in range(blocks)]
    hop = [(a * blocks + b, (a + 1 - b % 2 * 2) * blocks + b) for a, b in everyone]
    hop = [(i, j) for i, j in hop if 0 <= j < groups * blocks]
    side = [(b, b ^ 1) for b in range(blocks)]
    mine_ghost = lax.ppermute(picked, both, hop)
    mine_ghost, wanted = lax.optimization_barrier((mine_ghost, wanted))
    other_ghost = lax.ppermute(mine_ghost, "blk", side)
    with jax.named_scope("laplacian"):
        parcels, left = call(
            functools.partial(laplacian_kernel, cap),
            [
                sds(parcel_shape(devices, 3 * cap * width, lanes)),
                sds((lanes, kblk * width), BF16),
            ],
            8,
            [pltpu.VMEM((kblk * width, lanes), F32), pltpu.VMEM((width, lanes), F32)],
            flops=FILL,
        )(group, mine_ghost, other_ghost, cols_t, lap_t, wanted, disp_t, dmg_t)
    asked = swap(parcels, both)
    with jax.named_scope("tangent"):
        mech, mech_total = call(
            tangent_kernel,
            [sds((width, lanes)), sds((1, lanes))],
            4,
            [pltpu.VMEM(tan_t.shape, BF16), pltpu.SemaphoreType.DMA((width // 8,))],
            flops=FILL,
            specs=[VM, ANY, VM, VM],
            limit=48 * 1024 * 1024,
        )(left, tan_t, dmg_t, load_t)
    asked, mech_total = lax.optimization_barrier((asked, mech_total))
    with jax.named_scope("source"):
        answer = call(
            functools.partial(source_kernel, cap),
            sds(parcel_shape(devices, cap * width + 2, lanes)),
            6,
            flops=FILL,
            specs=[VM, VM, VM, VM, SM, VM],
        )(asked, bucket, hist_t, strain_matrix, quad_weight[None, :], mech_total)
    got = swap(answer, both)
    with jax.named_scope("scale"):
        mech_out, dmg_out, norms = call(
            functools.partial(scale_kernel, cap, float(lanes * width * devices)),
            [sds((width, lanes)), sds((width, lanes)), sds((1, 2))],
            3,
        )(got, wanted, mech)
    return mech_out.T, dmg_out.T, norms[0]


def solution(mesh):
    rows = P(("dom", "blk"))
    in_specs = (rows,) * 6 + (P("dom"),) + (rows,) * 2 + (P(), P())
    out_specs = (rows, rows, P())
    return jax.shard_map(
        on_device, mesh=mesh, in_specs=in_specs, out_specs=out_specs, check_vma=False
    )
```

```python
import functools

import jax
import jax.numpy as jnp
from jax import lax
from jax.experimental import pallas as pl
from jax.experimental.pallas import tpu as pltpu
from jax.sharding import PartitionSpec as P

F32 = jnp.float32
BF16 = jnp.bfloat16
FILL = 10**10
VMEM_LIMIT = 4 * 1024 * 1024


def dot(a, b):
    return lax.dot_general(a, b, (((1,), (0,)), ((), ())), preferred_element_type=F32)


def dot_nt(a, b):
    return lax.dot_general(a, b, (((1,), (1,)), ((), ())), preferred_element_type=F32)


def split2(x):
    hi = x.astype(BF16)
    lo = (x - hi.astype(F32)).astype(BF16)
    return hi, lo


def split3(x):
    hi = x.astype(BF16)
    rest = x - hi.astype(F32)
    mid = rest.astype(BF16)
    lo = (rest - mid.astype(F32)).astype(BF16)
    return hi, mid, lo


def one_hot(cond):
    return jnp.where(cond, 1.0, 0.0).astype(BF16)


def iota(shape, dim):
    return lax.broadcasted_iota(jnp.int32, shape, dim)


def section_size(values, lanes):
    return -(-values // (4 * lanes))


def pack(hot, table, out, section, tail=0.0):
    devices, _, _, lanes = out.shape
    hi, lo = split2(table)
    moved = dot_nt(hot, hi) + dot_nt(hot, lo)
    cap, width = moved.shape[0] // devices, moved.shape[1]
    first, size = section
    rows = [moved[k * devices : (k + 1) * devices] for k in range(cap)]
    rows.append(jnp.zeros((devices, size * 4 * lanes - cap * width), F32))
    flat = jnp.concatenate(rows, axis=1)
    for j in range(size * 4):
        line = flat[:, j * lanes : (j + 1) * lanes]
        out[:, first + j // 4, j % 4, :] = line + tail if j == size * 4 - 1 else line


def unpack(hot, got, width, sections):
    devices, _, _, lanes = got.shape
    cap = hot.shape[0] // devices
    blank = jnp.zeros((cap * devices, -width % lanes), F32)
    tall = []
    for first, size in sections:
        lines = [got[:, first + j // 4, j % 4, :] for j in range(size * 4)]
        flat = jnp.concatenate(lines, axis=1)
        rows = [flat[:, k * width : (k + 1) * width] for k in range(cap)]
        tall.append(jnp.concatenate([jnp.concatenate(rows, axis=0), blank], axis=1).T[:width])
    hi, lo = split2(jnp.concatenate(tall, axis=0))
    found = dot(hi, hot) + dot(lo, hot)
    return [found[i * width : (i + 1) * width] for i in range(len(sections))]


def asked_hot(request, cap):
    devices, _, lanes = request.shape
    slots = request[:, 0, :]
    lane = iota((devices, lanes), 1).astype(F32)
    hots = [one_hot(lane == slots[:, k : k + 1] - 1.0) for k in range(cap)]
    return jnp.concatenate(hots, axis=0)


def asking_hot(bucket, cap, devices):
    place = iota((devices, bucket.shape[1]), 0) * cap
    hots = [one_hot(place + k == bucket[...]) for k in range(cap)]
    return jnp.concatenate(hots, axis=0)


def root_of(damage):
    return jnp.sqrt((1.0 - damage) ** 2 + 0.001)


def fields_kernel(stacked, fields):
    width = stacked.shape[0] // 2
    dmg = stacked[width:, :]
    fields[:width, :] = (root_of(dmg) * stacked[:width, :]).astype(BF16)
    fields[width:, :] = dmg.astype(BF16)


def request_kernel(cap, dest, request, bucket):
    devices, _, lanes = request.shape
    d = dest[...]
    owner = d // lanes
    slot = d - owner * lanes
    square = jnp.broadcast_to(owner.astype(F32), (lanes, lanes))
    diag = iota((lanes, lanes), 0) == iota((lanes, lanes), 1)
    column = jnp.sum(jnp.where(diag, square, 0.0), axis=1, keepdims=True)
    before = iota((lanes, lanes), 0) < iota((lanes, lanes), 1)
    same = (column == square) & before
    rank = jnp.sum(jnp.where(same, 1.0, 0.0), axis=0, keepdims=True).astype(jnp.int32)
    bucket[...] = owner * cap + rank
    wanted = jnp.where(iota((devices, lanes), 0) == owner, (slot + 1).astype(F32), 0.0)
    ranks = one_hot(iota((lanes, lanes), 0) == rank)
    request[...] = dot_nt(wanted.astype(BF16), ranks)[:, None, :]


def pick_kernel(group, lists, out):
    parts = group.shape[0]
    table = jnp.concatenate([group[j] for j in range(parts)], axis=1)
    odd = lax.axis_index("blk") % 2
    row = jnp.where(odd == 0, lists[1:2, :], lists[0:1, :])
    hot = one_hot(iota((table.shape[1], row.shape[1]), 0) == row)
    out[...] = dot(table, hot).astype(BF16)


def total_of(x):
    line = jnp.sum(x * x, axis=0, keepdims=True)
    return jnp.sum(line, axis=1, keepdims=True)


def source_kernel(cap, got, bucket, hist, smat, weight, mech_total, out):
    quads, width, lanes = hist.shape
    hot = asking_hot(bucket, cap, got.shape[0])
    size = got.shape[1] // 3
    disp, v, u = unpack(hot, got, width, [(i * size, size) for i in range(3)])
    gap = jnp.zeros((lanes - width, lanes), F32)
    d_hi, d_lo = split2(jnp.concatenate([disp, gap], axis=0))
    upper = jnp.concatenate([d_hi, d_lo], axis=1)
    lower = jnp.concatenate([d_hi, jnp.zeros_like(d_hi)], axis=1)
    sides = jnp.concatenate([upper, lower], axis=0)
    blank = jnp.zeros((width, lanes - width), F32)
    acc = jnp.zeros((width, lanes), F32)
    for q in range(quads):
        halves = split2(jnp.concatenate([smat[q], blank], axis=1))
        full = dot(jnp.concatenate(halves, axis=1), sides)
        strain = full[:, :lanes] + full[:, lanes:]
        acc = acc + weight[0, q] * jnp.maximum(hist[q], 0.5 * strain * strain)
    dmg_res = u + 2.0 * acc * v
    spare = iota((1, lanes), 1) - (lanes - 2)
    tail = jnp.where(spare == 0, mech_total[...], 0.0)
    tail = jnp.where(spare == 1, total_of(dmg_res), tail)
    pack(hot, dmg_res, out, (0, out.shape[1]), tail)


def columns_row(columns):
    return jnp.concatenate([columns[k : k + 1, :] for k in range(columns.shape[0])], axis=1)


def own_gather(group, rows, wanted):
    table = jnp.concatenate([group[j, rows, :] for j in range(group.shape[0])], axis=1)
    hot = one_hot(iota((table.shape[1], wanted.shape[1]), 0) == wanted)
    return dot(table, hot)


def ghost_gather(own, mine_ghost, other_ghost, rows, wanted):
    ghost = mine_ghost.shape[1]
    odd = lax.axis_index("blk") % 2
    table = jnp.concatenate([mine_ghost[rows, :], other_ghost[rows, :]], axis=1)
    hots = [
        one_hot(iota((ghost, wanted.shape[1]), 0) + start == wanted)
        for start in (own + odd * ghost, own + ghost - odd * ghost)
    ]
    return dot(table, jnp.concatenate(hots, axis=0))


def stacked_columns(found, kblk):
    lanes = found.shape[1] // kblk
    cut = [found[:, k * lanes : (k + 1) * lanes] for k in range(kblk)]
    return jnp.concatenate(cut, axis=0)


def early_kernel(cap, group, columns, request, disp, damage, found, sections):
    width = disp.shape[0]
    found[...] = own_gather(group, pl.ds(width, width), columns_row(columns))
    hot = asked_hot(request, cap)
    size = sections.shape[1] // 2
    pack(hot, disp[...], sections, (0, size))
    pack(hot, damage[...] - 1.0, sections, (size, size))


def laplacian_kernel(
    cap,
    found_own,
    mine_ghost,
    other_ghost,
    columns,
    lap,
    request,
    damage,
    sections,
    parcels,
    near,
    diff,
):
    kblk, rows, width, lanes = lap.shape
    own = lax.axis_size("blk") * lanes
    half = pl.ds(width, width)
    found = found_own[...] + ghost_gather(
        own, mine_ghost, other_ghost, half, columns_row(columns)
    )
    near[...] = stacked_columns(found, kblk)

    @pl.loop(0, rows // 8)
    def _(step):
        acc = [jnp.zeros((8, lanes), F32) for _ in range(8)]
        for k in range(kblk):
            for c in range(0, width, 16):
                base = k * width + c
                lo = near[base : base + 8, :]
                hi = near[base + 8 : base + 16, :]
                for r in range(8):
                    block = lap[k, step * 8 + r, c : c + 16, :].astype(F32)
                    acc[r] = acc[r] + (block[:8] * lo + block[8:] * hi)
        sums = [jnp.sum(a, axis=0, keepdims=True) for a in acc]
        diff[pl.ds(pl.multiple_of(step * 8, 8), 8), :] = jnp.concatenate(sums, axis=0)

    size = sections.shape[1] // 2
    parcels[:, : 2 * size, :, :] = sections[...]
    pack(asked_hot(request, cap), diff[...] + damage[...], parcels, (2 * size, size))


def tangent_kernel(
    group, mine_ghost, other_ghost, columns, tan_hbm, damage, load, mech, mech_total, tan, left_ref, sems
):
    kblk, rows, width, lanes = tan.shape
    depth = kblk * width
    steps = rows // 8

    def piece(step):
        place = pl.ds(pl.multiple_of(step * 8, 8), 8)
        return pltpu.make_async_copy(tan_hbm.at[:, place], tan.at[:, place], sems.at[step])

    @pl.loop(0, steps)
    def _(step):
        piece(step).start()

    wanted = columns_row(columns)
    own = group.shape[0] * lanes
    half = pl.ds(0, width)
    found = own_gather(group, half, wanted)
    found = found + ghost_gather(own, mine_ghost, other_ghost, half, wanted)
    left_ref[...] = stacked_columns(found, kblk).T.astype(BF16)
    lane = iota((8, 2 * lanes), 1) % lanes
    mine = iota((8, 2 * lanes), 0) == lane % 8

    @pl.loop(0, steps)
    def _(step):
        piece(step).wait()
        lines = []
        for r in range(0, 8, 2):
            pair = [tan[:, step * 8 + r + j].reshape(depth, lanes) for j in range(2)]
            full = dot(left_ref[...], jnp.concatenate(pair, axis=1))
            kept = full[:8]
            for g in range(1, lanes // 8):
                kept = jnp.where(lane // 8 == g, full[g * 8 : g * 8 + 8], kept)
            line = jnp.sum(jnp.where(mine, kept, 0.0), axis=0, keepdims=True)
            lines += [line[:, :lanes], line[:, lanes:]]
        mech[pl.ds(pl.multiple_of(step * 8, 8), 8), :] = jnp.concatenate(lines, axis=0)

    mech_res = root_of(damage[...]) * mech[...] - load[...]
    mech[...] = mech_res
    mech_total[...] = jnp.broadcast_to(total_of(mech_res), mech_total.shape)


def scale_kernel(cap, entries, got, request, mech, mech_out, dmg_out, norms):
    width, lanes = mech.shape
    last = got[:, got.shape[1] - 1, 3, :]
    total = jnp.sum(last, axis=0, keepdims=True)[:, lanes - 2 :]
    norm = jnp.sqrt(total / entries + 1e-06)
    mech_out[...] = mech[...] / norm[:, 0:1]
    (dmg,) = unpack(asked_hot(request, cap), got, width, [(0, got.shape[1])])
    dmg_out[...] = dmg / norm[:, 1:2]
    norms[...] = norm


VM = pl.BlockSpec(memory_space=pltpu.VMEM)
ANY = pl.BlockSpec(memory_space=pl.ANY)
SM = pl.BlockSpec(memory_space=pltpu.SMEM)


def call(body, outs, ins, scratch=(), flops=0, nbytes=0, specs=None, limit=VMEM_LIMIT):
    one = not isinstance(outs, (list, tuple))
    return pl.pallas_call(
        body,
        out_shape=outs,
        in_specs=specs or [VM] * ins,
        out_specs=VM if one else [VM] * len(outs),
        scratch_shapes=list(scratch),
        compiler_params=pltpu.CompilerParams(vmem_limit_bytes=limit),
        cost_estimate=pl.CostEstimate(flops=flops, bytes_accessed=nbytes, transcendentals=0),
    )


def sds(shape, dtype=F32):
    return jax.ShapeDtypeStruct(shape, dtype)


def swap(x, axes):
    return lax.all_to_all(x, axes, split_axis=0, concat_axis=0, tiled=True)


def on_device(
    displacement,
    damage,
    applied_load,
    tangent,
    laplacian,
    block_columns,
    send_lists,
    hist_mech,
    mech_dest,
    strain_matrix,
    quad_weight,
):
    lanes, width = displacement.shape
    kblk = tangent.shape[1]
    quads = hist_mech.shape[1]
    ghost = send_lists.shape[2]
    both = ("dom", "blk")
    devices = lax.axis_size(both)
    groups = lax.axis_size("dom")
    disp_t = displacement.T
    dmg_t = damage.T
    load_t = applied_load.T
    tan_t = jnp.transpose(tangent, (1, 2, 3, 0))
    lap_t = jnp.transpose(laplacian, (1, 2, 3, 0))
    hist_t = jnp.transpose(hist_mech, (1, 2, 0))
    cols_t = block_columns.T

    cap = lanes // devices + 1
    stacked = jnp.concatenate([disp_t, dmg_t], axis=0)
    with jax.named_scope("fields"):
        fields = call(fields_kernel, sds(stacked.shape, BF16), 1, flops=FILL)(stacked)
    group = lax.all_gather(fields, "blk", axis=0, tiled=False)
    with jax.named_scope("picks"):
        picked = call(pick_kernel, sds((2 * width, ghost), BF16), 2, flops=20 * FILL)(
            group, send_lists[0]
        )
    picked, mech_dest = lax.optimization_barrier((picked, mech_dest))
    with jax.named_scope("requests"):
        request, bucket = call(
            functools.partial(request_kernel, cap),
            [sds((devices, 1, lanes)), sds((1, lanes), jnp.int32)],
            1,
            flops=FILL,
        )(mech_dest[None, :])
    wanted = swap(request, both)
    blocks = lax.axis_size("blk")
    everyone = [(a, b) for a in range(groups) for b in range(blocks)]
    hop = [(a * blocks + b, (a + 1 - b % 2 * 2) * blocks + b) for a, b in everyone]
    hop = [(i, j) for i, j in hop if 0 <= j < groups * blocks]
    side = [(b, b ^ 1) for b in range(blocks)]
    mine_ghost = lax.ppermute(picked, both, hop)
    mine_ghost, wanted = lax.optimization_barrier((mine_ghost, wanted))
    other_ghost = lax.ppermute(mine_ghost, "blk", side)
    size = section_size(cap * width, lanes)
    with jax.named_scope("early"):
        found, sections = call(
            functools.partial(early_kernel, cap),
            [sds((width, kblk * lanes)), sds((devices, 2 * size, 4, lanes))],
            5,
        )(group, cols_t, wanted, disp_t, dmg_t)
    with jax.named_scope("laplacian"):
        parcels = call(
            functools.partial(laplacian_kernel, cap),
            sds((devices, 3 * size, 4, lanes)),
            8,
            [pltpu.VMEM((kblk * width, lanes), F32), pltpu.VMEM((width, lanes), F32)],
            flops=FILL,
        )(found, mine_ghost, other_ghost, cols_t, lap_t, wanted, dmg_t, sections)
    asked = swap(parcels, both)
    with jax.named_scope("tangent"):
        mech, mech_total = call(
            tangent_kernel,
            [sds((width, lanes)), sds((1, lanes))],
            7,
            [
                pltpu.VMEM(tan_t.shape, BF16),
                pltpu.VMEM((lanes, kblk * width), BF16),
                pltpu.SemaphoreType.DMA((width // 8,)),
            ],
            flops=FILL,
            specs=[VM, VM, VM, VM, ANY, VM, VM],
            limit=48 * 1024 * 1024,
        )(group, mine_ghost, other_ghost, cols_t, tan_t, dmg_t, load_t)
    asked, mech_total = lax.optimization_barrier((asked, mech_total))
    with jax.named_scope("source"):
        answer = call(
            functools.partial(source_kernel, cap),
            sds((devices, section_size(cap * width + 2, lanes), 4, lanes)),
            6,
            flops=FILL,
            specs=[VM, VM, VM, VM, SM, VM],
        )(asked, bucket, hist_t, strain_matrix, quad_weight[None, :], mech_total)
    got = swap(answer, both)
    with jax.named_scope("scale"):
        mech_out, dmg_out, norms = call(
            functools.partial(scale_kernel, cap, float(lanes * width * devices)),
            [sds((width, lanes)), sds((width, lanes)), sds((1, 2))],
            3,
        )(got, wanted, mech)
    return mech_out.T, dmg_out.T, norms[0]


def solution(mesh):
    rows = P(("dom", "blk"))
    in_specs = (rows,) * 6 + (P("dom"),) + (rows,) * 2 + (P(), P())
    out_specs = (rows, rows, P())
    return jax.shard_map(
        on_device, mesh=mesh, in_specs=in_specs, out_specs=out_specs, check_vma=False
    )
```

```python
import functools

import jax
import jax.numpy as jnp
from jax import lax
from jax.experimental import pallas as pl
from jax.experimental.pallas import tpu as pltpu
from jax.sharding import PartitionSpec as P

F32 = jnp.float32
BF16 = jnp.bfloat16
FILL = 10**10
POINTS = 9
STEP = 16
VMEM_LIMIT = 4 * 1024 * 1024


def dot(a, b):
    return lax.dot_general(a, b, (((1,), (0,)), ((), ())), preferred_element_type=F32)


def dot_nt(a, b):
    return lax.dot_general(a, b, (((1,), (1,)), ((), ())), preferred_element_type=F32)


def split2(x):
    hi = x.astype(BF16)
    lo = (x - hi.astype(F32)).astype(BF16)
    return hi, lo


def split3(x):
    hi = x.astype(BF16)
    rest = x - hi.astype(F32)
    mid = rest.astype(BF16)
    lo = (rest - mid.astype(F32)).astype(BF16)
    return hi, mid, lo


def one_hot(cond):
    return jnp.where(cond, 1.0, 0.0).astype(BF16)


def iota(shape, dim):
    return lax.broadcasted_iota(jnp.int32, shape, dim)


def section_size(values, lanes):
    return -(-values // (4 * lanes))


def pack(hot, table, out, section, tail=0.0):
    devices, _, _, lanes = out.shape
    hi, lo = split2(table)
    moved = dot_nt(hot, hi) + dot_nt(hot, lo)
    cap, width = moved.shape[0] // devices, moved.shape[1]
    first, size = section
    rows = [moved[k * devices : (k + 1) * devices] for k in range(cap)]
    rows.append(jnp.zeros((devices, size * 4 * lanes - cap * width), F32))
    flat = jnp.concatenate(rows, axis=1)
    for j in range(size * 4):
        line = flat[:, j * lanes : (j + 1) * lanes]
        out[:, first + j // 4, j % 4, :] = line + tail if j == size * 4 - 1 else line


def unpack(hot, got, width, sections):
    devices, _, _, lanes = got.shape
    cap = hot.shape[0] // devices
    blank = jnp.zeros((cap * devices, -width % lanes), F32)
    tall = []
    for first, size in sections:
        lines = [got[:, first + j // 4, j % 4, :] for j in range(size * 4)]
        flat = jnp.concatenate(lines, axis=1)
        rows = [flat[:, k * width : (k + 1) * width] for k in range(cap)]
        tall.append(jnp.concatenate([jnp.concatenate(rows, axis=0), blank], axis=1).T[:width])
    hi, lo = split2(jnp.concatenate(tall, axis=0))
    found = dot(hi, hot) + dot(lo, hot)
    return [found[i * width : (i + 1) * width] for i in range(len(sections))]


def asked_hot(request, cap):
    devices, _, lanes = request.shape
    slots = request[:, 0, :]
    lane = iota((devices, lanes), 1).astype(F32)
    hots = [one_hot(lane == slots[:, k : k + 1] - 1.0) for k in range(cap)]
    return jnp.concatenate(hots, axis=0)


def asking_hot(bucket, cap, devices):
    place = iota((devices, bucket.shape[1]), 0) * cap
    hots = [one_hot(place + k == bucket[...]) for k in range(cap)]
    return jnp.concatenate(hots, axis=0)


def root_of(damage):
    return jnp.sqrt((1.0 - damage) ** 2 + 0.001)


def fields_kernel(stacked, fields):
    width = stacked.shape[0] // 2
    dmg = stacked[width:, :]
    fields[:width, :] = (root_of(dmg) * stacked[:width, :]).astype(BF16)
    fields[width:, :] = dmg.astype(BF16)


def request_kernel(cap, dest, request, bucket):
    devices, _, lanes = request.shape
    d = dest[...]
    owner = d // lanes
    slot = d - owner * lanes
    square = jnp.broadcast_to(owner.astype(F32), (lanes, lanes))
    diag = iota((lanes, lanes), 0) == iota((lanes, lanes), 1)
    column = jnp.sum(jnp.where(diag, square, 0.0), axis=1, keepdims=True)
    before = iota((lanes, lanes), 0) < iota((lanes, lanes), 1)
    same = (column == square) & before
    rank = jnp.sum(jnp.where(same, 1.0, 0.0), axis=0, keepdims=True).astype(jnp.int32)
    bucket[...] = owner * cap + rank
    wanted = jnp.where(iota((devices, lanes), 0) == owner, (slot + 1).astype(F32), 0.0)
    ranks = one_hot(iota((lanes, lanes), 0) == rank)
    request[...] = dot_nt(wanted.astype(BF16), ranks)[:, None, :]


def pick_kernel(group, lists, out):
    parts = group.shape[0]
    table = jnp.concatenate([group[j] for j in range(parts)], axis=1)
    odd = lax.axis_index("blk") % 2
    row = jnp.where(odd == 0, lists[1:2, :], lists[0:1, :])
    hot = one_hot(iota((table.shape[1], row.shape[1]), 0) == row)
    out[...] = dot(table, hot).astype(BF16)


def total_of(x):
    line = jnp.sum(x * x, axis=0, keepdims=True)
    return jnp.sum(line, axis=1, keepdims=True)


def source_kernel(cap, got, bucket, hist, smat, weight, mech_total, out):
    quads, width, lanes = hist.shape
    hot = asking_hot(bucket, cap, got.shape[0])
    size = got.shape[1] // 3
    disp, v, u = unpack(hot, got, width, [(i * size, size) for i in range(3)])
    gap = jnp.zeros((lanes - width, lanes), F32)
    d_hi, d_lo = split2(jnp.concatenate([disp, gap], axis=0))
    upper = jnp.concatenate([d_hi, d_lo], axis=1)
    lower = jnp.concatenate([d_hi, jnp.zeros_like(d_hi)], axis=1)
    sides = jnp.concatenate([upper, lower], axis=0)
    acc = jnp.zeros((width, lanes), F32)
    for first in range(0, quads, POINTS):
        points = range(first, min(first + POINTS, quads))
        rows = smat[pl.ds(first, len(points))].reshape(len(points) * width, width)
        blank = jnp.zeros((rows.shape[0], lanes - width), F32)
        halves = split2(jnp.concatenate([rows, blank], axis=1))
        full = dot(jnp.concatenate(halves, axis=1), sides)
        strain = full[:, :lanes] + full[:, lanes:]
        energy = 0.5 * strain * strain
        for q in points:
            part = energy[(q - first) * width : (q - first + 1) * width]
            acc = acc + weight[0, q] * jnp.maximum(hist[q], part)
    dmg_res = u + 2.0 * acc * v
    spare = iota((1, lanes), 1) - (lanes - 2)
    tail = jnp.where(spare == 0, mech_total[...], 0.0)
    tail = jnp.where(spare == 1, total_of(dmg_res), tail)
    pack(hot, dmg_res, out, (0, out.shape[1]), tail)


def columns_row(columns):
    return jnp.concatenate([columns[k : k + 1, :] for k in range(columns.shape[0])], axis=1)


def own_gather(group, rows, wanted):
    table = jnp.concatenate([group[j, rows, :] for j in range(group.shape[0])], axis=1)
    hot = one_hot(iota((table.shape[1], wanted.shape[1]), 0) == wanted)
    return dot(table, hot)


def ghost_gather(own, mine_ghost, other_ghost, rows, wanted):
    ghost = mine_ghost.shape[1]
    odd = lax.axis_index("blk") % 2
    table = jnp.concatenate([mine_ghost[rows, :], other_ghost[rows, :]], axis=1)
    hots = [
        one_hot(iota((ghost, wanted.shape[1]), 0) + start == wanted)
        for start in (own + odd * ghost, own + ghost - odd * ghost)
    ]
    return dot(table, jnp.concatenate(hots, axis=0))


def stacked_columns(found, kblk):
    lanes = found.shape[1] // kblk
    cut = [found[:, k * lanes : (k + 1) * lanes] for k in range(kblk)]
    return jnp.concatenate(cut, axis=0)


def early_kernel(cap, group, columns, request, disp, damage, found, sections, asked):
    width = disp.shape[0]
    found[...] = own_gather(group, pl.ds(width, width), columns_row(columns))
    hot = asked_hot(request, cap)
    asked[...] = hot
    size = sections.shape[1] // 2
    pack(hot, disp[...], sections, (0, size))
    pack(hot, damage[...] - 1.0, sections, (size, size))


def laplacian_kernel(
    found_own,
    mine_ghost,
    other_ghost,
    columns,
    lap,
    asked,
    damage,
    sections,
    parcels,
    near,
    diff,
):
    kblk, rows, width, lanes = lap.shape
    own = lax.axis_size("blk") * lanes
    half = pl.ds(width, width)
    found = found_own[...] + ghost_gather(
        own, mine_ghost, other_ghost, half, columns_row(columns)
    )
    near[...] = stacked_columns(found, kblk)

    @pl.loop(0, rows // STEP)
    def _(step):
        acc = [jnp.zeros((8, lanes), F32) for _ in range(STEP)]
        for k in range(kblk):
            for c in range(0, width, 16):
                base = k * width + c
                lo = near[base : base + 8, :]
                hi = near[base + 8 : base + 16, :]
                for r in range(STEP):
                    block = lap[k, step * STEP + r, c : c + 16, :].astype(F32)
                    acc[r] = acc[r] + (block[:8] * lo + block[8:] * hi)
        sums = [jnp.sum(a, axis=0, keepdims=True) for a in acc]
        place = pl.ds(pl.multiple_of(step * STEP, STEP), STEP)
        diff[place, :] = jnp.concatenate(sums, axis=0)

    size = sections.shape[1] // 2
    parcels[:, : 2 * size, :, :] = sections[...]
    pack(asked[...], diff[...] + damage[...], parcels, (2 * size, size))


def tangent_kernel(
    group, mine_ghost, other_ghost, columns, tan_hbm, damage, load, mech, mech_total, tan, left_ref, sems
):
    kblk, rows, width, lanes = tan.shape
    depth = kblk * width
    steps = rows // 8

    def piece(step):
        place = pl.ds(pl.multiple_of(step * 8, 8), 8)
        return pltpu.make_async_copy(tan_hbm.at[:, place], tan.at[:, place], sems.at[step])

    @pl.loop(0, steps)
    def _(step):
        piece(step).start()

    wanted = columns_row(columns)
    own = group.shape[0] * lanes
    half = pl.ds(0, width)
    found = own_gather(group, half, wanted)
    found = found + ghost_gather(own, mine_ghost, other_ghost, half, wanted)
    left_ref[...] = stacked_columns(found, kblk).T.astype(BF16)
    lane = iota((8, 2 * lanes), 1) % lanes
    mine = iota((8, 2 * lanes), 0) == lane % 8

    @pl.loop(0, steps)
    def _(step):
        piece(step).wait()
        lines = []
        for r in range(0, 8, 2):
            pair = [tan[:, step * 8 + r + j].reshape(depth, lanes) for j in range(2)]
            full = dot(left_ref[...], jnp.concatenate(pair, axis=1))
            kept = full[:8]
            for g in range(1, lanes // 8):
                kept = jnp.where(lane // 8 == g, full[g * 8 : g * 8 + 8], kept)
            line = jnp.sum(jnp.where(mine, kept, 0.0), axis=0, keepdims=True)
            lines += [line[:, :lanes], line[:, lanes:]]
        mech[pl.ds(pl.multiple_of(step * 8, 8), 8), :] = jnp.concatenate(lines, axis=0)

    mech_res = root_of(damage[...]) * mech[...] - load[...]
    mech[...] = mech_res
    mech_total[...] = jnp.broadcast_to(total_of(mech_res), mech_total.shape)


def scale_kernel(cap, entries, got, request, mech, mech_out, dmg_out, norms):
    width, lanes = mech.shape
    last = got[:, got.shape[1] - 1, 3, :]
    total = jnp.sum(last, axis=0, keepdims=True)[:, lanes - 2 :]
    norm = jnp.sqrt(total / entries + 1e-06)
    mech_out[...] = mech[...] / norm[:, 0:1]
    (dmg,) = unpack(asked_hot(request, cap), got, width, [(0, got.shape[1])])
    dmg_out[...] = dmg / norm[:, 1:2]
    norms[...] = norm


VM = pl.BlockSpec(memory_space=pltpu.VMEM)
ANY = pl.BlockSpec(memory_space=pl.ANY)
SM = pl.BlockSpec(memory_space=pltpu.SMEM)


def call(body, outs, ins, scratch=(), flops=0, nbytes=0, specs=None, limit=VMEM_LIMIT):
    one = not isinstance(outs, (list, tuple))
    return pl.pallas_call(
        body,
        out_shape=outs,
        in_specs=specs or [VM] * ins,
        out_specs=VM if one else [VM] * len(outs),
        scratch_shapes=list(scratch),
        compiler_params=pltpu.CompilerParams(vmem_limit_bytes=limit),
        cost_estimate=pl.CostEstimate(flops=flops, bytes_accessed=nbytes, transcendentals=0),
    )


def sds(shape, dtype=F32):
    return jax.ShapeDtypeStruct(shape, dtype)


def swap(x, axes):
    return lax.all_to_all(x, axes, split_axis=0, concat_axis=0, tiled=True)


def on_device(
    displacement,
    damage,
    applied_load,
    tangent,
    laplacian,
    block_columns,
    send_lists,
    hist_mech,
    mech_dest,
    strain_matrix,
    quad_weight,
):
    lanes, width = displacement.shape
    kblk = tangent.shape[1]
    quads = hist_mech.shape[1]
    ghost = send_lists.shape[2]
    both = ("dom", "blk")
    devices = lax.axis_size(both)
    groups = lax.axis_size("dom")
    disp_t = displacement.T
    dmg_t = damage.T
    load_t = applied_load.T
    tan_t = jnp.transpose(tangent, (1, 2, 3, 0))
    lap_t = jnp.transpose(laplacian, (1, 2, 3, 0))
    hist_t = jnp.transpose(hist_mech, (1, 2, 0))
    cols_t = block_columns.T

    cap = lanes // devices + 1
    stacked = jnp.concatenate([disp_t, dmg_t], axis=0)
    with jax.named_scope("fields"):
        fields = call(fields_kernel, sds(stacked.shape, BF16), 1, flops=FILL)(stacked)
    group = lax.all_gather(fields, "blk", axis=0, tiled=False)
    with jax.named_scope("picks"):
        picked = call(pick_kernel, sds((2 * width, ghost), BF16), 2, flops=20 * FILL)(
            group, send_lists[0]
        )
    picked, mech_dest = lax.optimization_barrier((picked, mech_dest))
    with jax.named_scope("requests"):
        request, bucket = call(
            functools.partial(request_kernel, cap),
            [sds((devices, 1, lanes)), sds((1, lanes), jnp.int32)],
            1,
            flops=FILL,
        )(mech_dest[None, :])
    wanted = swap(request, both)
    blocks = lax.axis_size("blk")
    everyone = [(a, b) for a in range(groups) for b in range(blocks)]
    hop = [(a * blocks + b, (a + 1 - b % 2 * 2) * blocks + b) for a, b in everyone]
    hop = [(i, j) for i, j in hop if 0 <= j < groups * blocks]
    side = [(b, b ^ 1) for b in range(blocks)]
    mine_ghost = lax.ppermute(picked, both, hop)
    mine_ghost, wanted = lax.optimization_barrier((mine_ghost, wanted))
    other_ghost = lax.ppermute(mine_ghost, "blk", side)
    size = section_size(cap * width, lanes)
    with jax.named_scope("early"):
        found, sections, asked_by = call(
            functools.partial(early_kernel, cap),
            [
                sds((width, kblk * lanes)),
                sds((devices, 2 * size, 4, lanes)),
                sds((cap * devices, lanes), BF16),
            ],
            5,
        )(group, cols_t, wanted, disp_t, dmg_t)
    with jax.named_scope("laplacian"):
        parcels = call(
            laplacian_kernel,
            sds((devices, 3 * size, 4, lanes)),
            8,
            [pltpu.VMEM((kblk * width, lanes), F32), pltpu.VMEM((width, lanes), F32)],
            flops=FILL,
        )(found, mine_ghost, other_ghost, cols_t, lap_t, asked_by, dmg_t, sections)
    asked = swap(parcels, both)
    with jax.named_scope("tangent"):
        mech, mech_total = call(
            tangent_kernel,
            [sds((width, lanes)), sds((1, lanes))],
            7,
            [
                pltpu.VMEM(tan_t.shape, BF16),
                pltpu.VMEM((lanes, kblk * width), BF16),
                pltpu.SemaphoreType.DMA((width // 8,)),
            ],
            flops=FILL,
            specs=[VM, VM, VM, VM, ANY, VM, VM],
            limit=48 * 1024 * 1024,
        )(group, mine_ghost, other_ghost, cols_t, tan_t, dmg_t, load_t)
    asked, mech_total = lax.optimization_barrier((asked, mech_total))
    with jax.named_scope("source"):
        answer = call(
            functools.partial(source_kernel, cap),
            sds((devices, section_size(cap * width + 2, lanes), 4, lanes)),
            6,
            flops=FILL,
            specs=[VM, VM, VM, VM, SM, VM],
            limit=3 * VMEM_LIMIT,
        )(asked, bucket, hist_t, strain_matrix, quad_weight[None, :], mech_total)
    got = swap(answer, both)
    with jax.named_scope("scale"):
        mech_out, dmg_out, norms = call(
            functools.partial(scale_kernel, cap, float(lanes * width * devices)),
            [sds((width, lanes)), sds((width, lanes)), sds((1, 2))],
            3,
        )(got, wanted, mech)
    return mech_out.T, dmg_out.T, norms[0]


def solution(mesh):
    rows = P(("dom", "blk"))
    in_specs = (rows,) * 6 + (P("dom"),) + (rows,) * 2 + (P(), P())
    out_specs = (rows, rows, P())
    return jax.shard_map(
        on_device, mesh=mesh, in_specs=in_specs, out_specs=out_specs, check_vma=False
    )
```

```python
import functools

import jax
import jax.numpy as jnp
from jax import lax
from jax.experimental import pallas as pl
from jax.experimental.pallas import tpu as pltpu
from jax.sharding import PartitionSpec as P

F32 = jnp.float32
BF16 = jnp.bfloat16
FILL = 10**10
POINTS = 9
STEP = 16
VMEM_LIMIT = 4 * 1024 * 1024


def dot(a, b):
    return lax.dot_general(a, b, (((1,), (0,)), ((), ())), preferred_element_type=F32)


def dot_nt(a, b):
    return lax.dot_general(a, b, (((1,), (1,)), ((), ())), preferred_element_type=F32)


def split2(x):
    hi = x.astype(BF16)
    lo = (x - hi.astype(F32)).astype(BF16)
    return hi, lo


def split3(x):
    hi = x.astype(BF16)
    rest = x - hi.astype(F32)
    mid = rest.astype(BF16)
    lo = (rest - mid.astype(F32)).astype(BF16)
    return hi, mid, lo


def one_hot(cond):
    return jnp.where(cond, 1.0, 0.0).astype(BF16)


def iota(shape, dim):
    return lax.broadcasted_iota(jnp.int32, shape, dim)


def section_size(values, lanes):
    return -(-values // (4 * lanes))


def pack(hot, table, out, section, tail=0.0):
    devices, _, _, lanes = out.shape
    hi, lo = split2(table)
    moved = dot_nt(hot, hi) + dot_nt(hot, lo)
    cap, width = moved.shape[0] // devices, moved.shape[1]
    first, size = section
    rows = [moved[k * devices : (k + 1) * devices] for k in range(cap)]
    rows.append(jnp.zeros((devices, size * 4 * lanes - cap * width), F32))
    flat = jnp.concatenate(rows, axis=1)
    for j in range(size * 4):
        line = flat[:, j * lanes : (j + 1) * lanes]
        out[:, first + j // 4, j % 4, :] = line + tail if j == size * 4 - 1 else line


def unpack(hot, got, width, sections):
    devices, _, _, lanes = got.shape
    cap = hot.shape[0] // devices
    blank = jnp.zeros((cap * devices, -width % lanes), F32)
    tall = []
    for first, size in sections:
        lines = [got[:, first + j // 4, j % 4, :] for j in range(size * 4)]
        flat = jnp.concatenate(lines, axis=1)
        rows = [flat[:, k * width : (k + 1) * width] for k in range(cap)]
        tall.append(jnp.concatenate([jnp.concatenate(rows, axis=0), blank], axis=1).T[:width])
    hi, lo = split2(jnp.concatenate(tall, axis=0))
    found = dot(hi, hot) + dot(lo, hot)
    return [found[i * width : (i + 1) * width] for i in range(len(sections))]


def asked_hot(request, cap):
    devices, _, lanes = request.shape
    slots = request[:, 0, :]
    lane = iota((devices, lanes), 1).astype(F32)
    hots = [one_hot(lane == slots[:, k : k + 1] - 1.0) for k in range(cap)]
    return jnp.concatenate(hots, axis=0)


def asking_hot(bucket, cap, devices):
    place = iota((devices, bucket.shape[1]), 0) * cap
    hots = [one_hot(place + k == bucket[...]) for k in range(cap)]
    return jnp.concatenate(hots, axis=0)


def root_of(damage):
    return jnp.sqrt((1.0 - damage) ** 2 + 0.001)


def fields_kernel(stacked, fields):
    width = stacked.shape[0] // 2
    dmg = stacked[width:, :]
    fields[:width, :] = (root_of(dmg) * stacked[:width, :]).astype(BF16)
    fields[width:, :] = dmg.astype(BF16)


def request_kernel(cap, dest, request, bucket):
    devices, _, lanes = request.shape
    d = dest[...]
    owner = d // lanes
    slot = d - owner * lanes
    blocks = lax.axis_size("blk")
    owner = owner % blocks * (devices // blocks) + owner // blocks
    square = jnp.broadcast_to(owner.astype(F32), (lanes, lanes))
    diag = iota((lanes, lanes), 0) == iota((lanes, lanes), 1)
    column = jnp.sum(jnp.where(diag, square, 0.0), axis=1, keepdims=True)
    before = iota((lanes, lanes), 0) < iota((lanes, lanes), 1)
    same = (column == square) & before
    rank = jnp.sum(jnp.where(same, 1.0, 0.0), axis=0, keepdims=True).astype(jnp.int32)
    bucket[...] = owner * cap + rank
    wanted = jnp.where(iota((devices, lanes), 0) == owner, (slot + 1).astype(F32), 0.0)
    ranks = one_hot(iota((lanes, lanes), 0) == rank)
    request[...] = dot_nt(wanted.astype(BF16), ranks)[:, None, :]


def pick_kernel(group, lists, out):
    parts = group.shape[0]
    table = jnp.concatenate([group[j] for j in range(parts)], axis=1)
    odd = lax.axis_index("blk") % 2
    row = jnp.where(odd == 0, lists[1:2, :], lists[0:1, :])
    hot = one_hot(iota((table.shape[1], row.shape[1]), 0) == row)
    out[...] = dot(table, hot).astype(BF16)


def total_of(x):
    line = jnp.sum(x * x, axis=0, keepdims=True)
    return jnp.sum(line, axis=1, keepdims=True)


def source_kernel(cap, got, bucket, hist, smat, weight, mech_total, out):
    quads, width, lanes = hist.shape
    hot = asking_hot(bucket, cap, got.shape[0])
    size = got.shape[1] // 3
    disp, v, u = unpack(hot, got, width, [(i * size, size) for i in range(3)])
    gap = jnp.zeros((lanes - width, lanes), F32)
    d_hi, d_lo = split2(jnp.concatenate([disp, gap], axis=0))
    upper = jnp.concatenate([d_hi, d_lo], axis=1)
    lower = jnp.concatenate([d_hi, jnp.zeros_like(d_hi)], axis=1)
    sides = jnp.concatenate([upper, lower], axis=0)
    acc = jnp.zeros((width, lanes), F32)
    for first in range(0, quads, POINTS):
        points = range(first, min(first + POINTS, quads))
        rows = smat[pl.ds(first, len(points))].reshape(len(points) * width, width)
        blank = jnp.zeros((rows.shape[0], lanes - width), F32)
        halves = split2(jnp.concatenate([rows, blank], axis=1))
        full = dot(jnp.concatenate(halves, axis=1), sides)
        strain = full[:, :lanes] + full[:, lanes:]
        energy = 0.5 * strain * strain
        for q in points:
            part = energy[(q - first) * width : (q - first + 1) * width]
            acc = acc + weight[0, q] * jnp.maximum(hist[q], part)
    dmg_res = u + 2.0 * acc * v
    spare = iota((1, lanes), 1) - (lanes - 2)
    tail = jnp.where(spare == 0, mech_total[...], 0.0)
    tail = jnp.where(spare == 1, total_of(dmg_res), tail)
    pack(hot, dmg_res, out, (0, out.shape[1]), tail)


def columns_row(columns):
    return jnp.concatenate([columns[k : k + 1, :] for k in range(columns.shape[0])], axis=1)


def own_gather(group, rows, wanted):
    table = jnp.concatenate([group[j, rows, :] for j in range(group.shape[0])], axis=1)
    hot = one_hot(iota((table.shape[1], wanted.shape[1]), 0) == wanted)
    return dot(table, hot)


def ghost_gather(own, mine_ghost, other_ghost, rows, wanted):
    ghost = mine_ghost.shape[1]
    odd = lax.axis_index("blk") % 2
    table = jnp.concatenate([mine_ghost[rows, :], other_ghost[rows, :]], axis=1)
    hots = [
        one_hot(iota((ghost, wanted.shape[1]), 0) + start == wanted)
        for start in (own + odd * ghost, own + ghost - odd * ghost)
    ]
    return dot(table, jnp.concatenate(hots, axis=0))


def stacked_columns(found, kblk):
    lanes = found.shape[1] // kblk
    cut = [found[:, k * lanes : (k + 1) * lanes] for k in range(kblk)]
    return jnp.concatenate(cut, axis=0)


def early_kernel(cap, group, columns, request, disp, damage, found, sections, asked):
    width = disp.shape[0]
    found[...] = own_gather(group, pl.ds(width, width), columns_row(columns))
    hot = asked_hot(request, cap)
    asked[...] = hot
    size = sections.shape[1] // 2
    pack(hot, disp[...], sections, (0, size))
    pack(hot, damage[...] - 1.0, sections, (size, size))


def laplacian_kernel(
    found_own,
    mine_ghost,
    other_ghost,
    columns,
    lap,
    asked,
    damage,
    sections,
    parcels,
    near,
    diff,
):
    kblk, rows, width, lanes = lap.shape
    own = lax.axis_size("blk") * lanes
    half = pl.ds(width, width)
    found = found_own[...] + ghost_gather(
        own, mine_ghost, other_ghost, half, columns_row(columns)
    )
    near[...] = stacked_columns(found, kblk)

    @pl.loop(0, rows // STEP)
    def _(step):
        acc = [jnp.zeros((8, lanes), F32) for _ in range(STEP)]
        for k in range(kblk):
            for c in range(0, width, 16):
                base = k * width + c
                lo = near[base : base + 8, :]
                hi = near[base + 8 : base + 16, :]
                for r in range(STEP):
                    block = lap[k, step * STEP + r, c : c + 16, :].astype(F32)
                    acc[r] = acc[r] + (block[:8] * lo + block[8:] * hi)
        sums = [jnp.sum(a, axis=0, keepdims=True) for a in acc]
        place = pl.ds(pl.multiple_of(step * STEP, STEP), STEP)
        diff[place, :] = jnp.concatenate(sums, axis=0)

    size = sections.shape[1] // 2
    parcels[:, : 2 * size, :, :] = sections[...]
    pack(asked[...], diff[...] + damage[...], parcels, (2 * size, size))


def tangent_kernel(
    group, mine_ghost, other_ghost, columns, tan_hbm, damage, load, mech, mech_total, tan, left_ref, sems
):
    kblk, rows, width, lanes = tan.shape
    depth = kblk * width
    steps = rows // 8

    def piece(step):
        place = pl.ds(pl.multiple_of(step * 8, 8), 8)
        return pltpu.make_async_copy(tan_hbm.at[:, place], tan.at[:, place], sems.at[step])

    @pl.loop(0, steps)
    def _(step):
        piece(step).start()

    wanted = columns_row(columns)
    own = group.shape[0] * lanes
    half = pl.ds(0, width)
    found = own_gather(group, half, wanted)
    found = found + ghost_gather(own, mine_ghost, other_ghost, half, wanted)
    left_ref[...] = stacked_columns(found, kblk).T.astype(BF16)
    lane = iota((8, 2 * lanes), 1) % lanes
    mine = iota((8, 2 * lanes), 0) == lane % 8

    @pl.loop(0, steps)
    def _(step):
        piece(step).wait()
        lines = []
        for r in range(0, 8, 2):
            pair = [tan[:, step * 8 + r + j].reshape(depth, lanes) for j in range(2)]
            full = dot(left_ref[...], jnp.concatenate(pair, axis=1))
            kept = full[:8]
            for g in range(1, lanes // 8):
                kept = jnp.where(lane // 8 == g, full[g * 8 : g * 8 + 8], kept)
            line = jnp.sum(jnp.where(mine, kept, 0.0), axis=0, keepdims=True)
            lines += [line[:, :lanes], line[:, lanes:]]
        mech[pl.ds(pl.multiple_of(step * 8, 8), 8), :] = jnp.concatenate(lines, axis=0)

    mech_res = root_of(damage[...]) * mech[...] - load[...]
    mech[...] = mech_res
    mech_total[...] = jnp.broadcast_to(total_of(mech_res), mech_total.shape)


def scale_kernel(cap, entries, got, request, mech, mech_out, dmg_out, norms):
    width, lanes = mech.shape
    last = got[:, got.shape[1] - 1, 3, :]
    total = jnp.sum(last, axis=0, keepdims=True)[:, lanes - 2 :]
    norm = jnp.sqrt(total / entries + 1e-06)
    mech_out[...] = mech[...] / norm[:, 0:1]
    (dmg,) = unpack(asked_hot(request, cap), got, width, [(0, got.shape[1])])
    dmg_out[...] = dmg / norm[:, 1:2]
    norms[...] = norm


VM = pl.BlockSpec(memory_space=pltpu.VMEM)
ANY = pl.BlockSpec(memory_space=pl.ANY)
SM = pl.BlockSpec(memory_space=pltpu.SMEM)


def call(body, outs, ins, scratch=(), flops=0, nbytes=0, specs=None, limit=VMEM_LIMIT):
    one = not isinstance(outs, (list, tuple))
    return pl.pallas_call(
        body,
        out_shape=outs,
        in_specs=specs or [VM] * ins,
        out_specs=VM if one else [VM] * len(outs),
        scratch_shapes=list(scratch),
        compiler_params=pltpu.CompilerParams(vmem_limit_bytes=limit),
        cost_estimate=pl.CostEstimate(flops=flops, bytes_accessed=nbytes, transcendentals=0),
    )


def sds(shape, dtype=F32):
    return jax.ShapeDtypeStruct(shape, dtype)


def swap(x, axes):
    return lax.all_to_all(x, axes, split_axis=0, concat_axis=0, tiled=True)


def on_device(
    displacement,
    damage,
    applied_load,
    tangent,
    laplacian,
    block_columns,
    send_lists,
    hist_mech,
    mech_dest,
    strain_matrix,
    quad_weight,
):
    lanes, width = displacement.shape
    kblk = tangent.shape[1]
    quads = hist_mech.shape[1]
    ghost = send_lists.shape[2]
    both = ("blk", "dom")
    devices = lax.axis_size(both)
    groups = lax.axis_size("dom")
    disp_t = displacement.T
    dmg_t = damage.T
    load_t = applied_load.T
    tan_t = jnp.transpose(tangent, (1, 2, 3, 0))
    lap_t = jnp.transpose(laplacian, (1, 2, 3, 0))
    hist_t = jnp.transpose(hist_mech, (1, 2, 0))
    cols_t = block_columns.T

    cap = lanes // devices + 1
    stacked = jnp.concatenate([disp_t, dmg_t], axis=0)
    with jax.named_scope("fields"):
        fields = call(fields_kernel, sds(stacked.shape, BF16), 1, flops=FILL)(stacked)
    group = lax.all_gather(fields, "blk", axis=0, tiled=False)
    with jax.named_scope("picks"):
        picked = call(pick_kernel, sds((2 * width, ghost), BF16), 2, flops=20 * FILL)(
            group, send_lists[0]
        )
    picked, mech_dest = lax.optimization_barrier((picked, mech_dest))
    with jax.named_scope("requests"):
        request, bucket = call(
            functools.partial(request_kernel, cap),
            [sds((devices, 1, lanes)), sds((1, lanes), jnp.int32)],
            1,
            flops=FILL,
        )(mech_dest[None, :])
    wanted = swap(request, both)
    blocks = lax.axis_size("blk")
    everyone = [(a, b) for a in range(groups) for b in range(blocks)]
    hop = [(a * blocks + b, (a + 1 - b % 2 * 2) * blocks + b) for a, b in everyone]
    hop = [(i, j) for i, j in hop if 0 <= j < groups * blocks]
    side = [(b, b ^ 1) for b in range(blocks)]
    mine_ghost = lax.ppermute(picked, ("dom", "blk"), hop)
    mine_ghost, wanted = lax.optimization_barrier((mine_ghost, wanted))
    other_ghost = lax.ppermute(mine_ghost, "blk", side)
    size = section_size(cap * width, lanes)
    with jax.named_scope("early"):
        found, sections, asked_by = call(
            functools.partial(early_kernel, cap),
            [
                sds((width, kblk * lanes)),
                sds((devices, 2 * size, 4, lanes)),
                sds((cap * devices, lanes), BF16),
            ],
            5,
        )(group, cols_t, wanted, disp_t, dmg_t)
    with jax.named_scope("laplacian"):
        parcels = call(
            laplacian_kernel,
            sds((devices, 3 * size, 4, lanes)),
            8,
            [pltpu.VMEM((kblk * width, lanes), F32), pltpu.VMEM((width, lanes), F32)],
            flops=FILL,
        )(found, mine_ghost, other_ghost, cols_t, lap_t, asked_by, dmg_t, sections)
    asked = swap(parcels, both)
    with jax.named_scope("tangent"):
        mech, mech_total = call(
            tangent_kernel,
            [sds((width, lanes)), sds((1, lanes))],
            7,
            [
                pltpu.VMEM(tan_t.shape, BF16),
                pltpu.VMEM((lanes, kblk * width), BF16),
                pltpu.SemaphoreType.DMA((width // 8,)),
            ],
            flops=FILL,
            specs=[VM, VM, VM, VM, ANY, VM, VM],
            limit=48 * 1024 * 1024,
        )(group, mine_ghost, other_ghost, cols_t, tan_t, dmg_t, load_t)
    asked, mech_total = lax.optimization_barrier((asked, mech_total))
    with jax.named_scope("source"):
        answer = call(
            functools.partial(source_kernel, cap),
            sds((devices, section_size(cap * width + 2, lanes), 4, lanes)),
            6,
            flops=FILL,
            specs=[VM, VM, VM, VM, SM, VM],
            limit=3 * VMEM_LIMIT,
        )(asked, bucket, hist_t, strain_matrix, quad_weight[None, :], mech_total)
    got = swap(answer, both)
    with jax.named_scope("scale"):
        mech_out, dmg_out, norms = call(
            functools.partial(scale_kernel, cap, float(lanes * width * devices)),
            [sds((width, lanes)), sds((width, lanes)), sds((1, 2))],
            3,
        )(got, wanted, mech)
    return mech_out.T, dmg_out.T, norms[0]


def solution(mesh):
    rows = P(("dom", "blk"))
    in_specs = (rows,) * 6 + (P("dom"),) + (rows,) * 2 + (P(), P())
    out_specs = (rows, rows, P())
    return jax.shard_map(
        on_device, mesh=mesh, in_specs=in_specs, out_specs=out_specs, check_vma=False
    )
```

```python
import functools

import jax
import jax.numpy as jnp
from jax import lax
from jax.experimental import pallas as pl
from jax.experimental.pallas import tpu as pltpu
from jax.sharding import PartitionSpec as P

F32 = jnp.float32
BF16 = jnp.bfloat16
FILL = 10**10
POINTS = 9
STEP = 16
VMEM_LIMIT = 4 * 1024 * 1024


def dot(a, b):
    return lax.dot_general(a, b, (((1,), (0,)), ((), ())), preferred_element_type=F32)


def dot_nt(a, b):
    return lax.dot_general(a, b, (((1,), (1,)), ((), ())), preferred_element_type=F32)


def split2(x):
    hi = x.astype(BF16)
    lo = (x - hi.astype(F32)).astype(BF16)
    return hi, lo


def split3(x):
    hi = x.astype(BF16)
    rest = x - hi.astype(F32)
    mid = rest.astype(BF16)
    lo = (rest - mid.astype(F32)).astype(BF16)
    return hi, mid, lo


def one_hot(cond):
    return jnp.where(cond, 1.0, 0.0).astype(BF16)


def iota(shape, dim):
    return lax.broadcasted_iota(jnp.int32, shape, dim)


def section_size(values, lanes):
    return -(-values // (4 * lanes))


def pack(hot, table, out, section, tail=0.0):
    devices, _, _, lanes = out.shape
    hi, lo = split2(table)
    moved = dot_nt(hot, hi) + dot_nt(hot, lo)
    cap, width = moved.shape[0] // devices, moved.shape[1]
    first, size = section
    rows = [moved[k * devices : (k + 1) * devices] for k in range(cap)]
    rows.append(jnp.zeros((devices, size * 4 * lanes - cap * width), F32))
    flat = jnp.concatenate(rows, axis=1)
    for j in range(size * 4):
        line = flat[:, j * lanes : (j + 1) * lanes]
        out[:, first + j // 4, j % 4, :] = line + tail if j == size * 4 - 1 else line


def unpack(hot, got, width, sections):
    devices, _, _, lanes = got.shape
    cap = hot.shape[0] // devices
    blank = jnp.zeros((cap * devices, -width % lanes), F32)
    tall = []
    for first, size in sections:
        lines = [got[:, first + j // 4, j % 4, :] for j in range(size * 4)]
        flat = jnp.concatenate(lines, axis=1)
        rows = [flat[:, k * width : (k + 1) * width] for k in range(cap)]
        tall.append(jnp.concatenate([jnp.concatenate(rows, axis=0), blank], axis=1).T[:width])
    hi, lo = split2(jnp.concatenate(tall, axis=0))
    found = dot(hi, hot) + dot(lo, hot)
    return [found[i * width : (i + 1) * width] for i in range(len(sections))]


def asked_hot(request, cap):
    devices, _, lanes = request.shape
    slots = request[:, 0, :]
    lane = iota((devices, lanes), 1).astype(F32)
    hots = [one_hot(lane == slots[:, k : k + 1] - 1.0) for k in range(cap)]
    return jnp.concatenate(hots, axis=0)


def asking_hot(bucket, cap, devices):
    place = iota((devices, bucket.shape[1]), 0) * cap
    hots = [one_hot(place + k == bucket[...]) for k in range(cap)]
    return jnp.concatenate(hots, axis=0)


def root_of(damage):
    return jnp.sqrt((1.0 - damage) ** 2 + 0.001)


def fields_kernel(stacked, fields):
    width = stacked.shape[0] // 2
    dmg = stacked[width:, :]
    fields[:width, :] = (root_of(dmg) * stacked[:width, :]).astype(BF16)
    fields[width:, :] = dmg.astype(BF16)


def request_kernel(cap, dest, request, bucket):
    devices, _, lanes = request.shape
    d = dest[...]
    owner = d // lanes
    slot = d - owner * lanes
    blocks = lax.axis_size("blk")
    owner = owner % blocks * (devices // blocks) + owner // blocks
    square = jnp.broadcast_to(owner.astype(F32), (lanes, lanes))
    diag = iota((lanes, lanes), 0) == iota((lanes, lanes), 1)
    column = jnp.sum(jnp.where(diag, square, 0.0), axis=1, keepdims=True)
    before = iota((lanes, lanes), 0) < iota((lanes, lanes), 1)
    same = (column == square) & before
    rank = jnp.sum(jnp.where(same, 1.0, 0.0), axis=0, keepdims=True).astype(jnp.int32)
    bucket[...] = owner * cap + rank
    wanted = jnp.where(iota((devices, lanes), 0) == owner, (slot + 1).astype(F32), 0.0)
    ranks = one_hot(iota((lanes, lanes), 0) == rank)
    request[...] = dot_nt(wanted.astype(BF16), ranks)[:, None, :]


def pick_kernel(group, lists, out):
    parts = group.shape[0]
    table = jnp.concatenate([group[j] for j in range(parts)], axis=1)
    odd = lax.axis_index("blk") % 2
    row = jnp.where(odd == 0, lists[1:2, :], lists[0:1, :])
    hot = one_hot(iota((table.shape[1], row.shape[1]), 0) == row)
    out[...] = dot(table, hot).astype(BF16)


def total_of(x):
    line = jnp.sum(x * x, axis=0, keepdims=True)
    return jnp.sum(line, axis=1, keepdims=True)


def halves_kernel(smat, out):
    quads, width, lanes = smat.shape[0], smat.shape[1], out.shape[1] // 2
    for first in range(0, quads, POINTS):
        count = min(POINTS, quads - first)
        rows = smat[pl.ds(first, count)].reshape(count * width, width)
        blank = jnp.zeros((rows.shape[0], lanes - width), F32)
        halves = split2(jnp.concatenate([rows, blank], axis=1))
        out[pl.ds(first * width, count * width), :] = jnp.concatenate(halves, axis=1)


def source_kernel(cap, got, bucket, hist, halves, weight, mech_total, out):
    quads, width, lanes = hist.shape
    hot = asking_hot(bucket, cap, got.shape[0])
    size = got.shape[1] // 3
    disp, v, u = unpack(hot, got, width, [(i * size, size) for i in range(3)])
    gap = jnp.zeros((lanes - width, lanes), F32)
    d_hi, d_lo = split2(jnp.concatenate([disp, gap], axis=0))
    upper = jnp.concatenate([d_hi, d_lo], axis=1)
    lower = jnp.concatenate([d_hi, jnp.zeros_like(d_hi)], axis=1)
    sides = jnp.concatenate([upper, lower], axis=0)
    acc = jnp.zeros((width, lanes), F32)
    for first in range(0, quads, POINTS):
        points = range(first, min(first + POINTS, quads))
        full = dot(halves[pl.ds(first * width, len(points) * width), :], sides)
        strain = full[:, :lanes] + full[:, lanes:]
        energy = 0.5 * strain * strain
        for q in points:
            part = energy[(q - first) * width : (q - first + 1) * width]
            acc = acc + weight[0, q] * jnp.maximum(hist[q], part)
    dmg_res = u + 2.0 * acc * v
    spare = iota((1, lanes), 1) - (lanes - 2)
    tail = jnp.where(spare == 0, mech_total[...], 0.0)
    tail = jnp.where(spare == 1, total_of(dmg_res), tail)
    pack(hot, dmg_res, out, (0, out.shape[1]), tail)


def columns_row(columns):
    return jnp.concatenate([columns[k : k + 1, :] for k in range(columns.shape[0])], axis=1)


def own_gather(group, rows, wanted):
    table = jnp.concatenate([group[j, rows, :] for j in range(group.shape[0])], axis=1)
    hot = one_hot(iota((table.shape[1], wanted.shape[1]), 0) == wanted)
    return dot(table, hot)


def ghost_gather(own, mine_ghost, other_ghost, rows, wanted):
    ghost = mine_ghost.shape[1]
    odd = lax.axis_index("blk") % 2
    table = jnp.concatenate([mine_ghost[rows, :], other_ghost[rows, :]], axis=1)
    hots = [
        one_hot(iota((ghost, wanted.shape[1]), 0) + start == wanted)
        for start in (own + odd * ghost, own + ghost - odd * ghost)
    ]
    return dot(table, jnp.concatenate(hots, axis=0))


def stacked_columns(found, kblk):
    lanes = found.shape[1] // kblk
    cut = [found[:, k * lanes : (k + 1) * lanes] for k in range(kblk)]
    return jnp.concatenate(cut, axis=0)


def early_kernel(cap, group, columns, request, disp, damage, found, sections, asked):
    width = disp.shape[0]
    found[...] = own_gather(group, pl.ds(width, width), columns_row(columns))
    hot = asked_hot(request, cap)
    asked[...] = hot
    size = sections.shape[1] // 2
    pack(hot, disp[...], sections, (0, size))
    pack(hot, damage[...] - 1.0, sections, (size, size))


def laplacian_kernel(
    found_own,
    mine_ghost,
    other_ghost,
    columns,
    lap,
    asked,
    damage,
    sections,
    parcels,
    near,
    diff,
):
    kblk, rows, width, lanes = lap.shape
    own = lax.axis_size("blk") * lanes
    half = pl.ds(width, width)
    found = found_own[...] + ghost_gather(
        own, mine_ghost, other_ghost, half, columns_row(columns)
    )
    near[...] = stacked_columns(found, kblk)

    @pl.loop(0, rows // STEP)
    def _(step):
        acc = [jnp.zeros((8, lanes), F32) for _ in range(STEP)]
        for k in range(kblk):
            for c in range(0, width, 16):
                base = k * width + c
                lo = near[base : base + 8, :]
                hi = near[base + 8 : base + 16, :]
                for r in range(STEP):
                    block = lap[k, step * STEP + r, c : c + 16, :].astype(F32)
                    acc[r] = acc[r] + (block[:8] * lo + block[8:] * hi)
        sums = [jnp.sum(a, axis=0, keepdims=True) for a in acc]
        place = pl.ds(pl.multiple_of(step * STEP, STEP), STEP)
        diff[place, :] = jnp.concatenate(sums, axis=0)

    size = sections.shape[1] // 2
    parcels[:, : 2 * size, :, :] = sections[...]
    pack(asked[...], diff[...] + damage[...], parcels, (2 * size, size))


def tangent_kernel(
    group, mine_ghost, other_ghost, columns, tan_hbm, damage, load, mech, mech_total, tan, left_ref, sems
):
    kblk, rows, width, lanes = tan.shape
    depth = kblk * width
    steps = rows // 8

    def piece(step):
        place = pl.ds(pl.multiple_of(step * 8, 8), 8)
        return pltpu.make_async_copy(tan_hbm.at[:, place], tan.at[:, place], sems.at[step])

    @pl.loop(0, steps)
    def _(step):
        piece(step).start()

    wanted = columns_row(columns)
    own = group.shape[0] * lanes
    half = pl.ds(0, width)
    found = own_gather(group, half, wanted)
    found = found + ghost_gather(own, mine_ghost, other_ghost, half, wanted)
    left_ref[...] = stacked_columns(found, kblk).T.astype(BF16)
    lane = iota((8, 2 * lanes), 1) % lanes
    mine = iota((8, 2 * lanes), 0) == lane % 8

    @pl.loop(0, steps)
    def _(step):
        piece(step).wait()
        lines = []
        for r in range(0, 8, 2):
            pair = [tan[:, step * 8 + r + j].reshape(depth, lanes) for j in range(2)]
            full = dot(left_ref[...], jnp.concatenate(pair, axis=1))
            kept = full[:8]
            for g in range(1, lanes // 8):
                kept = jnp.where(lane // 8 == g, full[g * 8 : g * 8 + 8], kept)
            line = jnp.sum(jnp.where(mine, kept, 0.0), axis=0, keepdims=True)
            lines += [line[:, :lanes], line[:, lanes:]]
        mech[pl.ds(pl.multiple_of(step * 8, 8), 8), :] = jnp.concatenate(lines, axis=0)

    mech_res = root_of(damage[...]) * mech[...] - load[...]
    mech[...] = mech_res
    mech_total[...] = jnp.broadcast_to(total_of(mech_res), mech_total.shape)


def scale_kernel(cap, entries, got, request, mech, mech_out, dmg_out, norms):
    width, lanes = mech.shape
    last = got[:, got.shape[1] - 1, 3, :]
    total = jnp.sum(last, axis=0, keepdims=True)[:, lanes - 2 :]
    norm = jnp.sqrt(total / entries + 1e-06)
    mech_out[...] = mech[...] / norm[:, 0:1]
    (dmg,) = unpack(asked_hot(request, cap), got, width, [(0, got.shape[1])])
    dmg_out[...] = dmg / norm[:, 1:2]
    norms[...] = norm


VM = pl.BlockSpec(memory_space=pltpu.VMEM)
ANY = pl.BlockSpec(memory_space=pl.ANY)
SM = pl.BlockSpec(memory_space=pltpu.SMEM)


def call(body, outs, ins, scratch=(), flops=0, nbytes=0, specs=None, limit=VMEM_LIMIT):
    one = not isinstance(outs, (list, tuple))
    return pl.pallas_call(
        body,
        out_shape=outs,
        in_specs=specs or [VM] * ins,
        out_specs=VM if one else [VM] * len(outs),
        scratch_shapes=list(scratch),
        compiler_params=pltpu.CompilerParams(vmem_limit_bytes=limit),
        cost_estimate=pl.CostEstimate(flops=flops, bytes_accessed=nbytes, transcendentals=0),
    )


def sds(shape, dtype=F32):
    return jax.ShapeDtypeStruct(shape, dtype)


def swap(x, axes):
    return lax.all_to_all(x, axes, split_axis=0, concat_axis=0, tiled=True)


def on_device(
    displacement,
    damage,
    applied_load,
    tangent,
    laplacian,
    block_columns,
    send_lists,
    hist_mech,
    mech_dest,
    strain_matrix,
    quad_weight,
):
    lanes, width = displacement.shape
    kblk = tangent.shape[1]
    quads = hist_mech.shape[1]
    ghost = send_lists.shape[2]
    both = ("blk", "dom")
    devices = lax.axis_size(both)
    groups = lax.axis_size("dom")
    disp_t = displacement.T
    dmg_t = damage.T
    load_t = applied_load.T
    tan_t = jnp.transpose(tangent, (1, 2, 3, 0))
    lap_t = jnp.transpose(laplacian, (1, 2, 3, 0))
    hist_t = jnp.transpose(hist_mech, (1, 2, 0))
    cols_t = block_columns.T

    cap = lanes // devices + 1
    stacked = jnp.concatenate([disp_t, dmg_t], axis=0)
    with jax.named_scope("fields"):
        fields = call(fields_kernel, sds(stacked.shape, BF16), 1, flops=FILL)(stacked)
    group = lax.all_gather(fields, "blk", axis=0, tiled=False)
    with jax.named_scope("picks"):
        picked = call(pick_kernel, sds((2 * width, ghost), BF16), 2, flops=20 * FILL)(
            group, send_lists[0]
        )
    picked, mech_dest = lax.optimization_barrier((picked, mech_dest))
    with jax.named_scope("requests"):
        request, bucket = call(
            functools.partial(request_kernel, cap),
            [sds((devices, 1, lanes)), sds((1, lanes), jnp.int32)],
            1,
            flops=FILL,
        )(mech_dest[None, :])
    wanted = swap(request, both)
    blocks = lax.axis_size("blk")
    everyone = [(a, b) for a in range(groups) for b in range(blocks)]
    hop = [(a * blocks + b, (a + 1 - b % 2 * 2) * blocks + b) for a, b in everyone]
    hop = [(i, j) for i, j in hop if 0 <= j < groups * blocks]
    side = [(b, b ^ 1) for b in range(blocks)]
    mine_ghost = lax.ppermute(picked, ("dom", "blk"), hop)
    mine_ghost, wanted = lax.optimization_barrier((mine_ghost, wanted))
    other_ghost = lax.ppermute(mine_ghost, "blk", side)
    size = section_size(cap * width, lanes)
    with jax.named_scope("early"):
        found, sections, asked_by = call(
            functools.partial(early_kernel, cap),
            [
                sds((width, kblk * lanes)),
                sds((devices, 2 * size, 4, lanes)),
                sds((cap * devices, lanes), BF16),
            ],
            5,
        )(group, cols_t, wanted, disp_t, dmg_t)
    with jax.named_scope("laplacian"):
        parcels = call(
            laplacian_kernel,
            sds((devices, 3 * size, 4, lanes)),
            8,
            [pltpu.VMEM((kblk * width, lanes), F32), pltpu.VMEM((width, lanes), F32)],
            flops=FILL,
        )(found, mine_ghost, other_ghost, cols_t, lap_t, asked_by, dmg_t, sections)
    asked = swap(parcels, both)
    with jax.named_scope("tangent"):
        mech, mech_total = call(
            tangent_kernel,
            [sds((width, lanes)), sds((1, lanes))],
            7,
            [
                pltpu.VMEM(tan_t.shape, BF16),
                pltpu.VMEM((lanes, kblk * width), BF16),
                pltpu.SemaphoreType.DMA((width // 8,)),
            ],
            flops=FILL,
            specs=[VM, VM, VM, VM, ANY, VM, VM],
            limit=48 * 1024 * 1024,
        )(group, mine_ghost, other_ghost, cols_t, tan_t, dmg_t, load_t)
    mech_total, strain_matrix = lax.optimization_barrier((mech_total, strain_matrix))
    with jax.named_scope("halves"):
        halves = call(halves_kernel, sds((quads * width, 2 * lanes), BF16), 1)(strain_matrix)
    asked, halves = lax.optimization_barrier((asked, halves))
    with jax.named_scope("source"):
        answer = call(
            functools.partial(source_kernel, cap),
            sds((devices, section_size(cap * width + 2, lanes), 4, lanes)),
            6,
            flops=FILL,
            specs=[VM, VM, VM, VM, SM, VM],
            limit=3 * VMEM_LIMIT,
        )(asked, bucket, hist_t, halves, quad_weight[None, :], mech_total)
    got = swap(answer, both)
    with jax.named_scope("scale"):
        mech_out, dmg_out, norms = call(
            functools.partial(scale_kernel, cap, float(lanes * width * devices)),
            [sds((width, lanes)), sds((width, lanes)), sds((1, 2))],
            3,
        )(got, wanted, mech)
    return mech_out.T, dmg_out.T, norms[0]


def solution(mesh):
    rows = P(("dom", "blk"))
    in_specs = (rows,) * 6 + (P("dom"),) + (rows,) * 2 + (P(), P())
    out_specs = (rows, rows, P())
    return jax.shard_map(
        on_device, mesh=mesh, in_specs=in_specs, out_specs=out_specs, check_vma=False
    )
```
